32 devices in a mesh: chan: 16 (over z, y, x), tm: 2 (over core).
Axes of the slice: x: 2, y: 2, z: 4, core: 2. Of those that a mesh axis runs over, the one named last changes fastest.
Arguments:
- traces: float32 [2048, 8192], P('chan', 'tm'), may hold values from -600 to 600
- channel_ok: int32 [2048], P('chan'), may hold values 0 or 1
- time_taps: float32 [33], replicated, may hold values from -4 to 4
- space_taps: float32 [5], replicated, may hold values from -4 to 4
- pair_blocks: int32 [256, 2], P('chan'), may hold values from 0 to 15, as said below
- pair_count: int32 [16], P('chan'), may hold values from 4 to 16, as said below
Outputs:
- stacks: float32 [256, 201, 128], P(('chan', 'tm'))
The draws below stay inside these ranges and needn't reach their ends.
Inputs may be any that keep to these rules, and one draw needn't show every extreme that they name: `pair_blocks`: a != b, |a - b| <= 4, and both a and b lie within 4 of the owner's index p. Owner p uses its first pair_count[p] slots; the other slots' pairs are ignored. Some owner uses all 16 slots.
All inputs are finite; a program needn't handle non-finite values. No bound on the sum of `channel_ok` on one device may be relied on, other than what follows from the above.
Results may differ from the reference program's by a relative error of at most 0.0049.
Values may be sent and summed in bfloat16 or wider, within the bound.
No kernel may reach another device: no remote copies, remote signals or barrier semaphores. Data moves between devices by JAX's collectives and lax.ppermute only.
A program may use at most 128 MiB of HBM per device.

```python
import math
import jax
import jax.numpy as jnp
from jax import lax

BLOCK = 128
SEG = 256
MAXLAG = 100
TAPS = 33
STAPS = 5
CUT = 4
SLOTS = 16
CHANNELS = 2048
SEGMENTS = 32
SAMPLES = 8192
PAIRS = 256
NFFT = 510
LAGS = 201
N_CHAN = 16


def draw_traces(key, part):
    key_noise, key_chan, key_seg = jax.random.split(key, 3)
    noise = jnp.clip(jax.random.normal(key_noise, (CHANNELS, SAMPLES), jnp.float32), -6.0, 6.0)
    chan_gain = jnp.exp(jax.random.uniform(key_chan, (CHANNELS, 1), jnp.float32, 0.0, 2.3))
    seg_gain = jnp.exp(jax.random.uniform(key_seg, (CHANNELS, SAMPLES // SEG, 1), jnp.float32, 0.0, 2.3))
    seg_gain = jnp.broadcast_to(seg_gain, (CHANNELS, SAMPLES // SEG, SEG)).reshape(CHANNELS, SAMPLES)
    return noise * chan_gain * seg_gain


def draw_pair_blocks(key, part):
    key_first, key_dist = jax.random.split(jax.random.fold_in(key, 11), 2)
    block_count = CHANNELS // BLOCK
    owner_index = jnp.arange(PAIRS, dtype=jnp.int32) // SLOTS
    low_end = jnp.maximum(owner_index - CUT, 0)
    high_end = jnp.minimum(owner_index + CUT, block_count - 1)
    first_block = jax.random.randint(key_first, (PAIRS,), low_end, high_end + 1, jnp.int32)
    distance = jax.random.randint(key_dist, (PAIRS,), 1, CUT + 1, jnp.int32)
    other_end = jnp.where(first_block == high_end, low_end, high_end)
    second_block = jnp.where(first_block + distance <= high_end, first_block + distance, jnp.where(first_block - distance >= low_end, first_block - distance, other_end))
    return jnp.stack([first_block, second_block], axis=1).astype(jnp.int32)


def draw_pair_count(key, part):
    key_level, key_full = jax.random.split(jax.random.fold_in(key, 23), 2)
    block_count = CHANNELS // BLOCK
    level = jax.random.randint(key_level, (block_count,), 0, 3, jnp.int32)
    counts = jnp.where(level == 0, SLOTS, jnp.where(level == 1, SLOTS // 2, SLOTS // 4))
    full_owner = jax.random.randint(key_full, (), 0, block_count, jnp.int32)
    counts = jnp.where(jnp.arange(block_count, dtype=jnp.int32) == full_owner, SLOTS, counts)
    return counts.astype(jnp.int32)


def set_ends(result, rng, least, top_value):
    extent = result.shape
    spot = [jax.random.randint(jax.random.fold_in(rng, axis), (), 0, extent[axis]) for axis in range(len(extent))]
    result = result.at[tuple(spot)].set(least)
    longest = extent.index(max(extent))
    spot[longest] = (spot[longest] + 1) % extent[longest]
    return result.at[tuple(spot)].set(top_value)


def normal_values(rng, dims, scale, limit, kind=jnp.bfloat16):
    entries = jax.random.normal(rng, dims, jnp.float32) * scale
    return jnp.minimum(jnp.maximum(entries, -limit), limit).astype(kind)


def setup_inputs(seed: int = 0) -> dict:
    keys = jax.random.split(jax.random.key(seed), 7)
    return {
        "traces": draw_traces(jax.random.fold_in(keys[6], 71), 0),
        "channel_ok": set_ends((jax.random.randint(keys[1], (CHANNELS,), 0, 8) < 7).astype(jnp.int32), jax.random.fold_in(keys[1], 1), 0, 1),
        "time_taps": normal_values(keys[2], (TAPS,), 1.0, 4.0, jnp.float32),
        "space_taps": normal_values(keys[3], (STAPS,), 1.0, 4.0, jnp.float32),
        "pair_blocks": draw_pair_blocks(jax.random.fold_in(keys[6], 71), 0),
        "pair_count": draw_pair_count(jax.random.fold_in(keys[6], 71), 0),
    }


def dft_matrix():
    sample_pos = jnp.arange(SEG, dtype=jnp.int32)[:, None]
    bin_pos = jnp.arange(SEG, dtype=jnp.int32)[None, :]
    phase_angle = (sample_pos * bin_pos % NFFT).astype(jnp.float32) * (2.0 * math.pi / NFFT)
    return jnp.concatenate([jnp.cos(phase_angle), -jnp.sin(phase_angle)], axis=1).astype(jnp.bfloat16)

def reference(traces, channel_ok, time_taps, space_taps, pair_blocks, pair_count):
    half_taps = (TAPS - 1) // 2
    masked = traces * channel_ok.astype(jnp.float32)[:, None]
    padded = jnp.pad(masked, ((0, 0), (half_taps, half_taps)))
    time_filtered = jnp.zeros_like(masked)
    for tap_index in range(TAPS):
        time_filtered = time_filtered + time_taps[tap_index] * padded[:, tap_index:tap_index + SAMPLES]
    half_space = (STAPS - 1) // 2
    rim_rows = jnp.pad(time_filtered, ((half_space, half_space), (0, 0)))
    filtered = jnp.zeros_like(masked)
    for tap_index in range(STAPS):
        filtered = filtered + space_taps[tap_index] * rim_rows[tap_index:tap_index + CHANNELS]
    segment_view = filtered.reshape(CHANNELS, SEGMENTS, SEG)
    seg_power = lax.optimization_barrier(jnp.mean(segment_view * segment_view, axis=2, keepdims=True))
    whitened = (segment_view / jnp.sqrt(seg_power + 1e-05)).astype(jnp.bfloat16)
    blocks_view = whitened.reshape(N_CHAN, BLOCK, SEGMENTS, SEG)
    dft_table = dft_matrix()

    def transform(block_rows):
        flat_rows = block_rows.reshape(BLOCK * SEGMENTS, SEG)
        spectrum = jnp.dot(flat_rows, dft_table, preferred_element_type=jnp.float32)
        spectrum = spectrum.reshape(BLOCK, SEGMENTS, 2 * SEG)
        return (spectrum[..., :SEG].astype(jnp.bfloat16), spectrum[..., SEG:].astype(jnp.bfloat16))
    spec_real, spec_imag = lax.map(transform, blocks_view)
    count_all = jnp.repeat(pair_count, SLOTS)
    slot_index = jnp.arange(PAIRS, dtype=jnp.int32) % SLOTS
    alive_flag = (slot_index < count_all).astype(jnp.float32)
    lag_index = (jnp.arange(LAGS, dtype=jnp.int32) - MAXLAG) % NFFT
    stack_scale = float(SEGMENTS * SEG) ** (-0.5)

    def correlate(pair_item):
        first_block, second, alive = pair_item
        left_re = spec_real[first_block].astype(jnp.float32)
        left_im = spec_imag[first_block].astype(jnp.float32)
        right_re = spec_real[second].astype(jnp.float32)
        right_im = spec_imag[second].astype(jnp.float32)
        cross_re = lax.optimization_barrier(jnp.sum(left_re * right_re + left_im * right_im, axis=1))
        cross_im = lax.optimization_barrier(jnp.sum(left_im * right_re - left_re * right_im, axis=1))
        lagged = jnp.fft.irfft(lax.complex(cross_re, cross_im), n=NFFT, axis=-1)[:, lag_index]
        return jnp.transpose(lagged) * stack_scale * alive
    return lax.map(correlate, (pair_blocks[:, 0], pair_blocks[:, 1], alive_flag))
```

```python
import math

import jax
import jax.numpy as jnp
import ml_dtypes
import numpy as np
from jax import lax
from jax.experimental import pallas as pl
from jax.experimental.pallas import tpu as pltpu
from jax.sharding import PartitionSpec as P

SEG = 256
MAXLAG = 100
TAPS = 33
STAPS = 5
SLOTS = 16
NFFT = 510
LAGS = 201
LAG_ROWS = 208
PLANE = 4
QG = 16
BOTH = ("chan", "tm")
F32 = jnp.float32
BF16 = jnp.bfloat16
VMEM_LIMIT = 56 * 1024 * 1024
PAIR_LIST = (
    [(2, 3), (2, 4), (2, 5), (3, 4), (3, 5), (4, 5)]
    + [(2, 6), (3, 6), (4, 6), (5, 6), (3, 7), (4, 7), (5, 7)]
    + [(0, 4), (1, 4), (1, 5)]
)
N_PAIRS = len(PAIR_LIST)


def split_np(table):
    high = table.astype(np.float32).astype(ml_dtypes.bfloat16)
    low = (table - high.astype(np.float64)).astype(np.float32).astype(ml_dtypes.bfloat16)
    return high, low


def forward_np():
    sample = np.arange(SEG)[:, None]
    bins = np.arange(SEG)[None, :]
    angle = (sample * bins % NFFT) * (2.0 * math.pi / NFFT)
    table = np.concatenate([np.cos(angle), -np.sin(angle)], axis=1)
    return table.astype(np.float32).astype(ml_dtypes.bfloat16)


def inverse_np(scale):
    lag = np.arange(LAG_ROWS)[:, None] - MAXLAG
    bins = np.arange(SEG)[None, :]
    angle = (lag * bins % NFFT) * (2.0 * math.pi / NFFT)
    weight = np.where((bins == 0) | (bins == SEG - 1), 1.0, 2.0) / NFFT * scale
    table = np.concatenate([weight * np.cos(angle), -weight * np.sin(angle)], axis=1)
    table[LAGS:] = 0.0
    return split_np(table)


def reverse_np():
    rows = np.arange(LAG_ROWS)
    table = (rows[:, None] + rows[None, :] == LAGS - 1).astype(np.float32)
    return table.astype(ml_dtypes.bfloat16)


def split_terms(value):
    high = value.astype(BF16)
    low = (value - high.astype(F32)).astype(BF16)
    return high, low


def mxu(a, b):
    return jnp.dot(a, b, preferred_element_type=F32)


def my_place():
    return lax.axis_index("chan") % PLANE, lax.axis_index("tm")


def pair_id(first, second, plane):
    low, high = jnp.minimum(first, second), jnp.maximum(first, second)
    low_plane, low_at = low // PLANE, low % PLANE
    high_plane, high_at = high // PLANE, high % PLANE
    near = (low_plane == high_plane) | (high_at < 2)
    handler = jnp.where(near, low_plane, high_plane)
    left = jnp.where(near, low_at + 2, low_at - 2)
    right = jnp.where(low_plane == high_plane, high_at + 2, jnp.where(near, high_at + 6, high_at + 2))
    index = jnp.int32(0)
    for k, (a, b) in enumerate(PAIR_LIST):
        index = jnp.where((left == a) & (right == b), k, index)
    return (handler - plane + 1) * N_PAIRS + index


def prepare_kernel(taps, pairs, t_high, t_low, pid):
    plane = lax.axis_index("chan") // PLANE
    tap = (
        lax.broadcasted_iota(jnp.int32, (2 * SEG, SEG), 0)
        - lax.broadcasted_iota(jnp.int32, (2 * SEG, SEG), 1)
        - (SEG // 2 - (TAPS - 1) // 2)
    )
    table = jnp.zeros((2 * SEG, SEG), F32)
    for j in range(TAPS):
        table = jnp.where(tap == j, taps[j], table)
    t_high[...], t_low[...] = split_terms(table)
    slot = lax.broadcasted_iota(jnp.int32, pid.shape, 1) >> 4
    ids = jnp.zeros(pid.shape, jnp.int32)
    for s in range(SLOTS):
        ids = jnp.where(slot == s, pair_id(pairs[s, 0], pairs[s, 1], plane), ids)
    pid[...] = ids.astype(F32).astype(BF16)


def filter_kernel(
    space, own, other, halo_own, halo_other, ok, t_high, t_low, pid,
    out_0, out_1, out_2, out_3, x_high, x_low, edge, white, ok_column,
):
    member, core = my_place()
    half = own.shape[1]
    rows = own.shape[0] // 2
    pad = SEG // 2
    first_row = pl.multiple_of(core * rows, rows)
    edge_row = pl.multiple_of(rows - 8 + 8 * (1 - core), 8)
    zeros = jnp.zeros((rows + 16, pad), BF16)
    total = 2 * half
    for buf in (x_high, x_low):
        buf[:, 0:pad] = zeros
        buf[:, pad + total : 2 * pad + total] = zeros
    width = ok.shape[1]
    diagonal = lax.broadcasted_iota(jnp.int32, (width, width), 0) == lax.broadcasted_iota(
        jnp.int32, (width, width), 1
    )
    spread = jnp.where(diagonal, ok[...].astype(F32), 0.0)
    ok_column[...] = jnp.broadcast_to(jnp.sum(spread, axis=1, keepdims=True), ok_column.shape)
    ok_rows = ok_column[pl.ds(first_row, rows), 0:1]
    ok_edge = ok_column[pl.ds(edge_row, 8), 0:1]
    for source, halo, slot in ((own, halo_own, core), (other, halo_other, 1 - core)):
        lanes = pl.ds(pl.multiple_of(pad + slot * half, pad), half)
        high, low = split_terms(source[pl.ds(first_row, rows), :] * ok_rows)
        x_high[0:rows, lanes] = high
        x_low[0:rows, lanes] = low
        for k in range(4):
            edge[2 * k : 2 * k + 2, :] = halo[...]
        near = source[pl.ds(edge_row, 8), :] * ok_edge
        far = edge[...]
        is_low = core == 0
        tile = jnp.concatenate([jnp.where(is_low, far, near), jnp.where(is_low, near, far)], axis=0)
        high, low = split_terms(tile)
        x_high[rows : rows + 16, lanes] = high
        x_low[rows : rows + 16, lanes] = low
    segs = total // SEG
    chunk = 8
    height = rows + 16

    def body(step, carry):
        seg0 = step * chunk
        high = jnp.concatenate(
            [x_high[:, pl.ds(pl.multiple_of((seg0 + s) * SEG, SEG), 2 * SEG)] for s in range(chunk)], axis=0
        )
        low = jnp.concatenate(
            [x_low[:, pl.ds(pl.multiple_of((seg0 + s) * SEG, SEG), 2 * SEG)] for s in range(chunk)], axis=0
        )
        y = mxu(high, t_high[...]) + mxu(low, t_high[...]) + mxu(high, t_low[...])
        for s in range(chunk):
            block = y[s * height : (s + 1) * height]
            ext = jnp.concatenate(
                [block[rows : rows + 8], block[0:rows], block[rows + 8 : rows + 16]], axis=0
            )
            filtered = space[0] * ext[6 : 6 + rows]
            for j in range(1, STAPS):
                filtered = filtered + space[j] * ext[6 + j : 6 + j + rows]
            power = jnp.mean(filtered * filtered, axis=1, keepdims=True)
            white[seg0 + s] = (filtered * (1.0 / jnp.sqrt(power + 1e-5))).astype(BF16)
        return carry

    lax.fori_loop(0, segs // chunk, body, 0)
    for rel, out in enumerate((out_0, out_1, out_2, out_3)):
        row = pl.multiple_of((member ^ rel) * QG, QG)
        out[0:segs] = white[:, pl.ds(row, QG), :]
        out[segs] = pid[...]


def pair_kernel(b0, b1, b2, b3, z0, z1, z2, z3, table, l_high, l_low, out, spec, cross):
    member, _ = my_place()
    segs = spec.shape[1]
    for rel, ref in enumerate((b0, b1, b2, b3)):
        slot = 2 + (member ^ rel)
        value = mxu(ref[0:segs].reshape(segs * QG, SEG), table[...])
        spec[slot] = value.astype(BF16).astype(F32).reshape(segs, QG, 2 * SEG)
    for rel, ref in enumerate((z0, z1, z2, z3)):
        block = member ^ rel
        slot = jnp.where(block < 2, block + 6, block - 2)
        value = mxu(ref[0:segs].reshape(segs * QG, SEG), table[...])
        spec[slot] = value.astype(BF16).astype(F32).reshape(segs, QG, 2 * SEG)
    for q8 in range(QG // 8):
        for part in range(SEG // 128):
            rows = slice(q8 * 8, q8 * 8 + 8)
            re_lanes = slice(part * 128, part * 128 + 128)
            im_lanes = slice(SEG + part * 128, SEG + part * 128 + 128)

            def body(seg, sums):
                real = [spec[w, seg, rows, re_lanes] for w in range(8)]
                imag = [spec[w, seg, rows, im_lanes] for w in range(8)]
                out_sums = []
                for index, (a, b) in enumerate(PAIR_LIST):
                    out_sums.append(sums[2 * index] + (real[a] * real[b] + imag[a] * imag[b]))
                    out_sums.append(sums[2 * index + 1] + (imag[a] * real[b] - real[a] * imag[b]))
                return tuple(out_sums)

            zero = jnp.zeros((8, 128), F32)
            sums = lax.fori_loop(0, segs, body, (zero,) * (2 * N_PAIRS), unroll=2)
            for index in range(N_PAIRS):
                at = slice(index * QG + q8 * 8, index * QG + q8 * 8 + 8)
                cross[at, re_lanes] = sums[2 * index]
                cross[at, im_lanes] = sums[2 * index + 1]
    high, low = split_terms(cross[...])

    def turned(left, right):
        return lax.dot_general(left, right, (((1,), (1,)), ((), ())), preferred_element_type=F32)

    lagged = turned(l_high[...], high) + turned(l_high[...], low) + turned(l_low[...], high)
    out[...] = lagged.astype(BF16)


def select_kernel(below, here, above, pid_0, pid_1, pid_2, pid_3, *refs):
    outs, picked = refs[:8], refs[8]
    _, core = my_place()
    width = N_PAIRS * QG
    row_id = lax.broadcasted_iota(jnp.int32, (3 * width, SLOTS * QG), 0)
    col_id = lax.broadcasted_iota(jnp.int32, (3 * width, SLOTS * QG), 1)
    row_pair = (row_id >> 4).astype(F32)
    same_q = (row_id & 15) == (col_id & 15)
    row_key = jnp.where(same_q, row_pair, -1.0)
    lags = jnp.concatenate([below[...], here[...], above[...]], axis=1)
    for rel, pid in enumerate((pid_0, pid_1, pid_2, pid_3)):
        ids = pid[0].astype(F32)[0:1, :]
        chosen = jnp.where(row_key == ids, 1.0, 0.0).astype(BF16)
        picked[...] = mxu(lags, chosen).astype(BF16)
        for side in range(2):
            lane = pl.multiple_of((core ^ side) * 128, 128)
            outs[2 * rel + side][...] = picked[:, pl.ds(lane, 128)]


def finish_kernel(pairs, count, *refs):
    pieces, table, out, stage, flat, done, sems = refs[:8], *refs[8:14]
    member, core = my_place()
    for rel in range(4):
        for side in range(2):
            spot = (core ^ side) * 4 + (member ^ rel)
            stage[spot] = pieces[2 * rel + side][...].astype(F32)
    group = lax.broadcasted_iota(jnp.int32, (LAG_ROWS, 128), 1) >> 4
    for s in range(SLOTS // 2):
        value = jnp.zeros((LAG_ROWS, 128), F32)
        for m in range(8):
            shift = ((m - s) * QG) % 128
            piece = stage[m]
            moved = pltpu.roll(piece, shift, 1) if shift else piece
            value = jnp.where(group == m, moved, value)
        flat[:, s * 128 : (s + 1) * 128] = value
    back = mxu(table[...], flat[...].astype(BF16))
    copies = []
    for s in range(SLOTS // 2):
        lanes = slice(s * 128, (s + 1) * 128)
        slot = core * (SLOTS // 2) + s
        value = jnp.where(pairs[slot, 0] > pairs[slot, 1], back[:, lanes], flat[:, lanes])
        done[s] = jnp.where(slot < count[0], value, 0.0)[0:LAGS]
        copies.append(pltpu.make_async_copy(done.at[s], out.at[s], sems.at[s]))
        copies[-1].start()
    for copy in copies:
        copy.wait()


VM = pl.BlockSpec(memory_space=pltpu.VMEM)
SM = pl.BlockSpec(memory_space=pltpu.SMEM)
PARAMS = pltpu.CompilerParams(vmem_limit_bytes=VMEM_LIMIT)


def shape(dims, kind):
    return jax.ShapeDtypeStruct(dims, kind)


def local(traces, channel_ok, time_taps, space_taps, pair_blocks, pair_count):
    n_chan = lax.axis_size("chan")
    chan_width, half = traces.shape
    segs = 2 * half // SEG
    core = lax.axis_index("tm")

    def to_core(x):
        return lax.ppermute(x, "tm", [(0, 1), (1, 0)])

    def in_plane(x, rel, side=0):
        if rel == 0 and side == 0:
            return x
        route = [(k, k ^ (2 * rel + side)) for k in range(2 * n_chan)]
        return lax.ppermute(x, BOTH, route)

    def to_next_plane(x, rel):
        route = []
        for c in range(n_chan):
            target = c - PLANE if (c ^ rel) % PLANE < 2 else c + PLANE
            if 0 <= target < n_chan:
                route.append((c, target))
        return lax.ppermute(x, "chan", route)

    other = to_core(traces)
    ok = channel_ok.astype(F32)
    head = traces[0:2] * ok[0:2, None]
    tail = traces[chan_width - 2 :] * ok[chan_width - 2 :, None]
    same_half, cross_half = [], []
    for c in range(n_chan):
        if c + 1 < n_chan:
            same_half.append((2 * c, 2 * c + 2))
            cross_half.append((2 * c + 1, 2 * c + 2))
        if c > 0:
            same_half.append((2 * c + 1, 2 * c - 1))
            cross_half.append((2 * c, 2 * c - 1))
    halo_own = lax.ppermute(jnp.where(core == 0, tail, head), BOTH, same_half)
    halo_other = lax.ppermute(jnp.where(core == 0, head, tail), BOTH, cross_half)
    table = shape((2 * SEG, SEG), BF16)
    t_high, t_low, pid = pl.pallas_call(
        prepare_kernel,
        out_shape=[table, table, shape((QG, SLOTS * QG), BF16)],
        in_specs=[SM, SM],
        out_specs=[VM] * 3,
        compiler_params=PARAMS,
        name="prepare",
    )(time_taps, pair_blocks)
    block = shape((segs + 1, QG, SEG), BF16)
    rows = chan_width // 2
    sent = pl.pallas_call(
        filter_kernel,
        out_shape=[block] * 4,
        in_specs=[SM] + [VM] * 8,
        out_specs=[VM] * 4,
        scratch_shapes=[
            pltpu.VMEM((rows + 16, 2 * half + SEG), BF16),
            pltpu.VMEM((rows + 16, 2 * half + SEG), BF16),
            pltpu.VMEM((8, half), F32),
            pltpu.VMEM((segs, rows, SEG), BF16),
            pltpu.VMEM((chan_width, 128), F32),
        ],
        compiler_params=PARAMS,
        name="filter_whiten",
    )(space_taps, traces, other, halo_own, halo_other, channel_ok[None, :], t_high, t_low, pid)
    blocks = [in_plane(x, rel) for rel, x in enumerate(sent)]
    far = [to_next_plane(x, rel) for rel, x in enumerate(blocks)]
    scale = 1.0 / math.sqrt(segs * SEG)
    l_high, l_low = inverse_np(scale)
    lags = pl.pallas_call(
        pair_kernel,
        out_shape=shape((LAG_ROWS, N_PAIRS * QG), BF16),
        in_specs=[VM] * 11,
        out_specs=VM,
        scratch_shapes=[
            pltpu.VMEM((8, segs, QG, 2 * SEG), F32),
            pltpu.VMEM((N_PAIRS * QG, 2 * SEG), F32),
        ],
        compiler_params=PARAMS,
        name="pair_lags",
    )(*blocks, *far, jnp.asarray(forward_np()), jnp.asarray(l_high), jnp.asarray(l_low))
    below = lax.ppermute(lags, "chan", [(c, c + PLANE) for c in range(n_chan - PLANE)])
    above = lax.ppermute(lags, "chan", [(c + PLANE, c) for c in range(n_chan - PLANE)])
    pid_spec = pl.BlockSpec((1, QG, SEG), lambda step: (segs, 0, 0))
    picked = pl.pallas_call(
        select_kernel,
        grid=(1,),
        out_shape=[shape((LAG_ROWS, 128), BF16)] * 8,
        in_specs=[VM] * 3 + [pid_spec] * 4,
        out_specs=[VM] * 8,
        scratch_shapes=[pltpu.VMEM((LAG_ROWS, SLOTS * QG), BF16)],
        compiler_params=PARAMS,
        name="select_slots",
    )(below, lags, above, *blocks)
    pieces = [in_plane(x, k // 2, k % 2) for k, x in enumerate(picked)]
    return pl.pallas_call(
        finish_kernel,
        out_shape=shape((SLOTS // 2, LAGS, chan_width), F32),
        in_specs=[SM] * 2 + [VM] * 9,
        out_specs=pl.BlockSpec(memory_space=pl.ANY),
        scratch_shapes=[
            pltpu.VMEM((8, LAG_ROWS, 128), F32),
            pltpu.VMEM((LAG_ROWS, SLOTS // 2 * 128), F32),
            pltpu.VMEM((SLOTS // 2, LAGS, 128), F32),
            pltpu.SemaphoreType.DMA((SLOTS // 2,)),
        ],
        compiler_params=PARAMS,
        name="finish_slots",
    )(pair_blocks, pair_count, *pieces, jnp.asarray(reverse_np()))


def solution(mesh):
    return jax.shard_map(
        local,
        mesh=mesh,
        in_specs=(P("chan", "tm"), P("chan"), P(), P(), P("chan", None), P("chan")),
        out_specs=P(("chan", "tm"), None, None),
        check_vma=False,
    )
```

```python
import math

import jax
import jax.numpy as jnp
import ml_dtypes
import numpy as np
from jax import lax
from jax.experimental import pallas as pl
from jax.experimental.pallas import tpu as pltpu
from jax.sharding import PartitionSpec as P

SEG = 256
MAXLAG = 100
TAPS = 33
STAPS = 5
SLOTS = 16
NFFT = 510
LAGS = 201
LAG_ROWS = 208
PLANE = 4
QG = 16
BOTH = ("chan", "tm")
F32 = jnp.float32
BF16 = jnp.bfloat16
VMEM_LIMIT = 56 * 1024 * 1024
INNER = [(0, 1), (0, 2), (0, 3), (1, 2), (1, 3), (2, 3)]
CROSS = [(i, j) for i in range(PLANE) for j in range(i + 1)]
N_IN, N_CROSS = len(INNER), len(CROSS)
N_OWN = N_CROSS + N_IN + N_CROSS
N_SENT = N_IN + N_CROSS
N_ALL = N_OWN + 2 * N_SENT


def split_np(table):
    high = table.astype(np.float32).astype(ml_dtypes.bfloat16)
    low = (table - high.astype(np.float64)).astype(np.float32).astype(ml_dtypes.bfloat16)
    return high, low


def forward_np():
    sample = np.arange(SEG)[:, None]
    bins = np.arange(SEG)[None, :]
    angle = (sample * bins % NFFT) * (2.0 * math.pi / NFFT)
    table = np.concatenate([np.cos(angle), -np.sin(angle)], axis=1)
    return table.astype(np.float32).astype(ml_dtypes.bfloat16)


def inverse_np(scale):
    lag = np.arange(LAG_ROWS)[:, None] - MAXLAG
    bins = np.arange(SEG)[None, :]
    angle = (lag * bins % NFFT) * (2.0 * math.pi / NFFT)
    weight = np.where((bins == 0) | (bins == SEG - 1), 1.0, 2.0) / NFFT * scale
    table = np.concatenate([weight * np.cos(angle), -weight * np.sin(angle)], axis=1)
    table[LAGS:] = 0.0
    return split_np(table)


def reverse_np():
    rows = np.arange(LAG_ROWS)
    table = (rows[:, None] + rows[None, :] == LAGS - 1).astype(np.float32)
    return table.astype(ml_dtypes.bfloat16)


def split_terms(value):
    high = value.astype(BF16)
    low = (value - high.astype(F32)).astype(BF16)
    return high, low


def mxu(a, b):
    return jnp.dot(a, b, preferred_element_type=F32)


def my_place():
    chan = lax.axis_index("chan")
    return chan % PLANE, lax.axis_index("tm"), (chan // PLANE) % 2


def pair_ids(first, second, plane):
    low, high = jnp.minimum(first, second), jnp.maximum(first, second)
    low_plane, low_at = low // PLANE - plane, low % PLANE
    high_plane, high_at = high // PLANE - plane, high % PLANE
    inner = jnp.int32(0)
    for k, (i, j) in enumerate(INNER):
        inner = jnp.where((low_at == i) & (high_at == j), k, inner)
    cross = low_at * (low_at + 1) // 2 + high_at
    one = jnp.where(
        low_plane == 0,
        jnp.where(high_plane == 0, N_CROSS + inner, N_CROSS + N_IN + cross),
        jnp.where(
            low_plane > 0,
            N_OWN + N_SENT + N_CROSS + inner,
            jnp.where(high_plane == 0, cross, N_OWN + inner),
        ),
    )
    two = jnp.where(
        low_plane == high_plane,
        N_ALL,
        jnp.where(low_plane == 0, N_OWN + N_SENT + cross, N_OWN + N_IN + cross),
    )
    return one, two


def prepare_kernel(taps, pairs, t_high, t_low, pid):
    plane = lax.axis_index("chan") // PLANE
    tap = (
        lax.broadcasted_iota(jnp.int32, (2 * SEG, SEG), 0)
        - lax.broadcasted_iota(jnp.int32, (2 * SEG, SEG), 1)
        - (SEG // 2 - (TAPS - 1) // 2)
    )
    table = jnp.zeros((2 * SEG, SEG), F32)
    for j in range(TAPS):
        table = jnp.where(tap == j, taps[j], table)
    t_high[...], t_low[...] = split_terms(table)
    slot = lax.broadcasted_iota(jnp.int32, pid.shape, 1) >> 4
    upper = lax.broadcasted_iota(jnp.int32, pid.shape, 0) < 8
    ids = jnp.zeros(pid.shape, jnp.int32)
    for s in range(SLOTS):
        one, two = pair_ids(pairs[0, s], pairs[1, s], plane)
        ids = jnp.where(slot == s, jnp.where(upper, one, two), ids)
    pid[...] = ids.astype(F32).astype(BF16)


def filter_kernel(
    space, own, other, halos, ok, t_high, t_low, pid,
    out_first, out_second, out_1, out_2, out_3, x_high, x_low, edge, white, ok_column,
):
    member, core, odd = my_place()
    half = own.shape[1]
    rows = own.shape[0] // 2
    pad = SEG // 2
    first_row = pl.multiple_of(core * rows, rows)
    edge_row = pl.multiple_of(rows - 8 + 8 * (1 - core), 8)
    zeros = jnp.zeros((rows + 16, pad), BF16)
    total = 2 * half
    for buf in (x_high, x_low):
        buf[:, 0:pad] = zeros
        buf[:, pad + total : 2 * pad + total] = zeros
    width = ok.shape[1]
    diagonal = lax.broadcasted_iota(jnp.int32, (width, width), 0) == lax.broadcasted_iota(
        jnp.int32, (width, width), 1
    )
    spread = jnp.where(diagonal, ok[...].astype(F32), 0.0)
    ok_column[...] = jnp.broadcast_to(jnp.sum(spread, axis=1, keepdims=True), ok_column.shape)
    ok_rows = ok_column[pl.ds(first_row, rows), 0:1]
    ok_edge = ok_column[pl.ds(edge_row, 8), 0:1]
    for source, halo, slot in ((own, halos[2:4], core), (other, halos[0:2], 1 - core)):
        lanes = pl.ds(pl.multiple_of(pad + slot * half, pad), half)
        high, low = split_terms(source[pl.ds(first_row, rows), :] * ok_rows)
        x_high[0:rows, lanes] = high
        x_low[0:rows, lanes] = low
        for k in range(4):
            edge[2 * k : 2 * k + 2, :] = halo
        near = source[pl.ds(edge_row, 8), :] * ok_edge
        far = edge[...]
        is_low = core == 0
        tile = jnp.concatenate([jnp.where(is_low, far, near), jnp.where(is_low, near, far)], axis=0)
        high, low = split_terms(tile)
        x_high[rows : rows + 16, lanes] = high
        x_low[rows : rows + 16, lanes] = low
    segs = total // SEG
    chunk = 8
    height = rows + 16

    def body(step, carry):
        seg0 = step * chunk
        high = jnp.concatenate(
            [x_high[:, pl.ds(pl.multiple_of((seg0 + s) * SEG, SEG), 2 * SEG)] for s in range(chunk)], axis=0
        )
        low = jnp.concatenate(
            [x_low[:, pl.ds(pl.multiple_of((seg0 + s) * SEG, SEG), 2 * SEG)] for s in range(chunk)], axis=0
        )
        y = mxu(high, t_high[...]) + mxu(low, t_high[...]) + mxu(high, t_low[...])
        for s in range(chunk):
            block = y[s * height : (s + 1) * height]
            ext = jnp.concatenate(
                [block[rows : rows + 8], block[0:rows], block[rows + 8 : rows + 16]], axis=0
            )
            filtered = space[0] * ext[6 : 6 + rows]
            for j in range(1, STAPS):
                filtered = filtered + space[j] * ext[6 + j : 6 + j + rows]
            power = jnp.mean(filtered * filtered, axis=1, keepdims=True)
            white[seg0 + s] = (filtered * (1.0 / jnp.sqrt(power + 1e-5))).astype(BF16)
        return carry

    lax.fori_loop(0, segs // chunk, body, 0)
    own_row = pl.multiple_of(member * QG, QG)
    part = segs // 2
    out_first[...] = white[pl.ds((1 - odd) * part, part), pl.ds(own_row, QG), :]
    out_second[...] = white[pl.ds(odd * part, part), pl.ds(own_row, QG), :]
    for rel, out in ((1, out_1), (2, out_2), (3, out_3)):
        row = pl.multiple_of((member ^ rel) * QG, QG)
        out[0:segs] = white[:, pl.ds(row, QG), :]
        out[segs] = pid[...]


def pair_kernel(
    first, second, b1, b2, b3, near_0, far_0, near_1, far_1, near_2, far_2, near_3, far_3, table, l_high, l_low,
    out, out_first, out_second, spec, spec_z, cross,
):
    member, _, odd = my_place()
    segs = spec.shape[1]
    part = segs // 2

    def transform(block):
        value = mxu(block.reshape(block.shape[0] * QG, SEG), table[...])
        return value.astype(BF16).astype(F32).reshape(block.shape[0], QG, 2 * SEG)

    spec[member, pl.ds((1 - odd) * part, part)] = transform(first[...])
    spec[member, pl.ds(odd * part, part)] = transform(second[...])
    for rel, ref in ((1, b1), (2, b2), (3, b3)):
        spec[member ^ rel] = transform(ref[0:segs])
    for side, refs in ((odd, (near_0, near_1, near_2, near_3)), (1 - odd, (far_0, far_1, far_2, far_3))):
        for rel, ref in enumerate(refs):
            spec_z[side, member ^ rel] = transform(ref[...])
    for q8 in range(QG // 8):
        for lanes in range(SEG // 128):
            rows = slice(q8 * 8, q8 * 8 + 8)
            re_lanes = slice(lanes * 128, lanes * 128 + 128)
            im_lanes = slice(SEG + lanes * 128, SEG + lanes * 128 + 128)

            def add(sums, index, left, right):
                re = sums[2 * index] + (left[0] * right[0] + left[1] * right[1])
                im = sums[2 * index + 1] + (left[1] * right[0] - left[0] * right[1])
                return [re, im]

            def sweep(side, sums):
                def body(seg, sums):
                    at = seg + side * part
                    mine = [(spec[w, at, rows, re_lanes], spec[w, at, rows, im_lanes]) for w in range(PLANE)]
                    theirs = [
                        (spec_z[side, w, seg, rows, re_lanes], spec_z[side, w, seg, rows, im_lanes])
                        for w in range(PLANE)
                    ]
                    low, high = (theirs, mine) if side else (mine, theirs)
                    result = []
                    for k, (i, j) in enumerate(INNER):
                        result += add(sums, k, mine[i], mine[j])
                    for k, (i, j) in enumerate(CROSS):
                        result += add(sums, N_IN + k, low[i], high[j])
                    return tuple(result)

                return lax.fori_loop(0, part, body, sums, unroll=2)

            zero = jnp.zeros((8, 128), F32)
            up = sweep(0, (zero,) * (2 * N_SENT))
            down = sweep(1, up[: 2 * N_IN] + (zero,) * (2 * N_CROSS))
            order = down[2 * N_IN :] + down[: 2 * N_IN] + up[2 * N_IN :]
            for index in range(N_OWN):
                at = slice(index * QG + q8 * 8, index * QG + q8 * 8 + 8)
                cross[at, re_lanes] = order[2 * index]
                cross[at, im_lanes] = order[2 * index + 1]
    high, low = split_terms(cross[...])

    def turned(left, right):
        return lax.dot_general(left, right, (((1,), (1,)), ((), ())), preferred_element_type=F32)

    lagged = turned(l_high[...], high) + turned(l_high[...], low) + turned(l_low[...], high)
    out[...] = lagged.astype(BF16)
    to_above = lagged[:, N_CROSS * QG :]
    to_below = lagged[:, : N_SENT * QG]
    out_first[...] = jnp.where(odd == 1, to_below, to_above).astype(BF16)
    out_second[...] = jnp.where(odd == 1, to_above, to_below).astype(BF16)


def select_kernel(*refs):
    mine, swapped, pids, outs = refs[0:3], refs[3:6], refs[6:10], refs[10:14]
    chosen, lags = refs[14:16]
    _, core, odd = my_place()
    own, sent = N_OWN * QG, N_SENT * QG
    row_id = lax.broadcasted_iota(jnp.int32, (N_ALL * QG, 128), 0)
    col_id = lax.broadcasted_iota(jnp.int32, (N_ALL * QG, 128), 1)
    row_key = jnp.where((row_id & 15) == (col_id & 15), (row_id >> 4).astype(F32), -1.0)
    lane = pl.multiple_of(core * 128, 128)
    for rel, pid in enumerate(pids):
        ids = pid[0, :, pl.ds(lane, 128)].astype(F32)
        match = (row_key == ids[0:1, :]) | (row_key == ids[8:9, :])
        chosen[:, rel * 128 : (rel + 1) * 128] = jnp.where(match, 1.0, 0.0).astype(BF16)
    for side, (here, first, second) in enumerate((mine, swapped)):
        at = slice(side * LAG_ROWS, (side + 1) * LAG_ROWS)
        below = jnp.where(odd == 1, first[...].astype(F32), second[...].astype(F32)).astype(BF16)
        above = jnp.where(odd == 1, second[...].astype(F32), first[...].astype(F32)).astype(BF16)
        lags[at, 0:own] = here[...]
        lags[at, own : own + sent] = below
        lags[at, own + sent : own + 2 * sent] = above
    picked = mxu(lags[...], chosen[...]).astype(BF16)
    for rel in range(4):
        for side in range(2):
            outs[rel][side] = picked[side * LAG_ROWS : (side + 1) * LAG_ROWS, rel * 128 : (rel + 1) * 128]


def finish_kernel(pairs, count, *refs):
    pieces, table, out, stage, flat = refs[:4], *refs[4:8]
    member, core, _ = my_place()
    for rel in range(4):
        for side in range(2):
            stage[(core ^ side) * 4 + (member ^ rel)] = pieces[rel][side].astype(F32)
    group = lax.broadcasted_iota(jnp.int32, (LAG_ROWS, 128), 1) >> 4
    for s in range(SLOTS // 2):
        value = jnp.zeros((LAG_ROWS, 128), F32)
        for m in range(8):
            shift = ((m - s) * QG) % 128
            piece = stage[m]
            moved = pltpu.roll(piece, shift, 1) if shift else piece
            value = jnp.where(group == m, moved, value)
        flat[:, s * 128 : (s + 1) * 128] = value
    back = mxu(table[...], flat[...].astype(BF16))
    for s in range(SLOTS // 2):
        lanes = slice(s * 128, (s + 1) * 128)
        slot = core * (SLOTS // 2) + s
        value = jnp.where(pairs[0, slot] > pairs[1, slot], back[:, lanes], flat[:, lanes])
        out[:, s, :] = jnp.where(slot < count[0], value, 0.0)[0:LAGS]


VM = pl.BlockSpec(memory_space=pltpu.VMEM)
SM = pl.BlockSpec(memory_space=pltpu.SMEM)
PARAMS = pltpu.CompilerParams(vmem_limit_bytes=VMEM_LIMIT)


def shape(dims, kind):
    return jax.ShapeDtypeStruct(dims, kind)


def local(traces, channel_ok, time_taps, space_taps, pair_blocks, pair_count):
    n_chan = lax.axis_size("chan")
    n_plane = n_chan // PLANE
    chan_width, half = traces.shape
    segs = 2 * half // SEG
    part = segs // 2
    core = lax.axis_index("tm")
    odd = (lax.axis_index("chan") // PLANE) % 2
    pairs = jnp.transpose(pair_blocks)

    def to_core(x):
        return lax.ppermute(x, "tm", [(0, 1), (1, 0)])

    def in_plane(x, rel):
        return lax.ppermute(x, "chan", [(c, c ^ rel) for c in range(n_chan)])

    def plane_swap(x, start):
        route = []
        for p in range(start, n_plane - 1, 2):
            for k in range(PLANE):
                low, high = p * PLANE + k, (p + 1) * PLANE + k
                route += [(low, high), (high, low)]
        return lax.ppermute(x, "chan", route)

    ok = channel_ok.astype(F32)
    head = traces[0:2] * ok[0:2, None]
    tail = traces[chan_width - 2 :] * ok[chan_width - 2 :, None]
    got = to_core(jnp.where(core == 0, tail, head))
    mine = jnp.where(core == 0, head, tail)
    got, late = lax.optimization_barrier((got, traces))
    route = []
    for c in range(n_chan - 1):
        route += [(2 * c + 1, 2 * c + 2), (2 * c + 2, 2 * c + 1)]
    halos = lax.ppermute(jnp.concatenate([mine, got], axis=0), BOTH, route)
    other = to_core(late)
    table = shape((2 * SEG, SEG), BF16)
    t_high, t_low, pid = pl.pallas_call(
        prepare_kernel,
        out_shape=[table, table, shape((QG, SLOTS * QG), BF16)],
        in_specs=[SM, SM],
        out_specs=[VM] * 3,
        compiler_params=PARAMS,
        name="prepare",
    )(time_taps, pairs)
    block = shape((segs + 1, QG, SEG), BF16)
    short = shape((part, QG, SEG), BF16)
    rows = chan_width // 2
    first, second, *sent = pl.pallas_call(
        filter_kernel,
        out_shape=[short] * 2 + [block] * 3,
        in_specs=[SM] + [VM] * 7,
        out_specs=[VM] * 5,
        scratch_shapes=[
            pltpu.VMEM((rows + 16, 2 * half + SEG), BF16),
            pltpu.VMEM((rows + 16, 2 * half + SEG), BF16),
            pltpu.VMEM((8, half), F32),
            pltpu.VMEM((segs, rows, SEG), BF16),
            pltpu.VMEM((chan_width, 128), F32),
        ],
        compiler_params=PARAMS,
        name="filter_whiten",
    )(space_taps, traces, other, halos, channel_ok[None, :], t_high, t_low, pid)
    b1, b2, b3 = [in_plane(x, rel + 1) for rel, x in enumerate(sent)]

    def halves(x):
        near = lax.dynamic_slice_in_dim(x, (1 - odd) * part, part, axis=0)
        far = lax.dynamic_slice_in_dim(x, odd * part, part, axis=0)
        return near, far

    near_0, far_0 = plane_swap(first, 0), plane_swap(second, 1)
    b1, near_0, far_0 = lax.optimization_barrier((b1, near_0, far_0))
    (near_1, far_1), (near_2, far_2), (near_3, far_3) = halves(b1), halves(b2), halves(b3)
    near_1, far_1 = plane_swap(near_1, 0), plane_swap(far_1, 1)
    near_2, far_2 = plane_swap(near_2, 0), plane_swap(far_2, 1)
    near_3, far_3 = plane_swap(near_3, 0), plane_swap(far_3, 1)
    scale = 1.0 / math.sqrt(segs * SEG)
    l_high, l_low = inverse_np(scale)
    sent_shape = shape((LAG_ROWS, N_SENT * QG), BF16)
    lags, lags_first, lags_second = pl.pallas_call(
        pair_kernel,
        out_shape=[shape((LAG_ROWS, N_OWN * QG), BF16), sent_shape, sent_shape],
        in_specs=[VM] * 16,
        out_specs=[VM] * 3,
        scratch_shapes=[
            pltpu.VMEM((PLANE, segs, QG, 2 * SEG), F32),
            pltpu.VMEM((2, PLANE, part, QG, 2 * SEG), F32),
            pltpu.VMEM((N_OWN * QG, 2 * SEG), F32),
        ],
        compiler_params=PARAMS,
        name="pair_lags",
    )(
        first, second, b1, b2, b3, near_0, far_0, near_1, far_1, near_2, far_2, near_3, far_3,
        jnp.asarray(forward_np()), jnp.asarray(l_high), jnp.asarray(l_low),
    )
    from_first, from_second = plane_swap(lags_first, 0), plane_swap(lags_second, 1)
    known = [lags, from_first, from_second]
    pid_spec = pl.BlockSpec((1, QG, SEG), lambda step: (segs, 0, 0))
    own_spec = pl.BlockSpec((1, QG, SEG), lambda step: (0, 0, 0))
    slots_shape = shape((2, LAG_ROWS, 128), BF16)
    picked = pl.pallas_call(
        select_kernel,
        grid=(1,),
        out_shape=[slots_shape] * 4,
        in_specs=[VM] * 6 + [own_spec] + [pid_spec] * 3,
        out_specs=[VM] * 4,
        scratch_shapes=[
            pltpu.VMEM((N_ALL * QG, 512), BF16),
            pltpu.VMEM((2 * LAG_ROWS, N_ALL * QG), BF16),
        ],
        compiler_params=PARAMS,
        name="select_slots",
    )(*known, *[to_core(x) for x in known], pid[None], b1, b2, b3)
    pieces = [picked[0]] + [in_plane(x, rel + 1) for rel, x in enumerate(picked[1:])]
    out = pl.pallas_call(
        finish_kernel,
        out_shape=shape((LAGS, SLOTS // 2, chan_width), F32),
        in_specs=[SM] * 2 + [VM] * 5,
        out_specs=VM,
        scratch_shapes=[
            pltpu.VMEM((8, LAG_ROWS, 128), F32),
            pltpu.VMEM((LAG_ROWS, SLOTS // 2 * 128), F32),
        ],
        compiler_params=PARAMS,
        name="finish_slots",
    )(pairs, pair_count, *pieces, jnp.asarray(reverse_np()))
    return jnp.transpose(out, (1, 0, 2))


def solution(mesh):
    return jax.shard_map(
        local,
        mesh=mesh,
        in_specs=(P("chan", "tm"), P("chan"), P(), P(), P("chan", None), P("chan")),
        out_specs=P(("chan", "tm"), None, None),
        check_vma=False,
    )
```

```python
import math

import jax
import jax.numpy as jnp
import ml_dtypes
import numpy as np
from jax import lax
from jax.experimental import pallas as pl
from jax.experimental.pallas import tpu as pltpu
from jax.sharding import PartitionSpec as P

SEG = 256
MAXLAG = 100
TAPS = 33
STAPS = 5
SLOTS = 16
NFFT = 510
LAGS = 201
LAG_ROWS = 208
PLANE = 4
QG = 16
BOTH = ("chan", "tm")
F32 = jnp.float32
BF16 = jnp.bfloat16
VMEM_LIMIT = 20 * 1024 * 1024
INNER = [(0, 1), (0, 2), (0, 3), (1, 2), (1, 3), (2, 3)]
CROSS = [(i, j) for i in range(PLANE) for j in range(i + 1)]
N_IN, N_CROSS = len(INNER), len(CROSS)
N_OWN = N_CROSS + N_IN + N_CROSS
N_SENT = N_IN + N_CROSS
N_ALL = N_OWN + 2 * N_SENT


def split_np(table):
    high = table.astype(np.float32).astype(ml_dtypes.bfloat16)
    low = (table - high.astype(np.float64)).astype(np.float32).astype(ml_dtypes.bfloat16)
    return high, low


def forward_np():
    sample = np.arange(SEG)[:, None]
    bins = np.arange(SEG)[None, :]
    angle = (sample * bins % NFFT) * (2.0 * math.pi / NFFT)
    table = np.concatenate([np.cos(angle), -np.sin(angle)], axis=1)
    return table.astype(np.float32).astype(ml_dtypes.bfloat16)


def inverse_np(scale):
    lag = np.arange(LAG_ROWS)[:, None] - MAXLAG
    bins = np.arange(SEG)[None, :]
    angle = (lag * bins % NFFT) * (2.0 * math.pi / NFFT)
    weight = np.where((bins == 0) | (bins == SEG - 1), 1.0, 2.0) / NFFT * scale
    table = np.concatenate([weight * np.cos(angle), -weight * np.sin(angle)], axis=1)
    table[LAGS:] = 0.0
    return split_np(table)


def reverse_np():
    rows = np.arange(LAG_ROWS)
    table = (rows[:, None] + rows[None, :] == LAGS - 1).astype(np.float32)
    return table.astype(ml_dtypes.bfloat16)


def split_terms(value):
    high = value.astype(BF16)
    low = (value - high.astype(F32)).astype(BF16)
    return high, low


def mxu(a, b):
    return jnp.dot(a, b, preferred_element_type=F32)


def my_place():
    chan = lax.axis_index("chan")
    return chan % PLANE, lax.axis_index("tm"), (chan // PLANE) % 2


def pair_ids(first, second, plane):
    low, high = jnp.minimum(first, second), jnp.maximum(first, second)
    low_plane, low_at = low // PLANE - plane, low % PLANE
    high_plane, high_at = high // PLANE - plane, high % PLANE
    inner = jnp.int32(0)
    for k, (i, j) in enumerate(INNER):
        inner = jnp.where((low_at == i) & (high_at == j), k, inner)
    cross = low_at * (low_at + 1) // 2 + high_at
    one = jnp.where(
        low_plane == 0,
        jnp.where(high_plane == 0, N_CROSS + inner, N_CROSS + N_IN + cross),
        jnp.where(
            low_plane > 0,
            N_OWN + N_SENT + N_CROSS + inner,
            jnp.where(high_plane == 0, cross, N_OWN + inner),
        ),
    )
    two = jnp.where(
        low_plane == high_plane,
        N_ALL,
        jnp.where(low_plane == 0, N_OWN + N_SENT + cross, N_OWN + N_IN + cross),
    )
    return one, two


def tile_rows(own, core):
    rows = own.shape[0] // 2
    first_row = pl.multiple_of(core * rows, rows)
    near_row = pl.multiple_of(rows - 8 + 8 * (1 - core), 8)
    return pl.ds(first_row, rows), pl.ds(near_row, 8)


def prepare_kernel(small, own, t_high, t_low, pid, space, ok, own_high, own_low):
    _, core, _ = my_place()
    plane = lax.axis_index("chan") // PLANE
    t_high[...] = jnp.zeros(t_high.shape, BF16)
    t_low[...] = jnp.zeros(t_low.shape, BF16)
    shift = SEG // 2 - (TAPS - 1) // 2
    height = 128 + TAPS - 1
    tap = lax.broadcasted_iota(jnp.int32, (height, 128), 0) - lax.broadcasted_iota(
        jnp.int32, (height, 128), 1
    )
    band = jnp.zeros((height, 128), F32)
    for j in range(TAPS):
        band = jnp.where(tap == j, small[j], band)
    high, low = split_terms(band)
    for lanes in range(SEG // 128):
        at = (slice(lanes * 128 + shift, lanes * 128 + shift + height), slice(lanes * 128, lanes * 128 + 128))
        t_high[at] = high
        t_low[at] = low
    row = lax.broadcasted_iota(jnp.int32, space.shape, 0)
    taps = jnp.zeros(space.shape, F32)
    for j in range(STAPS):
        taps = jnp.where(row == j, small[TAPS + j], taps)
    space[...] = taps
    slot = lax.broadcasted_iota(jnp.int32, pid.shape, 1) >> 4
    upper = lax.broadcasted_iota(jnp.int32, pid.shape, 0) < 8
    ids = jnp.zeros(pid.shape, jnp.int32)
    for s in range(SLOTS):
        left = small[TAPS + STAPS + s].astype(jnp.int32)
        right = small[TAPS + STAPS + SLOTS + s].astype(jnp.int32)
        one, two = pair_ids(left, right, plane)
        ids = jnp.where(slot == s, jnp.where(upper, one, two), ids)
    pid[...] = ids.astype(F32).astype(BF16)
    at = lax.broadcasted_iota(jnp.int32, ok.shape, 0)
    values = jnp.zeros(ok.shape, F32)
    for k in range(ok.shape[0]):
        values = jnp.where(at == k, small[TAPS + STAPS + 2 * SLOTS + k], values)
    ok[...] = values
    main, near = tile_rows(own, core)
    own_high[...], own_low[...] = split_terms(own[main, :] * ok[main, 0:1])


def filter_kernel(
    own, own_high, own_low, other, halos, space, ok, t_high, t_low, pid,
    out_first, out_second, out_1, out_2, out_3, x_high, x_low, edge, white,
):
    member, core, odd = my_place()
    half = own.shape[1]
    rows = own_high.shape[0]
    main, near = tile_rows(own, core)
    pad = SEG // 2
    total = 2 * half
    zeros = jnp.zeros((rows + 16, pad), BF16)
    for buf in (x_high, x_low):
        buf[:, 0:pad] = zeros
        buf[:, pad + total : 2 * pad + total] = zeros
    own_lanes = pl.ds(pl.multiple_of(pad + core * half, pad), half)
    other_lanes = pl.ds(pl.multiple_of(pad + (1 - core) * half, pad), half)
    x_high[0:rows, own_lanes] = own_high[...]
    x_low[0:rows, own_lanes] = own_low[...]
    x_high[0:rows, other_lanes], x_low[0:rows, other_lanes] = split_terms(other[main, :] * ok[main, 0:1])
    ok_near = ok[near, 0:1]
    for source, halo, lanes in ((own, halos[2:4], own_lanes), (other, halos[0:2], other_lanes)):
        for k in range(4):
            edge[2 * k : 2 * k + 2, :] = halo
        inside = source[near, :] * ok_near
        outside = edge[...]
        above = jnp.where(core == 0, outside, inside)
        below = jnp.where(core == 0, inside, outside)
        high, low = split_terms(jnp.concatenate([above, below], axis=0))
        x_high[rows : rows + 16, lanes] = high
        x_low[rows : rows + 16, lanes] = low
    segs = total // SEG
    chunk = 8
    height = rows + 16
    taps = [space[j : j + 1, :] for j in range(STAPS)]

    def body(step, carry):
        seg0 = step * chunk
        spans = [pl.ds(pl.multiple_of((seg0 + s) * SEG, SEG), 2 * SEG) for s in range(chunk)]
        high = jnp.concatenate([x_high[:, span] for span in spans], axis=0)
        low = jnp.concatenate([x_low[:, span] for span in spans], axis=0)
        y = mxu(high, t_high[...]) + mxu(low, t_high[...]) + mxu(high, t_low[...])
        for s in range(chunk):
            block = y[s * height : (s + 1) * height]
            ext = jnp.concatenate(
                [block[rows : rows + 8], block[0:rows], block[rows + 8 : rows + 16]], axis=0
            )
            filtered = taps[0] * ext[6 : 6 + rows]
            for j in range(1, STAPS):
                filtered = filtered + taps[j] * ext[6 + j : 6 + j + rows]
            power = jnp.mean(filtered * filtered, axis=1, keepdims=True)
            white[seg0 + s] = (filtered * (1.0 / jnp.sqrt(power + 1e-5))).astype(BF16)
        return carry

    lax.fori_loop(0, segs // chunk, body, 0, unroll=True)
    own_row = pl.multiple_of(member * QG, QG)
    part = segs // 2
    out_first[...] = white[pl.ds((1 - odd) * part, part), pl.ds(own_row, QG), :]
    out_second[...] = white[pl.ds(odd * part, part), pl.ds(own_row, QG), :]
    for rel, out in ((1, out_1), (2, out_2), (3, out_3)):
        row = pl.multiple_of((member ^ rel) * QG, QG)
        out[0:segs] = white[:, pl.ds(row, QG), :]
        out[segs] = pid[...]


def pair_kernel(
    first, second, b1, b2, b3, near_0, far_0, near_12, far_12, near_3, far_3, table, l_high, l_low,
    out, out_first, out_second, spec, spec_z, cross,
):
    member, _, odd = my_place()
    segs = spec.shape[1]
    part = segs // 2

    def transform(block):
        value = mxu(block.reshape(block.shape[0] * QG, SEG), table[...])
        return value.astype(BF16).astype(F32).reshape(block.shape[0], QG, 2 * SEG)

    spec[member, pl.ds((1 - odd) * part, part)] = transform(first[...])
    spec[member, pl.ds(odd * part, part)] = transform(second[...])
    for rel, ref in ((1, b1), (2, b2), (3, b3)):
        spec[member ^ rel] = transform(ref[0:segs])
    for side, refs in ((odd, (near_0, near_12, near_3)), (1 - odd, (far_0, far_12, far_3))):
        spec_z[side, member] = transform(refs[0][...])
        spec_z[side, member ^ 1] = transform(refs[1][0])
        spec_z[side, member ^ 2] = transform(refs[1][1])
        spec_z[side, member ^ 3] = transform(refs[2][...])
    for q8 in range(QG // 8):
        for lanes in range(SEG // 128):
            rows = slice(q8 * 8, q8 * 8 + 8)
            re_lanes = slice(lanes * 128, lanes * 128 + 128)
            im_lanes = slice(SEG + lanes * 128, SEG + lanes * 128 + 128)

            def add(sums, index, left, right):
                re = sums[2 * index] + (left[0] * right[0] + left[1] * right[1])
                im = sums[2 * index + 1] + (left[1] * right[0] - left[0] * right[1])
                return [re, im]

            def sweep(side, sums):
                def body(seg, sums):
                    at = seg + side * part
                    mine = [(spec[w, at, rows, re_lanes], spec[w, at, rows, im_lanes]) for w in range(PLANE)]
                    theirs = [
                        (spec_z[side, w, seg, rows, re_lanes], spec_z[side, w, seg, rows, im_lanes])
                        for w in range(PLANE)
                    ]
                    low, high = (theirs, mine) if side else (mine, theirs)
                    result = []
                    for k, (i, j) in enumerate(INNER):
                        result += add(sums, k, mine[i], mine[j])
                    for k, (i, j) in enumerate(CROSS):
                        result += add(sums, N_IN + k, low[i], high[j])
                    return tuple(result)

                return lax.fori_loop(0, part, body, sums, unroll=4)

            zero = jnp.zeros((8, 128), F32)
            up = sweep(0, (zero,) * (2 * N_SENT))
            down = sweep(1, up[: 2 * N_IN] + (zero,) * (2 * N_CROSS))
            order = down[2 * N_IN :] + down[: 2 * N_IN] + up[2 * N_IN :]
            for index in range(N_OWN):
                at = slice(index * QG + q8 * 8, index * QG + q8 * 8 + 8)
                cross[at, re_lanes] = order[2 * index]
                cross[at, im_lanes] = order[2 * index + 1]
    high, low = split_terms(cross[...])

    def turned(left, right):
        return lax.dot_general(left, right, (((1,), (1,)), ((), ())), preferred_element_type=F32)

    lagged = turned(l_high[...], high) + turned(l_high[...], low) + turned(l_low[...], high)
    out[...] = lagged.astype(BF16)
    to_above = lagged[:, N_CROSS * QG :]
    to_below = lagged[:, : N_SENT * QG]
    out_first[...] = jnp.where(odd == 1, to_below, to_above).astype(BF16)
    out_second[...] = jnp.where(odd == 1, to_above, to_below).astype(BF16)


def select_kernel(*refs):
    mine, swapped, pids, outs = refs[0:3], refs[3:6], refs[6:10], refs[10:14]
    chosen, lags = refs[14:16]
    _, core, odd = my_place()
    own, sent = N_OWN * QG, N_SENT * QG
    row_id = lax.broadcasted_iota(jnp.int32, (N_ALL * QG, 128), 0)
    col_id = lax.broadcasted_iota(jnp.int32, (N_ALL * QG, 128), 1)
    row_key = jnp.where((row_id & 15) == (col_id & 15), (row_id >> 4).astype(F32), -1.0)
    lane = pl.multiple_of(core * 128, 128)
    for rel, pid in enumerate(pids):
        ids = pid[0, :, pl.ds(lane, 128)].astype(F32)
        match = (row_key == ids[0:1, :]) | (row_key == ids[8:9, :])
        chosen[:, rel * 128 : (rel + 1) * 128] = jnp.where(match, 1.0, 0.0).astype(BF16)
    for side, (here, first, second) in enumerate((mine, swapped)):
        at = slice(side * LAG_ROWS, (side + 1) * LAG_ROWS)
        below = jnp.where(odd == 1, first[...].astype(F32), second[...].astype(F32)).astype(BF16)
        above = jnp.where(odd == 1, second[...].astype(F32), first[...].astype(F32)).astype(BF16)
        lags[at, 0:own] = here[...]
        lags[at, own : own + sent] = below
        lags[at, own + sent : own + 2 * sent] = above
    picked = mxu(lags[...], chosen[...]).astype(BF16)
    for rel in range(4):
        for side in range(2):
            outs[rel][side] = picked[side * LAG_ROWS : (side + 1) * LAG_ROWS, rel * 128 : (rel + 1) * 128]


def finish_kernel(pairs, count, *refs):
    pieces, table, out, stage, flat = refs[:4], *refs[4:8]
    member, core, _ = my_place()
    for rel in range(4):
        for side in range(2):
            stage[(core ^ side) * 4 + (member ^ rel)] = pieces[rel][side].astype(F32)
    group = lax.broadcasted_iota(jnp.int32, (LAG_ROWS, 128), 1) >> 4
    for s in range(SLOTS // 2):
        value = jnp.zeros((LAG_ROWS, 128), F32)
        for m in range(8):
            shift = ((m - s) * QG) % 128
            piece = stage[m]
            moved = pltpu.roll(piece, shift, 1) if shift else piece
            value = jnp.where(group == m, moved, value)
        flat[:, s * 128 : (s + 1) * 128] = value
    back = mxu(table[...], flat[...].astype(BF16))
    for s in range(SLOTS // 2):
        lanes = slice(s * 128, (s + 1) * 128)
        slot = core * (SLOTS // 2) + s
        value = jnp.where(pairs[0, slot] > pairs[1, slot], back[:, lanes], flat[:, lanes])
        out[:, s, :] = jnp.where(slot < count[0], value, 0.0)[0:LAGS]


VM = pl.BlockSpec(memory_space=pltpu.VMEM)
SM = pl.BlockSpec(memory_space=pltpu.SMEM)
PARAMS = pltpu.CompilerParams(vmem_limit_bytes=VMEM_LIMIT)


def shape(dims, kind):
    return jax.ShapeDtypeStruct(dims, kind)


def local(traces, channel_ok, time_taps, space_taps, pair_blocks, pair_count):
    n_chan = lax.axis_size("chan")
    n_plane = n_chan // PLANE
    chan_width, half = traces.shape
    segs = 2 * half // SEG
    part = segs // 2
    core = lax.axis_index("tm")
    odd = (lax.axis_index("chan") // PLANE) % 2
    pairs = jnp.transpose(pair_blocks)

    def to_core(x):
        return lax.ppermute(x, "tm", [(0, 1), (1, 0)])

    def in_plane(x, rel):
        return lax.ppermute(x, "chan", [(c, c ^ rel) for c in range(n_chan)])

    def plane_swap(x, start):
        route = []
        for p in range(start, n_plane - 1, 2):
            for k in range(PLANE):
                low, high = p * PLANE + k, (p + 1) * PLANE + k
                route += [(low, high), (high, low)]
        return lax.ppermute(x, "chan", route)

    head, tail = traces[0:2], traces[chan_width - 2 :]
    got = to_core(jnp.where(core == 0, tail, head))
    mine = jnp.where(core == 0, head, tail)
    got, late, taps, space, ok, pairs = lax.optimization_barrier(
        (got, traces, time_taps, space_taps, channel_ok, pairs)
    )
    route = []
    for c in range(n_chan - 1):
        route += [(2 * c + 1, 2 * c + 2), (2 * c + 2, 2 * c + 1)]
    alive = jnp.where(core == 0, channel_ok[0:2], channel_ok[chan_width - 2 :]).astype(F32)[:, None]
    halos = lax.ppermute(jnp.concatenate([mine * alive, got * alive], axis=0), BOTH, route)
    other = to_core(late)
    parts = (taps, space, pairs[0].astype(F32), pairs[1].astype(F32), ok.astype(F32))
    small_size = sum(x.shape[0] for x in parts)
    small, at = jnp.zeros((small_size,), F32), 0
    for x in parts:
        small = small + jnp.pad(x, (at, small_size - at - x.shape[0]))
        at += x.shape[0]
    rows = chan_width // 2
    table = shape((2 * SEG, SEG), BF16)
    split = shape((rows, half), BF16)
    t_high, t_low, pid, space, ok, own_high, own_low = pl.pallas_call(
        prepare_kernel,
        out_shape=[
            table, table, shape((QG, SLOTS * QG), BF16), shape((8, SEG), F32), shape((chan_width, 128), F32),
            split, split,
        ],
        in_specs=[SM, VM],
        out_specs=[VM] * 7,
        compiler_params=PARAMS,
        name="prepare",
    )(small, late)
    block = shape((segs + 1, QG, SEG), BF16)
    short = shape((part, QG, SEG), BF16)
    first, second, *sent = pl.pallas_call(
        filter_kernel,
        out_shape=[short] * 2 + [block] * 3,
        in_specs=[VM] * 10,
        out_specs=[VM] * 5,
        scratch_shapes=[
            pltpu.VMEM((rows + 16, 2 * half + SEG), BF16),
            pltpu.VMEM((rows + 16, 2 * half + SEG), BF16),
            pltpu.VMEM((8, half), F32),
            pltpu.VMEM((segs, rows, SEG), BF16),
        ],
        compiler_params=PARAMS,
        name="filter_whiten",
    )(late, own_high, own_low, other, halos, space, ok, t_high, t_low, pid)
    b1, b2 = in_plane(sent[0], 1), in_plane(sent[1], 2)
    near_0, far_0 = plane_swap(first, 0), plane_swap(second, 1)
    near_0, far_0, last = lax.optimization_barrier((near_0, far_0, sent[2]))
    b3 = in_plane(last, 3)

    def halves(x):
        near = lax.dynamic_slice_in_dim(x, (1 - odd) * part, part, axis=0)
        far = lax.dynamic_slice_in_dim(x, odd * part, part, axis=0)
        return near, far

    (near_1, far_1), (near_2, far_2) = halves(b1), halves(b2)
    near_12 = plane_swap(jnp.stack([near_1, near_2]), 0)
    far_12 = plane_swap(jnp.stack([far_1, far_2]), 1)
    near_3, far_3 = halves(b3)
    near_3, far_3 = plane_swap(near_3, 0), plane_swap(far_3, 1)
    scale = 1.0 / math.sqrt(segs * SEG)
    l_high, l_low = inverse_np(scale)
    sent_shape = shape((LAG_ROWS, N_SENT * QG), BF16)
    lags, lags_first, lags_second = pl.pallas_call(
        pair_kernel,
        out_shape=[shape((LAG_ROWS, N_OWN * QG), BF16), sent_shape, sent_shape],
        in_specs=[VM] * 14,
        out_specs=[VM] * 3,
        scratch_shapes=[
            pltpu.VMEM((PLANE, segs, QG, 2 * SEG), F32),
            pltpu.VMEM((2, PLANE, part, QG, 2 * SEG), F32),
            pltpu.VMEM((N_OWN * QG, 2 * SEG), F32),
        ],
        compiler_params=PARAMS,
        name="pair_lags",
    )(
        first, second, b1, b2, b3, near_0, far_0, near_12, far_12, near_3, far_3,
        jnp.asarray(forward_np()), jnp.asarray(l_high), jnp.asarray(l_low),
    )
    from_first, from_second = plane_swap(lags_first, 0), plane_swap(lags_second, 1)
    known = [lags, from_first, from_second]
    pid_spec = pl.BlockSpec((1, QG, SEG), lambda step: (segs, 0, 0))
    own_spec = pl.BlockSpec((1, QG, SEG), lambda step: (0, 0, 0))
    slots_shape = shape((2, LAG_ROWS, 128), BF16)
    picked = pl.pallas_call(
        select_kernel,
        grid=(1,),
        out_shape=[slots_shape] * 4,
        in_specs=[VM] * 6 + [own_spec] + [pid_spec] * 3,
        out_specs=[VM] * 4,
        scratch_shapes=[
            pltpu.VMEM((N_ALL * QG, 512), BF16),
            pltpu.VMEM((2 * LAG_ROWS, N_ALL * QG), BF16),
        ],
        compiler_params=PARAMS,
        name="select_slots",
    )(*known, *[to_core(x) for x in known], pid[None], b1, b2, b3)
    pieces = [picked[0]] + [in_plane(x, rel + 1) for rel, x in enumerate(picked[1:])]
    out = pl.pallas_call(
        finish_kernel,
        out_shape=shape((LAGS, SLOTS // 2, chan_width), F32),
        in_specs=[SM] * 2 + [VM] * 5,
        out_specs=VM,
        scratch_shapes=[
            pltpu.VMEM((8, LAG_ROWS, 128), F32),
            pltpu.VMEM((LAG_ROWS, SLOTS // 2 * 128), F32),
        ],
        compiler_params=PARAMS,
        name="finish_slots",
    )(pairs, pair_count, *pieces, jnp.asarray(reverse_np()))
    return jnp.transpose(out, (1, 0, 2))


def solution(mesh):
    return jax.shard_map(
        local,
        mesh=mesh,
        in_specs=(P("chan", "tm"), P("chan"), P(), P(), P("chan", None), P("chan")),
        out_specs=P(("chan", "tm"), None, None),
        check_vma=False,
    )
```

```python
import math

import jax
import jax.numpy as jnp
import ml_dtypes
import numpy as np
from jax import lax
from jax.experimental import pallas as pl
from jax.experimental.pallas import tpu as pltpu
from jax.sharding import PartitionSpec as P

SEG = 256
MAXLAG = 100
TAPS = 33
STAPS = 5
SLOTS = 16
NFFT = 510
LAGS = 201
LAG_ROWS = 208
PLANE = 4
QG = 16
BOTH = ("chan", "tm")
F32 = jnp.float32
BF16 = jnp.bfloat16
VMEM_LIMIT = 20 * 1024 * 1024
INNER = [(0, 1), (0, 2), (0, 3), (1, 2), (1, 3), (2, 3)]
CROSS = [(i, j) for i in range(PLANE) for j in range(i + 1)]
N_IN, N_CROSS = len(INNER), len(CROSS)
N_OWN = N_CROSS + N_IN + N_CROSS
N_SENT = N_IN + N_CROSS
N_ALL = N_OWN + 2 * N_SENT


def split_np(table):
    high = table.astype(np.float32).astype(ml_dtypes.bfloat16)
    low = (table - high.astype(np.float64)).astype(np.float32).astype(ml_dtypes.bfloat16)
    return high, low


def forward_np():
    sample = np.arange(SEG)[:, None]
    bins = np.arange(SEG)[None, :]
    angle = (sample * bins % NFFT) * (2.0 * math.pi / NFFT)
    table = np.concatenate([np.cos(angle), -np.sin(angle)], axis=1)
    return table.astype(np.float32).astype(ml_dtypes.bfloat16)


def inverse_np(scale):
    lag = np.arange(LAG_ROWS)[:, None] - MAXLAG
    bins = np.arange(SEG)[None, :]
    angle = (lag * bins % NFFT) * (2.0 * math.pi / NFFT)
    weight = np.where((bins == 0) | (bins == SEG - 1), 1.0, 2.0) / NFFT * scale
    table = np.concatenate([weight * np.cos(angle), -weight * np.sin(angle)], axis=1)
    table[LAGS:] = 0.0
    return split_np(table)


def reverse_np():
    rows = np.arange(LAG_ROWS)
    table = (rows[:, None] + rows[None, :] == LAGS - 1).astype(np.float32)
    return table.astype(ml_dtypes.bfloat16)


def split_terms(value):
    high = value.astype(BF16)
    low = (value - high.astype(F32)).astype(BF16)
    return high, low


def mxu(a, b):
    return jnp.dot(a, b, preferred_element_type=F32)


def my_place():
    chan = lax.axis_index("chan")
    return chan % PLANE, lax.axis_index("tm"), (chan // PLANE) % 2


def pair_ids(first, second, plane):
    low, high = jnp.minimum(first, second), jnp.maximum(first, second)
    low_plane, low_at = low // PLANE - plane, low % PLANE
    high_plane, high_at = high // PLANE - plane, high % PLANE
    inner = jnp.int32(0)
    for k, (i, j) in enumerate(INNER):
        inner = jnp.where((low_at == i) & (high_at == j), k, inner)
    cross = low_at * (low_at + 1) // 2 + high_at
    one = jnp.where(
        low_plane == 0,
        jnp.where(high_plane == 0, N_CROSS + inner, N_CROSS + N_IN + cross),
        jnp.where(
            low_plane > 0,
            N_OWN + N_SENT + N_CROSS + inner,
            jnp.where(high_plane == 0, cross, N_OWN + inner),
        ),
    )
    two = jnp.where(
        low_plane == high_plane,
        N_ALL,
        jnp.where(low_plane == 0, N_OWN + N_SENT + cross, N_OWN + N_IN + cross),
    )
    return one, two


def tile_rows(own, core):
    rows = own.shape[0] // 2
    first_row = pl.multiple_of(core * rows, rows)
    near_row = pl.multiple_of(rows - 8 + 8 * (1 - core), 8)
    return pl.ds(first_row, rows), pl.ds(near_row, 8)


def prepare_kernel(
    small, whole, whole_rows, traces, t_high, t_low, pid, space, ok, own_high, own_low, own_near,
    main_rows, near_rows, sems,
):
    _, core, _ = my_place()
    plane = lax.axis_index("chan") // PLANE
    main, near = tile_rows(traces, core)
    copies = [
        pltpu.make_async_copy(traces.at[main], main_rows, sems.at[0]),
        pltpu.make_async_copy(traces.at[near], near_rows, sems.at[1]),
    ]
    for copy in copies:
        copy.start()
    t_high[...] = jnp.zeros(t_high.shape, BF16)
    t_low[...] = jnp.zeros(t_low.shape, BF16)
    shift = SEG // 2 - (TAPS - 1) // 2
    height = 128 + TAPS - 1
    tap = lax.broadcasted_iota(jnp.int32, (height, 128), 0) - lax.broadcasted_iota(
        jnp.int32, (height, 128), 1
    )
    band = jnp.zeros((height, 128), F32)
    for j in range(TAPS):
        band = jnp.where(tap == j, small[0, j], band)
    high, low = split_terms(band)
    for lanes in range(SEG // 128):
        at = (slice(lanes * 128 + shift, lanes * 128 + shift + height), slice(lanes * 128, lanes * 128 + 128))
        t_high[at] = high
        t_low[at] = low
    row = lax.broadcasted_iota(jnp.int32, space.shape, 0)
    value = jnp.zeros(space.shape, F32)
    for j in range(STAPS):
        value = jnp.where(row == j, small[1, j], value)
    space[...] = value
    slot = lax.broadcasted_iota(jnp.int32, pid.shape, 1) >> 4
    upper = lax.broadcasted_iota(jnp.int32, pid.shape, 0) < 8
    ids = jnp.zeros(pid.shape, jnp.int32)
    for s in range(SLOTS):
        one, two = pair_ids(whole[0, s], whole[1, s], plane)
        ids = jnp.where(slot == s, jnp.where(upper, one, two), ids)
    pid[...] = ids.astype(F32).astype(BF16)
    width = ok.shape[0]
    diagonal = lax.broadcasted_iota(jnp.int32, (width, width), 0) == lax.broadcasted_iota(
        jnp.int32, (width, width), 1
    )
    spread = jnp.where(diagonal, whole_rows[2:3, :width].astype(F32), 0.0)
    ok[...] = jnp.broadcast_to(jnp.sum(spread, axis=1, keepdims=True), ok.shape)
    for copy in copies:
        copy.wait()
    own_high[...], own_low[...] = split_terms(main_rows[...] * ok[main, 0:1])
    own_near[...] = near_rows[...] * ok[near, 0:1]


def filter_kernel(
    own_near, own_high, own_low, other, halos, space, ok, t_high, t_low, pid,
    out_first, out_second, out_1, out_2, out_3, x_high, x_low, edge, white,
):
    member, core, odd = my_place()
    rows, half = own_high.shape
    main, near = tile_rows(other, core)
    pad = SEG // 2
    total = 2 * half
    zeros = jnp.zeros((rows + 16, pad), BF16)
    for buf in (x_high, x_low):
        buf[:, 0:pad] = zeros
        buf[:, pad + total : 2 * pad + total] = zeros
    own_lanes = pl.ds(pl.multiple_of(pad + core * half, pad), half)
    other_lanes = pl.ds(pl.multiple_of(pad + (1 - core) * half, pad), half)
    x_high[0:rows, own_lanes] = own_high[...]
    x_low[0:rows, own_lanes] = own_low[...]
    x_high[0:rows, other_lanes], x_low[0:rows, other_lanes] = split_terms(other[main, :] * ok[main, 0:1])
    other_near = other[near, :] * ok[near, 0:1]
    for inside, halo, lanes in ((own_near[...], halos[2:4], own_lanes), (other_near, halos[0:2], other_lanes)):
        for k in range(4):
            edge[2 * k : 2 * k + 2, :] = halo
        outside = edge[...]
        above = jnp.where(core == 0, outside, inside)
        below = jnp.where(core == 0, inside, outside)
        high, low = split_terms(jnp.concatenate([above, below], axis=0))
        x_high[rows : rows + 16, lanes] = high
        x_low[rows : rows + 16, lanes] = low
    segs = total // SEG
    chunk = 8
    height = rows + 16
    taps = [space[j : j + 1, :] for j in range(STAPS)]

    def body(step, carry):
        seg0 = step * chunk
        spans = [pl.ds(pl.multiple_of((seg0 + s) * SEG, SEG), 2 * SEG) for s in range(chunk)]
        high = jnp.concatenate([x_high[:, span] for span in spans], axis=0)
        low = jnp.concatenate([x_low[:, span] for span in spans], axis=0)
        y = mxu(high, t_high[...]) + mxu(low, t_high[...]) + mxu(high, t_low[...])
        for s in range(chunk):
            block = y[s * height : (s + 1) * height]
            ext = jnp.concatenate(
                [block[rows : rows + 8], block[0:rows], block[rows + 8 : rows + 16]], axis=0
            )
            filtered = taps[0] * ext[6 : 6 + rows]
            for j in range(1, STAPS):
                filtered = filtered + taps[j] * ext[6 + j : 6 + j + rows]
            power = jnp.mean(filtered * filtered, axis=1, keepdims=True)
            white[seg0 + s] = (filtered * (1.0 / jnp.sqrt(power + 1e-5))).astype(BF16)
        return carry

    lax.fori_loop(0, segs // chunk, body, 0, unroll=True)
    own_row = pl.multiple_of(member * QG, QG)
    part = segs // 2
    out_first[...] = white[pl.ds((1 - odd) * part, part), pl.ds(own_row, QG), :]
    out_second[...] = white[pl.ds(odd * part, part), pl.ds(own_row, QG), :]
    for rel, out in ((1, out_1), (2, out_2), (3, out_3)):
        row = pl.multiple_of((member ^ rel) * QG, QG)
        out[0:segs] = white[:, pl.ds(row, QG), :]
        out[segs] = pid[...]


def transform(block, table):
    value = mxu(block.reshape(block.shape[0] * QG, SEG), table[...])
    return value.astype(BF16).astype(F32).reshape(block.shape[0], QG, 2 * SEG)


def bin_parts():
    for q8 in range(QG // 8):
        for lanes in range(SEG // 128):
            rows = slice(q8 * 8, q8 * 8 + 8)
            re_lanes = slice(lanes * 128, lanes * 128 + 128)
            im_lanes = slice(SEG + lanes * 128, SEG + lanes * 128 + 128)
            yield q8 * 8, rows, re_lanes, im_lanes


def add_product(sums, index, left, right):
    re = sums[2 * index] + (left[0] * right[0] + left[1] * right[1])
    im = sums[2 * index + 1] + (left[1] * right[0] - left[0] * right[1])
    return [re, im]


def store_sums(cross, first_pair, row, re_lanes, im_lanes, sums):
    for index in range(len(sums) // 2):
        at = slice((first_pair + index) * QG + row, (first_pair + index) * QG + row + 8)
        cross[at, re_lanes] = sums[2 * index]
        cross[at, im_lanes] = sums[2 * index + 1]


def inner_kernel(first, second, b1, b2, b3, near_0, far_0, table, spec, spec_near, spec_far, inner):
    member, _, odd = my_place()
    segs = spec.shape[1]
    part = segs // 2
    spec[member, pl.ds((1 - odd) * part, part)] = transform(first[...], table)
    spec[member, pl.ds(odd * part, part)] = transform(second[...], table)
    for rel, ref in ((1, b1), (2, b2), (3, b3)):
        spec[member ^ rel] = transform(ref[0:segs], table)
    spec_near[...] = transform(near_0[...], table)
    spec_far[...] = transform(far_0[...], table)
    for row, rows, re_lanes, im_lanes in bin_parts():

        def body(seg, sums):
            mine = [(spec[w, seg, rows, re_lanes], spec[w, seg, rows, im_lanes]) for w in range(PLANE)]
            result = []
            for k, (i, j) in enumerate(INNER):
                result += add_product(sums, k, mine[i], mine[j])
            return tuple(result)

        zero = jnp.zeros((8, 128), F32)
        sums = lax.fori_loop(0, segs, body, (zero,) * (2 * N_IN), unroll=4)
        store_sums(inner, 0, row, re_lanes, im_lanes, sums)


def cross_kernel(spec, spec_near, spec_far, inner, near_12, far_12, table, cross, spec_z):
    member, _, odd = my_place()
    part = spec_near.shape[0]
    for side, done, pair in ((odd, spec_near, near_12), (1 - odd, spec_far, far_12)):
        spec_z[side, member] = done[...]
        spec_z[side, member ^ 1] = transform(pair[0], table)
        spec_z[side, member ^ 2] = transform(pair[1], table)
        spec_z[side, member ^ 3] = jnp.zeros(done.shape, F32)
    cross[N_CROSS * QG : (N_CROSS + N_IN) * QG, :] = inner[...]
    for row, rows, re_lanes, im_lanes in bin_parts():
        for side, first_pair in ((0, N_CROSS + N_IN), (1, 0)):

            def body(seg, sums):
                at = seg + side * part
                mine = [(spec[w, at, rows, re_lanes], spec[w, at, rows, im_lanes]) for w in range(PLANE)]
                theirs = [
                    (spec_z[side, w, seg, rows, re_lanes], spec_z[side, w, seg, rows, im_lanes])
                    for w in range(PLANE)
                ]
                low, high = (theirs, mine) if side else (mine, theirs)
                result = []
                for k, (i, j) in enumerate(CROSS):
                    result += add_product(sums, k, low[i], high[j])
                return tuple(result)

            zero = jnp.zeros((8, 128), F32)
            sums = lax.fori_loop(0, part, body, (zero,) * (2 * N_CROSS), unroll=4)
            store_sums(cross, first_pair, row, re_lanes, im_lanes, sums)


def lags_kernel(
    spec, cross_in, near_3, far_3, table, l_high, l_low, out, out_first, out_second, last, cross
):
    member, _, odd = my_place()
    part = near_3.shape[0]
    diagonal = member ^ 3
    last[odd] = transform(near_3[...], table)
    last[1 - odd] = transform(far_3[...], table)
    cross[...] = cross_in[...]
    for row, rows, re_lanes, im_lanes in bin_parts():
        for side in range(2):

            def body(seg, sums):
                at = seg + side * part
                theirs = (last[side, seg, rows, re_lanes], last[side, seg, rows, im_lanes])
                result = []
                for w in range(PLANE):
                    mine = (spec[w, at, rows, re_lanes], spec[w, at, rows, im_lanes])
                    low, high = (theirs, mine) if side else (mine, theirs)
                    result += add_product(sums, w, low, high)
                return tuple(result)

            zero = jnp.zeros((8, 128), F32)
            sums = lax.fori_loop(0, part, body, (zero,) * (2 * PLANE), unroll=4)
            for w in range(PLANE):
                if side:
                    valid, pair = w <= diagonal, diagonal * (diagonal + 1) // 2 + w
                else:
                    valid, pair = w >= diagonal, N_CROSS + N_IN + w * (w + 1) // 2 + diagonal
                at = pl.ds(pl.multiple_of(jnp.where(valid, pair, 0) * QG + row, 8), 8)
                cross[at, re_lanes] += jnp.where(valid, sums[2 * w], 0.0)
                cross[at, im_lanes] += jnp.where(valid, sums[2 * w + 1], 0.0)
    high, low = split_terms(cross[...])

    def turned(left, right):
        return lax.dot_general(left, right, (((1,), (1,)), ((), ())), preferred_element_type=F32)

    lagged = turned(l_high[...], high) + turned(l_high[...], low) + turned(l_low[...], high)
    out[...] = lagged.astype(BF16)
    to_above = lagged[:, N_CROSS * QG :]
    to_below = lagged[:, : N_SENT * QG]
    out_first[...] = jnp.where(odd == 1, to_below, to_above).astype(BF16)
    out_second[...] = jnp.where(odd == 1, to_above, to_below).astype(BF16)


def choose_kernel(*refs):
    pids, chosen = refs[:4], refs[4]
    _, core, _ = my_place()
    row_id = lax.broadcasted_iota(jnp.int32, (N_ALL * QG, 128), 0)
    col_id = lax.broadcasted_iota(jnp.int32, (N_ALL * QG, 128), 1)
    row_key = jnp.where((row_id & 15) == (col_id & 15), (row_id >> 4).astype(F32), -1.0)
    lane = pl.multiple_of(core * 128, 128)
    for rel, pid in enumerate(pids):
        ids = pid[0, :, pl.ds(lane, 128)].astype(F32)
        match = (row_key == ids[0:1, :]) | (row_key == ids[8:9, :])
        chosen[:, rel * 128 : (rel + 1) * 128] = jnp.where(match, 1.0, 0.0).astype(BF16)


def select_kernel(chosen, *refs):
    mine, swapped, outs, lags = refs[0:3], refs[3:6], refs[6:10], refs[10]
    _, _, odd = my_place()
    own, sent = N_OWN * QG, N_SENT * QG
    for side, (here, first, second) in enumerate((mine, swapped)):
        at = slice(side * LAG_ROWS, (side + 1) * LAG_ROWS)
        below = jnp.where(odd == 1, first[...].astype(F32), second[...].astype(F32)).astype(BF16)
        above = jnp.where(odd == 1, second[...].astype(F32), first[...].astype(F32)).astype(BF16)
        lags[at, 0:own] = here[...]
        lags[at, own : own + sent] = below
        lags[at, own + sent : own + 2 * sent] = above
    picked = mxu(lags[...], chosen[...]).astype(BF16)
    for rel in range(4):
        for side in range(2):
            outs[rel][side] = picked[side * LAG_ROWS : (side + 1) * LAG_ROWS, rel * 128 : (rel + 1) * 128]


def finish_kernel(pairs, count, *refs):
    pieces, table, out, stage, flat = refs[:4], *refs[4:8]
    member, core, _ = my_place()
    for rel in range(4):
        for side in range(2):
            stage[(core ^ side) * 4 + (member ^ rel)] = pieces[rel][side].astype(F32)
    step = 16
    group = lax.broadcasted_iota(jnp.int32, (step, 128), 1) >> 4
    for row in range(0, LAG_ROWS, step):
        tiles = [stage[m, row : row + step] for m in range(8)]
        for bit in (4, 2, 1):
            upper = (group & bit) > 0
            for m in range(8):
                if not m & bit:
                    low, high = tiles[m], tiles[m | bit]
                    tiles[m] = jnp.where(upper, pltpu.roll(high, bit * QG, 1), low)
                    tiles[m | bit] = jnp.where(upper, high, pltpu.roll(low, 128 - bit * QG, 1))
        for s in range(8):
            flat[row : row + step, s * 128 : (s + 1) * 128] = tiles[s]
    back = mxu(table[...], flat[...].astype(BF16))
    for s in range(SLOTS // 2):
        lanes = slice(s * 128, (s + 1) * 128)
        slot = core * (SLOTS // 2) + s
        value = jnp.where(pairs[0, slot] > pairs[1, slot], back[:, lanes], flat[:, lanes])
        out[:, s, :] = jnp.where(slot < count[0], value, 0.0)[0:LAGS]


VM = pl.BlockSpec(memory_space=pltpu.VMEM)
SM = pl.BlockSpec(memory_space=pltpu.SMEM)
HB = pl.BlockSpec(memory_space=pltpu.HBM)
PARAMS = pltpu.CompilerParams(vmem_limit_bytes=VMEM_LIMIT)


def shape(dims, kind):
    return jax.ShapeDtypeStruct(dims, kind)


def local(traces, channel_ok, time_taps, space_taps, pair_blocks, pair_count):
    n_chan = lax.axis_size("chan")
    n_plane = n_chan // PLANE
    chan_width, half = traces.shape
    segs = 2 * half // SEG
    part = segs // 2
    core = lax.axis_index("tm")
    odd = (lax.axis_index("chan") // PLANE) % 2
    pairs = jnp.transpose(pair_blocks)

    def to_core(x):
        return lax.ppermute(x, "tm", [(0, 1), (1, 0)])

    def in_plane(x, rel):
        return lax.ppermute(x, "chan", [(c, c ^ rel) for c in range(n_chan)])

    def plane_swap(x, start):
        route = []
        for p in range(start, n_plane - 1, 2):
            for k in range(PLANE):
                low, high = p * PLANE + k, (p + 1) * PLANE + k
                route += [(low, high), (high, low)]
        return lax.ppermute(x, "chan", route)

    rows = chan_width // 2
    head, tail = traces[0:2], traces[chan_width - 2 :]
    got = to_core(jnp.where(core == 0, tail, head))
    mine = jnp.where(core == 0, head, tail)
    got, late = lax.optimization_barrier((got, traces))
    route = []
    for c in range(n_chan - 1):
        route += [(2 * c + 1, 2 * c + 2), (2 * c + 2, 2 * c + 1)]
    alive = (jnp.where(core == 0, channel_ok[0:2], channel_ok[chan_width - 2 :]) > 0)[:, None]
    edges = [jnp.where(alive, mine, 0.0), jnp.where(alive, got, 0.0)]
    halos = lax.ppermute(jnp.concatenate(edges, axis=0), BOTH, route)
    other = to_core(late)
    small = jnp.pad(time_taps[None, :], ((0, 7), (0, 128 - TAPS)))
    small = small + jnp.pad(space_taps[None, :], ((1, 6), (0, 128 - STAPS)))
    whole = jnp.pad(pairs, ((0, 6), (0, 128 - SLOTS)))
    whole = whole + jnp.pad(channel_ok[None, :], ((2, 5), (0, 128 - chan_width)))
    table = shape((2 * SEG, SEG), BF16)
    split = shape((rows, half), BF16)
    t_high, t_low, pid, space, ok, own_high, own_low, own_near = pl.pallas_call(
        prepare_kernel,
        out_shape=[
            table, table, shape((QG, SLOTS * QG), BF16), shape((8, SEG), F32), shape((chan_width, 128), F32),
            split, split, shape((8, half), F32),
        ],
        in_specs=[SM, SM, VM, HB],
        out_specs=[VM] * 8,
        scratch_shapes=[
            pltpu.VMEM((rows, half), F32),
            pltpu.VMEM((8, half), F32),
            pltpu.SemaphoreType.DMA((2,)),
        ],
        compiler_params=PARAMS,
        name="prepare",
    )(small, whole, whole, late)
    block = shape((segs + 1, QG, SEG), BF16)
    short = shape((part, QG, SEG), BF16)
    first, second, *sent = pl.pallas_call(
        filter_kernel,
        out_shape=[short] * 2 + [block] * 3,
        in_specs=[VM] * 10,
        out_specs=[VM] * 5,
        scratch_shapes=[
            pltpu.VMEM((rows + 16, 2 * half + SEG), BF16),
            pltpu.VMEM((rows + 16, 2 * half + SEG), BF16),
            pltpu.VMEM((8, half), F32),
            pltpu.VMEM((segs, rows, SEG), BF16),
        ],
        compiler_params=PARAMS,
        name="filter_whiten",
    )(own_near, own_high, own_low, other, halos, space, ok, t_high, t_low, pid)
    b1, b2 = in_plane(sent[0], 1), in_plane(sent[1], 2)
    far_0, near_0 = plane_swap(second, 1), plane_swap(first, 0)
    b1, last = lax.optimization_barrier((b1, sent[2]))
    b3 = in_plane(last, 3)
    b1, b2, near_0, far_0 = lax.optimization_barrier((b1, b2, near_0, far_0))
    def halves(x):
        near = lax.dynamic_slice_in_dim(x, (1 - odd) * part, part, axis=0)
        far = lax.dynamic_slice_in_dim(x, odd * part, part, axis=0)
        return near, far

    (near_1, far_1), (near_2, far_2) = halves(b1), halves(b2)
    far_12 = plane_swap(jnp.stack([far_1, far_2]), 1)
    near_12 = plane_swap(jnp.stack([near_1, near_2]), 0)
    near_3, far_3 = halves(b3)
    far_3, near_3 = plane_swap(far_3, 1), plane_swap(near_3, 0)
    scale = 1.0 / math.sqrt(segs * SEG)
    l_high, l_low = inverse_np(scale)
    sent_shape = shape((LAG_ROWS, N_SENT * QG), BF16)
    table = jnp.asarray(forward_np())
    short = shape((part, QG, 2 * SEG), F32)
    spec, spec_near, spec_far, inner = pl.pallas_call(
        inner_kernel,
        out_shape=[shape((PLANE, segs, QG, 2 * SEG), F32), short, short, shape((N_IN * QG, 2 * SEG), F32)],
        in_specs=[VM] * 8,
        out_specs=[VM] * 4,
        compiler_params=PARAMS,
        name="inner_pairs",
    )(first, second, b1, b2, b3, near_0, far_0, table)
    cross = pl.pallas_call(
        cross_kernel,
        out_shape=shape((N_OWN * QG, 2 * SEG), F32),
        in_specs=[VM] * 7,
        out_specs=VM,
        scratch_shapes=[pltpu.VMEM((2, PLANE, part, QG, 2 * SEG), F32)],
        compiler_params=PARAMS,
        name="cross_pairs",
    )(spec, spec_near, spec_far, inner, near_12, far_12, table)
    lags, lags_first, lags_second = pl.pallas_call(
        lags_kernel,
        out_shape=[shape((LAG_ROWS, N_OWN * QG), BF16), sent_shape, sent_shape],
        in_specs=[VM] * 7,
        out_specs=[VM] * 3,
        scratch_shapes=[
            pltpu.VMEM((2, part, QG, 2 * SEG), F32),
            pltpu.VMEM((N_OWN * QG, 2 * SEG), F32),
        ],
        compiler_params=PARAMS,
        name="pair_lags",
    )(spec, cross, near_3, far_3, table, jnp.asarray(l_high), jnp.asarray(l_low))
    from_first, from_second = plane_swap(lags_first, 0), plane_swap(lags_second, 1)
    known = [lags, from_first, from_second]
    pid_spec = pl.BlockSpec((1, QG, SEG), lambda step: (segs, 0, 0))
    own_spec = pl.BlockSpec((1, QG, SEG), lambda step: (0, 0, 0))
    slots_shape = shape((2, LAG_ROWS, 128), BF16)
    chosen = pl.pallas_call(
        choose_kernel,
        grid=(1,),
        out_shape=shape((N_ALL * QG, 512), BF16),
        in_specs=[own_spec] + [pid_spec] * 3,
        out_specs=VM,
        compiler_params=PARAMS,
        name="choose",
    )(pid[None], b1, b2, b3)
    picked = pl.pallas_call(
        select_kernel,
        out_shape=[slots_shape] * 4,
        in_specs=[VM] * 7,
        out_specs=[VM] * 4,
        scratch_shapes=[pltpu.VMEM((2 * LAG_ROWS, N_ALL * QG), BF16)],
        compiler_params=PARAMS,
        name="select_slots",
    )(chosen, *known, *[to_core(x) for x in known])
    pieces = [picked[0]] + [in_plane(x, rel + 1) for rel, x in enumerate(picked[1:])]
    out = pl.pallas_call(
        finish_kernel,
        out_shape=shape((LAGS, SLOTS // 2, chan_width), F32),
        in_specs=[SM] * 2 + [VM] * 5,
        out_specs=VM,
        scratch_shapes=[
            pltpu.VMEM((8, LAG_ROWS, 128), F32),
            pltpu.VMEM((LAG_ROWS, SLOTS // 2 * 128), F32),
        ],
        compiler_params=PARAMS,
        name="finish_slots",
    )(pairs, pair_count, *pieces, jnp.asarray(reverse_np()))
    return jnp.transpose(out, (1, 0, 2))


def solution(mesh):
    return jax.shard_map(
        local,
        mesh=mesh,
        in_specs=(P("chan", "tm"), P("chan"), P(), P(), P("chan", None), P("chan")),
        out_specs=P(("chan", "tm"), None, None),
        check_vma=False,
    )
```

```python
import math

import jax
import jax.numpy as jnp
import ml_dtypes
import numpy as np
from jax import lax
from jax.experimental import pallas as pl
from jax.experimental.pallas import tpu as pltpu
from jax.sharding import PartitionSpec as P

SEG = 256
MAXLAG = 100
TAPS = 33
STAPS = 5
SLOTS = 16
NFFT = 510
LAGS = 201
LAG_ROWS = 208
PLANE = 4
QG = 16
BOTH = ("chan", "tm")
F32 = jnp.float32
BF16 = jnp.bfloat16
VMEM_LIMIT = 20 * 1024 * 1024
INNER = [(0, 1), (0, 2), (0, 3), (1, 2), (1, 3), (2, 3)]
CROSS = [(i, j) for i in range(PLANE) for j in range(i + 1)]
N_IN, N_CROSS = len(INNER), len(CROSS)
N_OWN = N_CROSS + N_IN + N_CROSS
N_SENT = N_IN + N_CROSS
N_ALL = N_OWN + 2 * N_SENT


def split_np(table):
    high = table.astype(np.float32).astype(ml_dtypes.bfloat16)
    low = (table - high.astype(np.float64)).astype(np.float32).astype(ml_dtypes.bfloat16)
    return high, low


def forward_np():
    sample = np.arange(SEG)[:, None]
    bins = np.arange(SEG)[None, :]
    angle = (sample * bins % NFFT) * (2.0 * math.pi / NFFT)
    table = np.concatenate([np.cos(angle), -np.sin(angle)], axis=1)
    return table.astype(np.float32).astype(ml_dtypes.bfloat16)


def inverse_np(scale):
    lag = np.arange(LAG_ROWS)[:, None] - MAXLAG
    bins = np.arange(SEG)[None, :]
    angle = (lag * bins % NFFT) * (2.0 * math.pi / NFFT)
    weight = np.where((bins == 0) | (bins == SEG - 1), 1.0, 2.0) / NFFT * scale
    table = np.concatenate([weight * np.cos(angle), -weight * np.sin(angle)], axis=1)
    table[LAGS:] = 0.0
    return split_np(table)


def reverse_np():
    rows = np.arange(LAG_ROWS)
    table = (rows[:, None] + rows[None, :] == LAGS - 1).astype(np.float32)
    return table.astype(ml_dtypes.bfloat16)


def split_terms(value):
    high = value.astype(BF16)
    low = (value - high.astype(F32)).astype(BF16)
    return high, low


def mxu(a, b):
    return jnp.dot(a, b, preferred_element_type=F32)


def my_place():
    chan = lax.axis_index("chan")
    return chan % PLANE, lax.axis_index("tm"), (chan // PLANE) % 2


def pair_ids(first, second, plane):
    low, high = jnp.minimum(first, second), jnp.maximum(first, second)
    low_plane, low_at = low // PLANE - plane, low % PLANE
    high_plane, high_at = high // PLANE - plane, high % PLANE
    inner = jnp.int32(0)
    for k, (i, j) in enumerate(INNER):
        inner = jnp.where((low_at == i) & (high_at == j), k, inner)
    cross = low_at * (low_at + 1) // 2 + high_at
    one = jnp.where(
        low_plane == 0,
        jnp.where(high_plane == 0, N_CROSS + inner, N_CROSS + N_IN + cross),
        jnp.where(
            low_plane > 0,
            N_OWN + N_SENT + N_CROSS + inner,
            jnp.where(high_plane == 0, cross, N_OWN + inner),
        ),
    )
    two = jnp.where(
        low_plane == high_plane,
        N_ALL,
        jnp.where(low_plane == 0, N_OWN + N_SENT + cross, N_OWN + N_IN + cross),
    )
    return one, two


def tile_rows(own, core):
    rows = own.shape[0] // 2
    first_row = pl.multiple_of(core * rows, rows)
    near_row = pl.multiple_of(rows - 8 + 8 * (1 - core), 8)
    return pl.ds(first_row, rows), pl.ds(near_row, 8)


def prepare_kernel(
    small, whole, whole_rows, traces, t_high, t_low, pid, space, ok, own_high, own_low, own_near,
):
    _, core, _ = my_place()
    plane = lax.axis_index("chan") // PLANE
    main, near = tile_rows(traces, core)
    t_high[...] = jnp.zeros(t_high.shape, BF16)
    t_low[...] = jnp.zeros(t_low.shape, BF16)
    shift = SEG // 2 - (TAPS - 1) // 2
    height = 128 + TAPS - 1
    tap = lax.broadcasted_iota(jnp.int32, (height, 128), 0) - lax.broadcasted_iota(
        jnp.int32, (height, 128), 1
    )
    band = jnp.zeros((height, 128), F32)
    for j in range(TAPS):
        band = jnp.where(tap == j, small[0, j], band)
    high, low = split_terms(band)
    for lanes in range(SEG // 128):
        at = (slice(lanes * 128 + shift, lanes * 128 + shift + height), slice(lanes * 128, lanes * 128 + 128))
        t_high[at] = high
        t_low[at] = low
    row = lax.broadcasted_iota(jnp.int32, space.shape, 0)
    value = jnp.zeros(space.shape, F32)
    for j in range(STAPS):
        value = jnp.where(row == j, small[1, j], value)
    space[...] = value
    slot = lax.broadcasted_iota(jnp.int32, pid.shape, 1) >> 4
    upper = lax.broadcasted_iota(jnp.int32, pid.shape, 0) < 8
    ids = jnp.zeros(pid.shape, jnp.int32)
    for s in range(SLOTS):
        one, two = pair_ids(whole[0, s], whole[1, s], plane)
        ids = jnp.where(slot == s, jnp.where(upper, one, two), ids)
    pid[...] = ids.astype(F32).astype(BF16)
    width = ok.shape[0]
    diagonal = lax.broadcasted_iota(jnp.int32, (width, width), 0) == lax.broadcasted_iota(
        jnp.int32, (width, width), 1
    )
    spread = jnp.where(diagonal, whole_rows[2:3, :width].astype(F32), 0.0)
    ok[...] = jnp.broadcast_to(jnp.sum(spread, axis=1, keepdims=True), ok.shape)
    own_high[...], own_low[...] = split_terms(traces[main, :] * ok[main, 0:1])
    own_near[...] = traces[near, :] * ok[near, 0:1]


def filter_kernel(
    own_near, own_high, own_low, other, halos, space, ok, t_high, t_low, pid,
    out_first, out_second, out_1, out_2, out_3, x_high, x_low, edge, white,
):
    member, core, odd = my_place()
    rows, half = own_high.shape
    main, near = tile_rows(other, core)
    pad = SEG // 2
    total = 2 * half
    zeros = jnp.zeros((rows + 16, pad), BF16)
    for buf in (x_high, x_low):
        buf[:, 0:pad] = zeros
        buf[:, pad + total : 2 * pad + total] = zeros
    own_lanes = pl.ds(pl.multiple_of(pad + core * half, pad), half)
    other_lanes = pl.ds(pl.multiple_of(pad + (1 - core) * half, pad), half)
    x_high[0:rows, own_lanes] = own_high[...]
    x_low[0:rows, own_lanes] = own_low[...]
    x_high[0:rows, other_lanes], x_low[0:rows, other_lanes] = split_terms(other[main, :] * ok[main, 0:1])
    other_near = other[near, :] * ok[near, 0:1]
    for inside, halo, lanes in ((own_near[...], halos[2:4], own_lanes), (other_near, halos[0:2], other_lanes)):
        for k in range(4):
            edge[2 * k : 2 * k + 2, :] = halo
        outside = edge[...]
        above = jnp.where(core == 0, outside, inside)
        below = jnp.where(core == 0, inside, outside)
        high, low = split_terms(jnp.concatenate([above, below], axis=0))
        x_high[rows : rows + 16, lanes] = high
        x_low[rows : rows + 16, lanes] = low
    segs = total // SEG
    chunk = 8
    height = rows + 16
    taps = [space[j : j + 1, :] for j in range(STAPS)]

    def body(step, carry):
        seg0 = step * chunk
        spans = [pl.ds(pl.multiple_of((seg0 + s) * SEG, SEG), 2 * SEG) for s in range(chunk)]
        high = jnp.concatenate([x_high[:, span] for span in spans], axis=0)
        low = jnp.concatenate([x_low[:, span] for span in spans], axis=0)
        y = mxu(high, t_high[...]) + mxu(low, t_high[...]) + mxu(high, t_low[...])
        for s in range(chunk):
            block = y[s * height : (s + 1) * height]
            ext = jnp.concatenate(
                [block[rows : rows + 8], block[0:rows], block[rows + 8 : rows + 16]], axis=0
            )
            filtered = taps[0] * ext[6 : 6 + rows]
            for j in range(1, STAPS):
                filtered = filtered + taps[j] * ext[6 + j : 6 + j + rows]
            power = jnp.mean(filtered * filtered, axis=1, keepdims=True)
            white[seg0 + s] = (filtered * (1.0 / jnp.sqrt(power + 1e-5))).astype(BF16)
        return carry

    lax.fori_loop(0, segs // chunk, body, 0, unroll=True)
    own_row = pl.multiple_of(member * QG, QG)
    part = segs // 2
    out_first[...] = white[pl.ds((1 - odd) * part, part), pl.ds(own_row, QG), :]
    out_second[...] = white[pl.ds(odd * part, part), pl.ds(own_row, QG), :]
    for rel, out in ((1, out_1), (2, out_2), (3, out_3)):
        row = pl.multiple_of((member ^ rel) * QG, QG)
        out[0:segs] = white[:, pl.ds(row, QG), :]
        out[segs] = pid[...]


def transform(block, table):
    value = mxu(block.reshape(block.shape[0] * QG, SEG), table[...])
    return value.astype(BF16).astype(F32).reshape(block.shape[0], QG, 2 * SEG)


def bin_parts():
    for q8 in range(QG // 8):
        for lanes in range(SEG // 128):
            rows = slice(q8 * 8, q8 * 8 + 8)
            re_lanes = slice(lanes * 128, lanes * 128 + 128)
            im_lanes = slice(SEG + lanes * 128, SEG + lanes * 128 + 128)
            yield q8 * 8, rows, re_lanes, im_lanes


def add_product(sums, index, left, right):
    re = sums[2 * index] + (left[0] * right[0] + left[1] * right[1])
    im = sums[2 * index + 1] + (left[1] * right[0] - left[0] * right[1])
    return [re, im]


def store_sums(cross, first_pair, row, re_lanes, im_lanes, sums):
    for index in range(len(sums) // 2):
        at = slice((first_pair + index) * QG + row, (first_pair + index) * QG + row + 8)
        cross[at, re_lanes] = sums[2 * index]
        cross[at, im_lanes] = sums[2 * index + 1]


def inner_kernel(first, second, b1, b2, b3, near_0, far_0, table, spec, spec_near, spec_far, inner):
    member, _, odd = my_place()
    segs = spec.shape[1]
    part = segs // 2
    spec[member, pl.ds((1 - odd) * part, part)] = transform(first[...], table)
    spec[member, pl.ds(odd * part, part)] = transform(second[...], table)
    for rel, ref in ((1, b1), (2, b2), (3, b3)):
        spec[member ^ rel] = transform(ref[0:segs], table)
    spec_near[...] = transform(near_0[...], table)
    spec_far[...] = transform(far_0[...], table)
    for row, rows, re_lanes, im_lanes in bin_parts():

        def body(seg, sums):
            mine = [(spec[w, seg, rows, re_lanes], spec[w, seg, rows, im_lanes]) for w in range(PLANE)]
            result = []
            for k, (i, j) in enumerate(INNER):
                result += add_product(sums, k, mine[i], mine[j])
            return tuple(result)

        zero = jnp.zeros((8, 128), F32)
        sums = lax.fori_loop(0, segs, body, (zero,) * (2 * N_IN), unroll=4)
        store_sums(inner, 0, row, re_lanes, im_lanes, sums)


def cross_kernel(spec, spec_near, spec_far, inner, near_12, far_12, table, cross, spec_z):
    member, _, odd = my_place()
    part = spec_near.shape[0]
    for side, done, pair in ((odd, spec_near, near_12), (1 - odd, spec_far, far_12)):
        spec_z[side, member] = done[...]
        spec_z[side, member ^ 1] = transform(pair[0], table)
        spec_z[side, member ^ 2] = transform(pair[1], table)
        spec_z[side, member ^ 3] = jnp.zeros(done.shape, F32)
    cross[N_CROSS * QG : (N_CROSS + N_IN) * QG, :] = inner[...]
    for row, rows, re_lanes, im_lanes in bin_parts():
        for side, first_pair in ((0, N_CROSS + N_IN), (1, 0)):

            def body(seg, sums):
                at = seg + side * part
                mine = [(spec[w, at, rows, re_lanes], spec[w, at, rows, im_lanes]) for w in range(PLANE)]
                theirs = [
                    (spec_z[side, w, seg, rows, re_lanes], spec_z[side, w, seg, rows, im_lanes])
                    for w in range(PLANE)
                ]
                low, high = (theirs, mine) if side else (mine, theirs)
                result = []
                for k, (i, j) in enumerate(CROSS):
                    result += add_product(sums, k, low[i], high[j])
                return tuple(result)

            zero = jnp.zeros((8, 128), F32)
            sums = lax.fori_loop(0, part, body, (zero,) * (2 * N_CROSS), unroll=4)
            store_sums(cross, first_pair, row, re_lanes, im_lanes, sums)


def lags_kernel(
    spec, cross_in, near_3, far_3, table, l_high, l_low, out, out_first, out_second, last, cross
):
    member, _, odd = my_place()
    part = near_3.shape[0]
    diagonal = member ^ 3
    last[odd] = transform(near_3[...], table)
    last[1 - odd] = transform(far_3[...], table)
    cross[...] = cross_in[...]
    for row, rows, re_lanes, im_lanes in bin_parts():
        for side in range(2):

            def body(seg, sums):
                at = seg + side * part
                theirs = (last[side, seg, rows, re_lanes], last[side, seg, rows, im_lanes])
                result = []
                for w in range(PLANE):
                    mine = (spec[w, at, rows, re_lanes], spec[w, at, rows, im_lanes])
                    low, high = (theirs, mine) if side else (mine, theirs)
                    result += add_product(sums, w, low, high)
                return tuple(result)

            zero = jnp.zeros((8, 128), F32)
            sums = lax.fori_loop(0, part, body, (zero,) * (2 * PLANE), unroll=4)
            for w in range(PLANE):
                if side:
                    valid, pair = w <= diagonal, diagonal * (diagonal + 1) // 2 + w
                else:
                    valid, pair = w >= diagonal, N_CROSS + N_IN + w * (w + 1) // 2 + diagonal
                at = pl.ds(pl.multiple_of(jnp.where(valid, pair, 0) * QG + row, 8), 8)
                cross[at, re_lanes] += jnp.where(valid, sums[2 * w], 0.0)
                cross[at, im_lanes] += jnp.where(valid, sums[2 * w + 1], 0.0)
    high, low = split_terms(cross[...])

    def turned(left, right):
        return lax.dot_general(left, right, (((1,), (1,)), ((), ())), preferred_element_type=F32)

    lagged = turned(l_high[...], high) + turned(l_high[...], low) + turned(l_low[...], high)
    out[...] = lagged.astype(BF16)
    to_above = lagged[:, N_CROSS * QG :]
    to_below = lagged[:, : N_SENT * QG]
    out_first[...] = jnp.where(odd == 1, to_below, to_above).astype(BF16)
    out_second[...] = jnp.where(odd == 1, to_above, to_below).astype(BF16)


def choose_kernel(*refs):
    pids, chosen = refs[:4], refs[4]
    _, core, _ = my_place()
    row_id = lax.broadcasted_iota(jnp.int32, (N_ALL * QG, 128), 0)
    col_id = lax.broadcasted_iota(jnp.int32, (N_ALL * QG, 128), 1)
    row_key = jnp.where((row_id & 15) == (col_id & 15), (row_id >> 4).astype(F32), -1.0)
    lane = pl.multiple_of(core * 128, 128)
    for rel, pid in enumerate(pids):
        ids = pid[0, :, pl.ds(lane, 128)].astype(F32)
        match = (row_key == ids[0:1, :]) | (row_key == ids[8:9, :])
        chosen[:, rel * 128 : (rel + 1) * 128] = jnp.where(match, 1.0, 0.0).astype(BF16)


def select_kernel(chosen, *refs):
    mine, swapped, outs, lags = refs[0:3], refs[3:6], refs[6:10], refs[10]
    _, _, odd = my_place()
    own, sent = N_OWN * QG, N_SENT * QG
    for side, (here, first, second) in enumerate((mine, swapped)):
        at = slice(side * LAG_ROWS, (side + 1) * LAG_ROWS)
        below = jnp.where(odd == 1, first[...].astype(F32), second[...].astype(F32)).astype(BF16)
        above = jnp.where(odd == 1, second[...].astype(F32), first[...].astype(F32)).astype(BF16)
        lags[at, 0:own] = here[...]
        lags[at, own : own + sent] = below
        lags[at, own + sent : own + 2 * sent] = above
    picked = mxu(lags[...], chosen[...]).astype(BF16)
    for rel in range(4):
        for side in range(2):
            outs[rel][side] = picked[side * LAG_ROWS : (side + 1) * LAG_ROWS, rel * 128 : (rel + 1) * 128]


def finish_kernel(pairs, count, *refs):
    pieces, table, out, stage, flat = refs[:4], *refs[4:8]
    member, core, _ = my_place()
    for rel in range(4):
        for side in range(2):
            stage[(core ^ side) * 4 + (member ^ rel)] = pieces[rel][side].astype(F32)
    step = 16
    group = lax.broadcasted_iota(jnp.int32, (step, 128), 1) >> 4
    for row in range(0, LAG_ROWS, step):
        tiles = [stage[m, row : row + step] for m in range(8)]
        for bit in (4, 2, 1):
            upper = (group & bit) > 0
            for m in range(8):
                if not m & bit:
                    low, high = tiles[m], tiles[m | bit]
                    tiles[m] = jnp.where(upper, pltpu.roll(high, bit * QG, 1), low)
                    tiles[m | bit] = jnp.where(upper, high, pltpu.roll(low, 128 - bit * QG, 1))
        for s in range(8):
            flat[row : row + step, s * 128 : (s + 1) * 128] = tiles[s]
    back = mxu(table[...], flat[...].astype(BF16))
    for s in range(SLOTS // 2):
        lanes = slice(s * 128, (s + 1) * 128)
        slot = core * (SLOTS // 2) + s
        value = jnp.where(pairs[0, slot] > pairs[1, slot], back[:, lanes], flat[:, lanes])
        out[:, s, :] = jnp.where(slot < count[0], value, 0.0)[0:LAGS]


VM = pl.BlockSpec(memory_space=pltpu.VMEM)
SM = pl.BlockSpec(memory_space=pltpu.SMEM)
PARAMS = pltpu.CompilerParams(vmem_limit_bytes=VMEM_LIMIT)


def shape(dims, kind):
    return jax.ShapeDtypeStruct(dims, kind)


def local(traces, channel_ok, time_taps, space_taps, pair_blocks, pair_count):
    n_chan = lax.axis_size("chan")
    n_plane = n_chan // PLANE
    chan_width, half = traces.shape
    segs = 2 * half // SEG
    part = segs // 2
    core = lax.axis_index("tm")
    odd = (lax.axis_index("chan") // PLANE) % 2
    pairs = jnp.transpose(pair_blocks)

    def to_core(x):
        return lax.ppermute(x, "tm", [(0, 1), (1, 0)])

    def in_plane(x, rel):
        return lax.ppermute(x, "chan", [(c, c ^ rel) for c in range(n_chan)])

    def plane_swap(x, start):
        route = []
        for p in range(start, n_plane - 1, 2):
            for k in range(PLANE):
                low, high = p * PLANE + k, (p + 1) * PLANE + k
                route += [(low, high), (high, low)]
        return lax.ppermute(x, "chan", route)

    rows = chan_width // 2
    head, tail = traces[0:2], traces[chan_width - 2 :]
    give = jnp.where(core == 0, tail, head)
    mine = jnp.where(core == 0, head, tail)
    give, mine, time_taps, space_taps, channel_ok, pairs = lax.optimization_barrier(
        (give, mine, time_taps, space_taps, channel_ok, pairs)
    )
    got = to_core(give)
    alive = (jnp.where(core == 0, channel_ok[0:2], channel_ok[chan_width - 2 :]) > 0)[:, None]
    mine = jnp.where(alive, mine, 0.0)
    small = jnp.pad(time_taps[None, :], ((0, 7), (0, 128 - TAPS)))
    small = small + jnp.pad(space_taps[None, :], ((1, 6), (0, 128 - STAPS)))
    whole = jnp.pad(pairs, ((0, 6), (0, 128 - SLOTS)))
    whole = whole + jnp.pad(channel_ok[None, :], ((2, 5), (0, 128 - chan_width)))
    got, mine, small, whole = lax.optimization_barrier((got, mine, small, whole))
    route = []
    for c in range(n_chan - 1):
        route += [(2 * c + 1, 2 * c + 2), (2 * c + 2, 2 * c + 1)]
    edges = jnp.concatenate([mine, jnp.where(alive, got, 0.0)], axis=0)
    edges, late = lax.optimization_barrier((edges, traces))
    halos = lax.ppermute(edges, BOTH, route)
    other = to_core(late)
    table = shape((2 * SEG, SEG), BF16)
    split = shape((rows, half), BF16)
    t_high, t_low, pid, space, ok, own_high, own_low, own_near = pl.pallas_call(
        prepare_kernel,
        out_shape=[
            table, table, shape((QG, SLOTS * QG), BF16), shape((8, SEG), F32), shape((chan_width, 128), F32),
            split, split, shape((8, half), F32),
        ],
        in_specs=[SM, SM, VM, VM],
        out_specs=[VM] * 8,
        compiler_params=PARAMS,
        name="prepare",
    )(small, whole, whole, late)
    block = shape((segs + 1, QG, SEG), BF16)
    short = shape((part, QG, SEG), BF16)
    first, second, *sent = pl.pallas_call(
        filter_kernel,
        out_shape=[short] * 2 + [block] * 3,
        in_specs=[VM] * 10,
        out_specs=[VM] * 5,
        scratch_shapes=[
            pltpu.VMEM((rows + 16, 2 * half + SEG), BF16),
            pltpu.VMEM((rows + 16, 2 * half + SEG), BF16),
            pltpu.VMEM((8, half), F32),
            pltpu.VMEM((segs, rows, SEG), BF16),
        ],
        compiler_params=PARAMS,
        name="filter_whiten",
    )(own_near, own_high, own_low, other, halos, space, ok, t_high, t_low, pid)
    b1, b2 = in_plane(sent[0], 1), in_plane(sent[1], 2)
    far_0, near_0 = plane_swap(second, 1), plane_swap(first, 0)
    near_0, last = lax.optimization_barrier((near_0, sent[2]))
    b3 = in_plane(last, 3)
    b1, b2, near_0, far_0 = lax.optimization_barrier((b1, b2, near_0, far_0))
    def halves(x):
        near = lax.dynamic_slice_in_dim(x, (1 - odd) * part, part, axis=0)
        far = lax.dynamic_slice_in_dim(x, odd * part, part, axis=0)
        return near, far

    (near_1, far_1), (near_2, far_2) = halves(b1), halves(b2)
    far_12 = plane_swap(jnp.stack([far_1, far_2]), 1)
    near_12 = plane_swap(jnp.stack([near_1, near_2]), 0)
    near_3, far_3 = halves(b3)
    far_3, near_3 = plane_swap(far_3, 1), plane_swap(near_3, 0)
    scale = 1.0 / math.sqrt(segs * SEG)
    l_high, l_low = inverse_np(scale)
    sent_shape = shape((LAG_ROWS, N_SENT * QG), BF16)
    table = jnp.asarray(forward_np())
    short = shape((part, QG, 2 * SEG), F32)
    spec, spec_near, spec_far, inner = pl.pallas_call(
        inner_kernel,
        out_shape=[shape((PLANE, segs, QG, 2 * SEG), F32), short, short, shape((N_IN * QG, 2 * SEG), F32)],
        in_specs=[VM] * 8,
        out_specs=[VM] * 4,
        compiler_params=PARAMS,
        name="inner_pairs",
    )(first, second, b1, b2, b3, near_0, far_0, table)
    cross = pl.pallas_call(
        cross_kernel,
        out_shape=shape((N_OWN * QG, 2 * SEG), F32),
        in_specs=[VM] * 7,
        out_specs=VM,
        scratch_shapes=[pltpu.VMEM((2, PLANE, part, QG, 2 * SEG), F32)],
        compiler_params=PARAMS,
        name="cross_pairs",
    )(spec, spec_near, spec_far, inner, near_12, far_12, table)
    lags, lags_first, lags_second = pl.pallas_call(
        lags_kernel,
        out_shape=[shape((LAG_ROWS, N_OWN * QG), BF16), sent_shape, sent_shape],
        in_specs=[VM] * 7,
        out_specs=[VM] * 3,
        scratch_shapes=[
            pltpu.VMEM((2, part, QG, 2 * SEG), F32),
            pltpu.VMEM((N_OWN * QG, 2 * SEG), F32),
        ],
        compiler_params=PARAMS,
        name="pair_lags",
    )(spec, cross, near_3, far_3, table, jnp.asarray(l_high), jnp.asarray(l_low))
    from_first, from_second = plane_swap(lags_first, 0), plane_swap(lags_second, 1)
    known = [lags, from_first, from_second]
    pid_spec = pl.BlockSpec((1, QG, SEG), lambda step: (segs, 0, 0))
    own_spec = pl.BlockSpec((1, QG, SEG), lambda step: (0, 0, 0))
    slots_shape = shape((2, LAG_ROWS, 128), BF16)
    chosen = pl.pallas_call(
        choose_kernel,
        grid=(1,),
        out_shape=shape((N_ALL * QG, 512), BF16),
        in_specs=[own_spec] + [pid_spec] * 3,
        out_specs=VM,
        compiler_params=PARAMS,
        name="choose",
    )(pid[None], b1, b2, b3)
    picked = pl.pallas_call(
        select_kernel,
        out_shape=[slots_shape] * 4,
        in_specs=[VM] * 7,
        out_specs=[VM] * 4,
        scratch_shapes=[pltpu.VMEM((2 * LAG_ROWS, N_ALL * QG), BF16)],
        compiler_params=PARAMS,
        name="select_slots",
    )(chosen, *known, *[to_core(x) for x in known])
    pieces = [picked[0]] + [in_plane(x, rel + 1) for rel, x in enumerate(picked[1:])]
    out = pl.pallas_call(
        finish_kernel,
        out_shape=shape((LAGS, SLOTS // 2, chan_width), F32),
        in_specs=[SM] * 2 + [VM] * 5,
        out_specs=VM,
        scratch_shapes=[
            pltpu.VMEM((8, LAG_ROWS, 128), F32),
            pltpu.VMEM((LAG_ROWS, SLOTS // 2 * 128), F32),
        ],
        compiler_params=PARAMS,
        name="finish_slots",
    )(pairs, pair_count, *pieces, jnp.asarray(reverse_np()))
    return jnp.transpose(out, (1, 0, 2))


def solution(mesh):
    return jax.shard_map(
        local,
        mesh=mesh,
        in_specs=(P("chan", "tm"), P("chan"), P(), P(), P("chan", None), P("chan")),
        out_specs=P(("chan", "tm"), None, None),
        check_vma=False,
    )
```

```python
import math

import jax
import jax.numpy as jnp
import ml_dtypes
import numpy as np
from jax import lax
from jax.experimental import pallas as pl
from jax.experimental.pallas import tpu as pltpu
from jax.sharding import PartitionSpec as P

SEG = 256
MAXLAG = 100
TAPS = 33
STAPS = 5
SLOTS = 16
NFFT = 510
LAGS = 201
LAG_ROWS = 208
PLANE = 4
QG = 16
BOTH = ("chan", "tm")
F32 = jnp.float32
BF16 = jnp.bfloat16
VMEM_LIMIT = 20 * 1024 * 1024
INNER = [(0, 1), (0, 2), (0, 3), (1, 2), (1, 3), (2, 3)]
CROSS = [(i, j) for i in range(PLANE) for j in range(i + 1)]
N_IN, N_CROSS = len(INNER), len(CROSS)
N_OWN = N_CROSS + N_IN + N_CROSS
N_SENT = N_IN + N_CROSS
N_ALL = N_OWN + 2 * N_SENT


def split_np(table):
    high = table.astype(np.float32).astype(ml_dtypes.bfloat16)
    low = (table - high.astype(np.float64)).astype(np.float32).astype(ml_dtypes.bfloat16)
    return high, low


def forward_np():
    sample = np.arange(SEG)[:, None]
    bins = np.arange(SEG)[None, :]
    angle = (sample * bins % NFFT) * (2.0 * math.pi / NFFT)
    table = np.concatenate([np.cos(angle), -np.sin(angle)], axis=1)
    return table.astype(np.float32).astype(ml_dtypes.bfloat16)


def inverse_np(scale):
    lag = np.arange(LAG_ROWS)[:, None] - MAXLAG
    bins = np.arange(SEG)[None, :]
    angle = (lag * bins % NFFT) * (2.0 * math.pi / NFFT)
    weight = np.where((bins == 0) | (bins == SEG - 1), 1.0, 2.0) / NFFT * scale
    table = np.concatenate([weight * np.cos(angle), -weight * np.sin(angle)], axis=1)
    table[LAGS:] = 0.0
    return split_np(table)


def reverse_np():
    rows = np.arange(LAG_ROWS)
    table = (rows[:, None] + rows[None, :] == LAGS - 1).astype(np.float32)
    return table.astype(ml_dtypes.bfloat16)


def split_terms(value):
    high = value.astype(BF16)
    low = (value - high.astype(F32)).astype(BF16)
    return high, low


def mxu(a, b):
    return jnp.dot(a, b, preferred_element_type=F32)


def my_place():
    chan = lax.axis_index("chan")
    return chan % PLANE, lax.axis_index("tm"), (chan // PLANE) % 2


def pair_ids(first, second, plane):
    low, high = jnp.minimum(first, second), jnp.maximum(first, second)
    low_plane, low_at = low // PLANE - plane, low % PLANE
    high_plane, high_at = high // PLANE - plane, high % PLANE
    inner = jnp.int32(0)
    for k, (i, j) in enumerate(INNER):
        inner = jnp.where((low_at == i) & (high_at == j), k, inner)
    cross = low_at * (low_at + 1) // 2 + high_at
    one = jnp.where(
        low_plane == 0,
        jnp.where(high_plane == 0, N_CROSS + inner, N_CROSS + N_IN + cross),
        jnp.where(
            low_plane > 0,
            N_OWN + N_SENT + N_CROSS + inner,
            jnp.where(high_plane == 0, cross, N_OWN + inner),
        ),
    )
    two = jnp.where(
        low_plane == high_plane,
        N_ALL,
        jnp.where(low_plane == 0, N_OWN + N_SENT + cross, N_OWN + N_IN + cross),
    )
    return one, two


def tile_rows(own, core):
    rows = own.shape[0] // 2
    first_row = pl.multiple_of(core * rows, rows)
    near_row = pl.multiple_of(rows - 8 + 8 * (1 - core), 8)
    return pl.ds(first_row, rows), pl.ds(near_row, 8)


def prepare_kernel(
    small, whole, whole_rows, traces, t_high, t_low, pid, space, ok, flags, own_high, own_low, own_near,
):
    _, core, _ = my_place()
    plane = lax.axis_index("chan") // PLANE
    main, near = tile_rows(traces, core)
    t_high[...] = jnp.zeros(t_high.shape, BF16)
    t_low[...] = jnp.zeros(t_low.shape, BF16)
    shift = SEG // 2 - (TAPS - 1) // 2
    height = 128 + TAPS - 1
    tap = lax.broadcasted_iota(jnp.int32, (height, 128), 0) - lax.broadcasted_iota(
        jnp.int32, (height, 128), 1
    )
    band = jnp.zeros((height, 128), F32)
    for j in range(TAPS):
        band = jnp.where(tap == j, small[0, j], band)
    high, low = split_terms(band)
    for lanes in range(SEG // 128):
        at = (slice(lanes * 128 + shift, lanes * 128 + shift + height), slice(lanes * 128, lanes * 128 + 128))
        t_high[at] = high
        t_low[at] = low
    row = lax.broadcasted_iota(jnp.int32, space.shape, 0)
    value = jnp.zeros(space.shape, F32)
    for j in range(STAPS):
        value = jnp.where(row == j, small[1, j], value)
    space[...] = value
    slot = lax.broadcasted_iota(jnp.int32, pid.shape, 1) >> 4
    upper = lax.broadcasted_iota(jnp.int32, pid.shape, 0) < 8
    ids = jnp.zeros(pid.shape, jnp.int32)
    for s in range(SLOTS):
        one, two = pair_ids(whole[0, s], whole[1, s], plane)
        ids = jnp.where(slot == s, jnp.where(upper, one, two), ids)
    pid[...] = ids.astype(F32).astype(BF16)
    row = lax.broadcasted_iota(jnp.int32, flags.shape, 0)
    value = jnp.zeros(flags.shape, F32)
    for s in range(SLOTS // 2):
        slot = core * (SLOTS // 2) + s
        value = jnp.where(row == s, (whole[0, slot] > whole[1, slot]).astype(F32), value)
    flags[...] = value
    width = ok.shape[0]
    diagonal = lax.broadcasted_iota(jnp.int32, (width, width), 0) == lax.broadcasted_iota(
        jnp.int32, (width, width), 1
    )
    spread = jnp.where(diagonal, whole_rows[2:3, :width].astype(F32), 0.0)
    ok[...] = jnp.broadcast_to(jnp.sum(spread, axis=1, keepdims=True), ok.shape)
    own_high[...], own_low[...] = split_terms(traces[main, :] * ok[main, 0:1])
    own_near[...] = traces[near, :] * ok[near, 0:1]


def filter_kernel(
    own_near, own_high, own_low, other, halos, space, ok, t_high, t_low, pid,
    out_first, out_second, out_1, out_2, out_3, x_high, x_low, edge, white,
):
    member, core, odd = my_place()
    rows, half = own_high.shape
    main, near = tile_rows(other, core)
    pad = SEG // 2
    total = 2 * half
    zeros = jnp.zeros((rows + 16, pad), BF16)
    for buf in (x_high, x_low):
        buf[:, 0:pad] = zeros
        buf[:, pad + total : 2 * pad + total] = zeros
    own_lanes = pl.ds(pl.multiple_of(pad + core * half, pad), half)
    other_lanes = pl.ds(pl.multiple_of(pad + (1 - core) * half, pad), half)
    x_high[0:rows, own_lanes] = own_high[...]
    x_low[0:rows, own_lanes] = own_low[...]
    x_high[0:rows, other_lanes], x_low[0:rows, other_lanes] = split_terms(other[main, :] * ok[main, 0:1])
    other_near = other[near, :] * ok[near, 0:1]
    for inside, halo, lanes in ((own_near[...], halos[2:4], own_lanes), (other_near, halos[0:2], other_lanes)):
        for k in range(4):
            edge[2 * k : 2 * k + 2, :] = halo
        outside = edge[...]
        above = jnp.where(core == 0, outside, inside)
        below = jnp.where(core == 0, inside, outside)
        high, low = split_terms(jnp.concatenate([above, below], axis=0))
        x_high[rows : rows + 16, lanes] = high
        x_low[rows : rows + 16, lanes] = low
    segs = total // SEG
    chunk = 8
    height = rows + 16
    taps = [space[j : j + 1, :] for j in range(STAPS)]

    def body(step, carry):
        seg0 = step * chunk
        spans = [pl.ds(pl.multiple_of((seg0 + s) * SEG, SEG), 2 * SEG) for s in range(chunk)]
        high = jnp.concatenate([x_high[:, span] for span in spans], axis=0)
        low = jnp.concatenate([x_low[:, span] for span in spans], axis=0)
        y = mxu(high, t_high[...]) + mxu(low, t_high[...]) + mxu(high, t_low[...])
        for s in range(chunk):
            block = y[s * height : (s + 1) * height]
            ext = jnp.concatenate(
                [block[rows : rows + 8], block[0:rows], block[rows + 8 : rows + 16]], axis=0
            )
            filtered = taps[0] * ext[6 : 6 + rows]
            for j in range(1, STAPS):
                filtered = filtered + taps[j] * ext[6 + j : 6 + j + rows]
            power = jnp.mean(filtered * filtered, axis=1, keepdims=True)
            white[seg0 + s] = (filtered * (1.0 / jnp.sqrt(power + 1e-5))).astype(BF16)
        return carry

    lax.fori_loop(0, segs // chunk, body, 0, unroll=True)
    own_row = pl.multiple_of(member * QG, QG)
    part = segs // 2
    out_first[...] = white[pl.ds((1 - odd) * part, part), pl.ds(own_row, QG), :]
    out_second[...] = white[pl.ds(odd * part, part), pl.ds(own_row, QG), :]
    for rel, out in ((1, out_1), (2, out_2), (3, out_3)):
        row = pl.multiple_of((member ^ rel) * QG, QG)
        out[0:segs] = white[:, pl.ds(row, QG), :]
        out[segs] = pid[...]


def transform(block, table):
    value = mxu(block.reshape(block.shape[0] * QG, SEG), table[...])
    return value.astype(BF16).astype(F32).reshape(block.shape[0], QG, 2 * SEG)


def bin_parts():
    for q8 in range(QG // 8):
        for lanes in range(SEG // 128):
            rows = slice(q8 * 8, q8 * 8 + 8)
            re_lanes = slice(lanes * 128, lanes * 128 + 128)
            im_lanes = slice(SEG + lanes * 128, SEG + lanes * 128 + 128)
            yield q8 * 8, rows, re_lanes, im_lanes


def add_product(sums, index, left, right):
    re = sums[2 * index] + (left[0] * right[0] + left[1] * right[1])
    im = sums[2 * index + 1] + (left[1] * right[0] - left[0] * right[1])
    return [re, im]


def store_sums(cross, first_pair, row, re_lanes, im_lanes, sums):
    for index in range(len(sums) // 2):
        at = slice((first_pair + index) * QG + row, (first_pair + index) * QG + row + 8)
        cross[at, re_lanes] = sums[2 * index]
        cross[at, im_lanes] = sums[2 * index + 1]


def inner_kernel(first, second, b1, b2, b3, near_0, far_0, table, spec, spec_near, spec_far, inner):
    member, _, odd = my_place()
    segs = spec.shape[1]
    part = segs // 2
    spec[member, pl.ds((1 - odd) * part, part)] = transform(first[...], table)
    spec[member, pl.ds(odd * part, part)] = transform(second[...], table)
    for rel, ref in ((1, b1), (2, b2), (3, b3)):
        spec[member ^ rel] = transform(ref[0:segs], table)
    spec_near[...] = transform(near_0[...], table)
    spec_far[...] = transform(far_0[...], table)
    for row, rows, re_lanes, im_lanes in bin_parts():

        def body(seg, sums):
            mine = [(spec[w, seg, rows, re_lanes], spec[w, seg, rows, im_lanes]) for w in range(PLANE)]
            result = []
            for k, (i, j) in enumerate(INNER):
                result += add_product(sums, k, mine[i], mine[j])
            return tuple(result)

        zero = jnp.zeros((8, 128), F32)
        sums = lax.fori_loop(0, segs, body, (zero,) * (2 * N_IN), unroll=4)
        store_sums(inner, 0, row, re_lanes, im_lanes, sums)


def cross_kernel(spec, spec_near, spec_far, inner, near_12, far_12, table, cross, spec_z):
    member, _, odd = my_place()
    part = spec_near.shape[0]
    for side, done, pair in ((odd, spec_near, near_12), (1 - odd, spec_far, far_12)):
        spec_z[side, member] = done[...]
        spec_z[side, member ^ 1] = transform(pair[0], table)
        spec_z[side, member ^ 2] = transform(pair[1], table)
        spec_z[side, member ^ 3] = jnp.zeros(done.shape, F32)
    cross[N_CROSS * QG : (N_CROSS + N_IN) * QG, :] = inner[...]
    for row, rows, re_lanes, im_lanes in bin_parts():
        for side, first_pair in ((0, N_CROSS + N_IN), (1, 0)):

            def body(seg, sums):
                at = seg + side * part
                mine = [(spec[w, at, rows, re_lanes], spec[w, at, rows, im_lanes]) for w in range(PLANE)]
                theirs = [
                    (spec_z[side, w, seg, rows, re_lanes], spec_z[side, w, seg, rows, im_lanes])
                    for w in range(PLANE)
                ]
                low, high = (theirs, mine) if side else (mine, theirs)
                result = []
                for k, (i, j) in enumerate(CROSS):
                    result += add_product(sums, k, low[i], high[j])
                return tuple(result)

            zero = jnp.zeros((8, 128), F32)
            sums = lax.fori_loop(0, part, body, (zero,) * (2 * N_CROSS), unroll=4)
            store_sums(cross, first_pair, row, re_lanes, im_lanes, sums)


def lags_kernel(
    spec, cross_in, near_3, far_3, table, l_high, l_low, out, out_first, out_second, last, cross
):
    member, _, odd = my_place()
    part = near_3.shape[0]
    diagonal = member ^ 3
    last[odd] = transform(near_3[...], table)
    last[1 - odd] = transform(far_3[...], table)
    cross[...] = cross_in[...]
    for row, rows, re_lanes, im_lanes in bin_parts():
        for side in range(2):

            def body(seg, sums):
                at = seg + side * part
                theirs = (last[side, seg, rows, re_lanes], last[side, seg, rows, im_lanes])
                result = []
                for w in range(PLANE):
                    mine = (spec[w, at, rows, re_lanes], spec[w, at, rows, im_lanes])
                    low, high = (theirs, mine) if side else (mine, theirs)
                    result += add_product(sums, w, low, high)
                return tuple(result)

            zero = jnp.zeros((8, 128), F32)
            sums = lax.fori_loop(0, part, body, (zero,) * (2 * PLANE), unroll=4)
            for w in range(PLANE):
                if side:
                    valid, pair = w <= diagonal, diagonal * (diagonal + 1) // 2 + w
                else:
                    valid, pair = w >= diagonal, N_CROSS + N_IN + w * (w + 1) // 2 + diagonal
                at = pl.ds(pl.multiple_of(jnp.where(valid, pair, 0) * QG + row, 8), 8)
                cross[at, re_lanes] += jnp.where(valid, sums[2 * w], 0.0)
                cross[at, im_lanes] += jnp.where(valid, sums[2 * w + 1], 0.0)
    high, low = split_terms(cross[...])

    def turned(left, right):
        return lax.dot_general(left, right, (((1,), (1,)), ((), ())), preferred_element_type=F32)

    lagged = turned(l_high[...], high) + turned(l_high[...], low) + turned(l_low[...], high)
    out[...] = lagged.astype(BF16)
    to_above = lagged[:, N_CROSS * QG :]
    to_below = lagged[:, : N_SENT * QG]
    out_first[...] = jnp.where(odd == 1, to_below, to_above).astype(BF16)
    out_second[...] = jnp.where(odd == 1, to_above, to_below).astype(BF16)


def choose_kernel(*refs):
    pids, chosen = refs[:4], refs[4]
    _, core, _ = my_place()
    row_id = lax.broadcasted_iota(jnp.int32, (N_ALL * QG, 128), 0)
    col_id = lax.broadcasted_iota(jnp.int32, (N_ALL * QG, 128), 1)
    row_key = jnp.where((row_id & 15) == (col_id & 15), (row_id >> 4).astype(F32), -1.0)
    lane = pl.multiple_of(core * 128, 128)
    for rel, pid in enumerate(pids):
        ids = pid[0, :, pl.ds(lane, 128)].astype(F32)
        match = (row_key == ids[0:1, :]) | (row_key == ids[8:9, :])
        chosen[:, rel * 128 : (rel + 1) * 128] = jnp.where(match, 1.0, 0.0).astype(BF16)


def select_kernel(chosen, *refs):
    mine, swapped, outs, lags = refs[0:3], refs[3:6], refs[6:10], refs[10]
    _, _, odd = my_place()
    own, sent = N_OWN * QG, N_SENT * QG
    for side, (here, first, second) in enumerate((mine, swapped)):
        at = slice(side * LAG_ROWS, (side + 1) * LAG_ROWS)
        below = jnp.where(odd == 1, first[...].astype(F32), second[...].astype(F32)).astype(BF16)
        above = jnp.where(odd == 1, second[...].astype(F32), first[...].astype(F32)).astype(BF16)
        lags[at, 0:own] = here[...]
        lags[at, own : own + sent] = below
        lags[at, own + sent : own + 2 * sent] = above
    picked = mxu(lags[...], chosen[...]).astype(BF16)
    for rel in range(4):
        for side in range(2):
            outs[rel][side] = picked[side * LAG_ROWS : (side + 1) * LAG_ROWS, rel * 128 : (rel + 1) * 128]


def finish_kernel(count, flags, *refs):
    pieces, table, out, stage, flat, done, sems = refs[:4], *refs[4:10]
    member, core, _ = my_place()
    for rel in range(4):
        for side in range(2):
            stage[(core ^ side) * 4 + (member ^ rel)] = pieces[rel][side].astype(F32)
    step = 16
    group = lax.broadcasted_iota(jnp.int32, (step, 128), 1) >> 4
    for row in range(0, LAG_ROWS, step):
        tiles = [stage[m, row : row + step] for m in range(8)]
        for bit in (4, 2, 1):
            upper = (group & bit) > 0
            for m in range(8):
                if not m & bit:
                    low, high = tiles[m], tiles[m | bit]
                    tiles[m] = jnp.where(upper, pltpu.roll(high, bit * QG, 1), low)
                    tiles[m | bit] = jnp.where(upper, high, pltpu.roll(low, 128 - bit * QG, 1))
        for s in range(8):
            flat[row : row + step, s * 128 : (s + 1) * 128] = tiles[s]
    flat_low = flat[...].astype(BF16)
    copies = []
    for k, (start, stop) in enumerate(((0, 64), (64, 128), (128, LAGS))):
        end = min(start + 80, LAG_ROWS) if stop == LAGS else stop
        back = mxu(table[start:end, :], flat_low)
        for s in range(SLOTS // 2):
            lanes = slice(s * 128, (s + 1) * 128)
            turned, alive = flags[s : s + 1, :] > 0.0, core * (SLOTS // 2) + s < count[0]
            value = jnp.where(turned, back[:, lanes], flat[start:end, lanes])
            done[start:stop, s, :] = jnp.where(alive, value, 0.0)[0 : stop - start]
        copies.append(pltpu.make_async_copy(done.at[start:stop], out.at[start:stop], sems.at[k]))
        copies[-1].start()
    for copy in copies:
        copy.wait()


VM = pl.BlockSpec(memory_space=pltpu.VMEM)
SM = pl.BlockSpec(memory_space=pltpu.SMEM)
PARAMS = pltpu.CompilerParams(vmem_limit_bytes=VMEM_LIMIT)


def shape(dims, kind):
    return jax.ShapeDtypeStruct(dims, kind)


def local(traces, channel_ok, time_taps, space_taps, pair_blocks, pair_count):
    n_chan = lax.axis_size("chan")
    n_plane = n_chan // PLANE
    chan_width, half = traces.shape
    segs = 2 * half // SEG
    part = segs // 2
    core = lax.axis_index("tm")
    odd = (lax.axis_index("chan") // PLANE) % 2
    pairs = jnp.transpose(pair_blocks)

    def to_core(x):
        return lax.ppermute(x, "tm", [(0, 1), (1, 0)])

    def in_plane(x, rel):
        return lax.ppermute(x, "chan", [(c, c ^ rel) for c in range(n_chan)])

    def plane_swap(x, start):
        route = []
        for p in range(start, n_plane - 1, 2):
            for k in range(PLANE):
                low, high = p * PLANE + k, (p + 1) * PLANE + k
                route += [(low, high), (high, low)]
        return lax.ppermute(x, "chan", route)

    rows = chan_width // 2
    head, tail = traces[0:2], traces[chan_width - 2 :]
    give = jnp.where(core == 0, tail, head)
    mine = jnp.where(core == 0, head, tail)
    give, mine, time_taps, space_taps, channel_ok, pairs = lax.optimization_barrier(
        (give, mine, time_taps, space_taps, channel_ok, pairs)
    )
    got = to_core(give)
    alive = (jnp.where(core == 0, channel_ok[0:2], channel_ok[chan_width - 2 :]) > 0)[:, None]
    mine = jnp.where(alive, mine, 0.0)
    small = jnp.pad(time_taps[None, :], ((0, 7), (0, 128 - TAPS)))
    small = small + jnp.pad(space_taps[None, :], ((1, 6), (0, 128 - STAPS)))
    whole = jnp.pad(pairs, ((0, 6), (0, 128 - SLOTS)))
    whole = whole + jnp.pad(channel_ok[None, :], ((2, 5), (0, 128 - chan_width)))
    got, mine, small, whole = lax.optimization_barrier((got, mine, small, whole))
    route = []
    for c in range(n_chan - 1):
        route += [(2 * c + 1, 2 * c + 2), (2 * c + 2, 2 * c + 1)]
    edges = jnp.concatenate([mine, jnp.where(alive, got, 0.0)], axis=0)
    edges, late = lax.optimization_barrier((edges, traces))
    halos = lax.ppermute(edges, BOTH, route)
    other = to_core(late)
    table = shape((2 * SEG, SEG), BF16)
    split = shape((rows, half), BF16)
    t_high, t_low, pid, space, ok, flags, own_high, own_low, own_near = pl.pallas_call(
        prepare_kernel,
        out_shape=[
            table, table, shape((QG, SLOTS * QG), BF16), shape((8, SEG), F32), shape((chan_width, 128), F32),
            shape((8, 128), F32), split, split, shape((8, half), F32),
        ],
        in_specs=[SM, SM, VM, VM],
        out_specs=[VM] * 9,
        compiler_params=PARAMS,
        name="prepare",
    )(small, whole, whole, late)
    block = shape((segs + 1, QG, SEG), BF16)
    short = shape((part, QG, SEG), BF16)
    first, second, *sent = pl.pallas_call(
        filter_kernel,
        out_shape=[short] * 2 + [block] * 3,
        in_specs=[VM] * 10,
        out_specs=[VM] * 5,
        scratch_shapes=[
            pltpu.VMEM((rows + 16, 2 * half + SEG), BF16),
            pltpu.VMEM((rows + 16, 2 * half + SEG), BF16),
            pltpu.VMEM((8, half), F32),
            pltpu.VMEM((segs, rows, SEG), BF16),
        ],
        compiler_params=PARAMS,
        name="filter_whiten",
    )(own_near, own_high, own_low, other, halos, space, ok, t_high, t_low, pid)
    b1, b2 = in_plane(sent[0], 1), in_plane(sent[1], 2)
    far_0, near_0 = plane_swap(second, 1), plane_swap(first, 0)
    near_0, last = lax.optimization_barrier((near_0, sent[2]))
    b3 = in_plane(last, 3)
    b1, b2, near_0, far_0 = lax.optimization_barrier((b1, b2, near_0, far_0))
    def halves(x):
        near = lax.dynamic_slice_in_dim(x, (1 - odd) * part, part, axis=0)
        far = lax.dynamic_slice_in_dim(x, odd * part, part, axis=0)
        return near, far

    (near_1, far_1), (near_2, far_2) = halves(b1), halves(b2)
    far_12 = plane_swap(jnp.stack([far_1, far_2]), 1)
    near_12 = plane_swap(jnp.stack([near_1, near_2]), 0)
    near_3, far_3 = halves(b3)
    far_3, near_3 = plane_swap(far_3, 1), plane_swap(near_3, 0)
    scale = 1.0 / math.sqrt(segs * SEG)
    l_high, l_low = inverse_np(scale)
    sent_shape = shape((LAG_ROWS, N_SENT * QG), BF16)
    table = jnp.asarray(forward_np())
    short = shape((part, QG, 2 * SEG), F32)
    spec, spec_near, spec_far, inner = pl.pallas_call(
        inner_kernel,
        out_shape=[shape((PLANE, segs, QG, 2 * SEG), F32), short, short, shape((N_IN * QG, 2 * SEG), F32)],
        in_specs=[VM] * 8,
        out_specs=[VM] * 4,
        compiler_params=PARAMS,
        name="inner_pairs",
    )(first, second, b1, b2, b3, near_0, far_0, table)
    cross = pl.pallas_call(
        cross_kernel,
        out_shape=shape((N_OWN * QG, 2 * SEG), F32),
        in_specs=[VM] * 7,
        out_specs=VM,
        scratch_shapes=[pltpu.VMEM((2, PLANE, part, QG, 2 * SEG), F32)],
        compiler_params=PARAMS,
        name="cross_pairs",
    )(spec, spec_near, spec_far, inner, near_12, far_12, table)
    lags, lags_first, lags_second = pl.pallas_call(
        lags_kernel,
        out_shape=[shape((LAG_ROWS, N_OWN * QG), BF16), sent_shape, sent_shape],
        in_specs=[VM] * 7,
        out_specs=[VM] * 3,
        scratch_shapes=[
            pltpu.VMEM((2, part, QG, 2 * SEG), F32),
            pltpu.VMEM((N_OWN * QG, 2 * SEG), F32),
        ],
        compiler_params=PARAMS,
        name="pair_lags",
    )(spec, cross, near_3, far_3, table, jnp.asarray(l_high), jnp.asarray(l_low))
    from_first, from_second = plane_swap(lags_first, 0), plane_swap(lags_second, 1)
    known = [lags, from_first, from_second]
    pid_spec = pl.BlockSpec((1, QG, SEG), lambda step: (segs, 0, 0))
    own_spec = pl.BlockSpec((1, QG, SEG), lambda step: (0, 0, 0))
    slots_shape = shape((2, LAG_ROWS, 128), BF16)
    chosen = pl.pallas_call(
        choose_kernel,
        grid=(1,),
        out_shape=shape((N_ALL * QG, 512), BF16),
        in_specs=[own_spec] + [pid_spec] * 3,
        out_specs=VM,
        compiler_params=PARAMS,
        name="choose",
    )(pid[None], b1, b2, b3)
    picked = pl.pallas_call(
        select_kernel,
        out_shape=[slots_shape] * 4,
        in_specs=[VM] * 7,
        out_specs=[VM] * 4,
        scratch_shapes=[pltpu.VMEM((2 * LAG_ROWS, N_ALL * QG), BF16)],
        compiler_params=PARAMS,
        name="select_slots",
    )(chosen, *known, *[to_core(x) for x in known])
    pieces = [picked[0]] + [in_plane(x, rel + 1) for rel, x in enumerate(picked[1:])]
    out = pl.pallas_call(
        finish_kernel,
        out_shape=shape((LAGS, SLOTS // 2, chan_width), F32),
        in_specs=[SM] + [VM] * 6,
        out_specs=pl.BlockSpec(memory_space=pl.ANY),
        scratch_shapes=[
            pltpu.VMEM((8, LAG_ROWS, 128), F32),
            pltpu.VMEM((LAG_ROWS, SLOTS // 2 * 128), F32),
            pltpu.VMEM((LAGS, SLOTS // 2, 128), F32),
            pltpu.SemaphoreType.DMA((3,)),
        ],
        compiler_params=PARAMS,
        name="finish_slots",
    )(pair_count, flags, *pieces, jnp.asarray(reverse_np()))
    return jnp.transpose(out, (1, 0, 2))


def solution(mesh):
    return jax.shard_map(
        local,
        mesh=mesh,
        in_specs=(P("chan", "tm"), P("chan"), P(), P(), P("chan", None), P("chan")),
        out_specs=P(("chan", "tm"), None, None),
        check_vma=False,
    )
```

```python
import math

import jax
import jax.numpy as jnp
import ml_dtypes
import numpy as np
from jax import lax
from jax.experimental import pallas as pl
from jax.experimental.pallas import tpu as pltpu
from jax.sharding import PartitionSpec as P

SEG = 256
MAXLAG = 100
TAPS = 33
STAPS = 5
SLOTS = 16
NFFT = 510
LAGS = 201
LAG_ROWS = 208
PLANE = 4
QG = 16
BOTH = ("chan", "tm")
F32 = jnp.float32
BF16 = jnp.bfloat16
VMEM_LIMIT = 20 * 1024 * 1024
INNER = [(0, 1), (0, 2), (0, 3), (1, 2), (1, 3), (2, 3)]
CROSS = [(i, j) for i in range(PLANE) for j in range(i + 1)]
N_IN, N_CROSS = len(INNER), len(CROSS)
N_OWN = N_CROSS + N_IN + N_CROSS
N_SENT = N_IN + N_CROSS
N_ALL = N_OWN + 2 * N_SENT


def split_np(table):
    high = table.astype(np.float32).astype(ml_dtypes.bfloat16)
    low = (table - high.astype(np.float64)).astype(np.float32).astype(ml_dtypes.bfloat16)
    return high, low


def forward_np():
    sample = np.arange(SEG)[:, None]
    bins = np.arange(SEG)[None, :]
    angle = (sample * bins % NFFT) * (2.0 * math.pi / NFFT)
    table = np.concatenate([np.cos(angle), -np.sin(angle)], axis=1)
    return table.astype(np.float32).astype(ml_dtypes.bfloat16)


def inverse_np(scale):
    lag = np.arange(LAG_ROWS)[:, None] - MAXLAG
    bins = np.arange(SEG)[None, :]
    angle = (lag * bins % NFFT) * (2.0 * math.pi / NFFT)
    weight = np.where((bins == 0) | (bins == SEG - 1), 1.0, 2.0) / NFFT * scale
    table = np.concatenate([weight * np.cos(angle), -weight * np.sin(angle)], axis=1)
    table[LAGS:] = 0.0
    return split_np(table)


def reverse_np():
    rows = np.arange(LAG_ROWS)
    table = (rows[:, None] + rows[None, :] == LAGS - 1).astype(np.float32)
    return table.astype(ml_dtypes.bfloat16)


def split_terms(value):
    high = value.astype(BF16)
    low = (value - high.astype(F32)).astype(BF16)
    return high, low


def mxu(a, b):
    return jnp.dot(a, b, preferred_element_type=F32)


def my_place():
    chan = lax.axis_index("chan")
    return chan % PLANE, lax.axis_index("tm"), (chan // PLANE) % 2


def pair_ids(first, second, plane):
    low, high = jnp.minimum(first, second), jnp.maximum(first, second)
    low_plane, low_at = low // PLANE - plane, low % PLANE
    high_plane, high_at = high // PLANE - plane, high % PLANE
    inner = jnp.int32(0)
    for k, (i, j) in enumerate(INNER):
        inner = jnp.where((low_at == i) & (high_at == j), k, inner)
    cross = low_at * (low_at + 1) // 2 + high_at
    one = jnp.where(
        low_plane == 0,
        jnp.where(high_plane == 0, N_CROSS + inner, N_CROSS + N_IN + cross),
        jnp.where(
            low_plane > 0,
            N_OWN + N_SENT + N_CROSS + inner,
            jnp.where(high_plane == 0, cross, N_OWN + inner),
        ),
    )
    two = jnp.where(
        low_plane == high_plane,
        N_ALL,
        jnp.where(low_plane == 0, N_OWN + N_SENT + cross, N_OWN + N_IN + cross),
    )
    return one, two


def tile_rows(own, core):
    rows = own.shape[0] // 2
    first_row = pl.multiple_of(core * rows, rows)
    near_row = pl.multiple_of(rows - 8 + 8 * (1 - core), 8)
    return pl.ds(first_row, rows), pl.ds(near_row, 8)


def prepare_kernel(
    small, whole, whole_rows, traces, t_high, t_low, pid, space, ok, flags, own_high, own_low, own_near,
):
    _, core, _ = my_place()
    plane = lax.axis_index("chan") // PLANE
    main, near = tile_rows(traces, core)
    t_high[...] = jnp.zeros(t_high.shape, BF16)
    t_low[...] = jnp.zeros(t_low.shape, BF16)
    shift = SEG // 2 - (TAPS - 1) // 2
    height = 128 + TAPS - 1
    tap = lax.broadcasted_iota(jnp.int32, (height, 128), 0) - lax.broadcasted_iota(
        jnp.int32, (height, 128), 1
    )
    band = jnp.zeros((height, 128), F32)
    for j in range(TAPS):
        band = jnp.where(tap == j, small[0, j], band)
    high, low = split_terms(band)
    for lanes in range(SEG // 128):
        at = (slice(lanes * 128 + shift, lanes * 128 + shift + height), slice(lanes * 128, lanes * 128 + 128))
        t_high[at] = high
        t_low[at] = low
    row = lax.broadcasted_iota(jnp.int32, space.shape, 0)
    value = jnp.zeros(space.shape, F32)
    for j in range(STAPS):
        value = jnp.where(row == j, small[1, j], value)
    space[...] = value
    slot = lax.broadcasted_iota(jnp.int32, pid.shape, 1) >> 4
    upper = lax.broadcasted_iota(jnp.int32, pid.shape, 0) < 8
    ids = jnp.zeros(pid.shape, jnp.int32)
    for s in range(SLOTS):
        one, two = pair_ids(whole[0, s], whole[1, s], plane)
        ids = jnp.where(slot == s, jnp.where(upper, one, two), ids)
    pid[...] = ids.astype(F32).astype(BF16)
    row = lax.broadcasted_iota(jnp.int32, flags.shape, 0)
    value = jnp.zeros(flags.shape, F32)
    for s in range(SLOTS // 2):
        slot = core * (SLOTS // 2) + s
        value = jnp.where(row == s, (whole[0, slot] > whole[1, slot]).astype(F32), value)
    flags[...] = value
    width = ok.shape[0]
    diagonal = lax.broadcasted_iota(jnp.int32, (width, width), 0) == lax.broadcasted_iota(
        jnp.int32, (width, width), 1
    )
    spread = jnp.where(diagonal, whole_rows[2:3, :width].astype(F32), 0.0)
    ok[...] = jnp.broadcast_to(jnp.sum(spread, axis=1, keepdims=True), ok.shape)
    own_high[...], own_low[...] = split_terms(traces[main, :] * ok[main, 0:1])
    own_near[...] = traces[near, :] * ok[near, 0:1]


def filter_kernel(
    own_near, own_high, own_low, other, halos, space, ok, t_high, t_low, pid,
    out_first, out_second, out_1, out_2, out_3, x_high, x_low, edge, white,
):
    member, core, odd = my_place()
    rows, half = own_high.shape
    main, near = tile_rows(other, core)
    pad = SEG // 2
    total = 2 * half
    zeros = jnp.zeros((rows + 16, pad), BF16)
    for buf in (x_high, x_low):
        buf[:, 0:pad] = zeros
        buf[:, pad + total : 2 * pad + total] = zeros
    own_lanes = pl.ds(pl.multiple_of(pad + core * half, pad), half)
    other_lanes = pl.ds(pl.multiple_of(pad + (1 - core) * half, pad), half)
    x_high[0:rows, own_lanes] = own_high[...]
    x_low[0:rows, own_lanes] = own_low[...]
    x_high[0:rows, other_lanes], x_low[0:rows, other_lanes] = split_terms(other[main, :] * ok[main, 0:1])
    other_near = other[near, :] * ok[near, 0:1]
    for inside, halo, lanes in ((own_near[...], halos[2:4], own_lanes), (other_near, halos[0:2], other_lanes)):
        for k in range(4):
            edge[2 * k : 2 * k + 2, :] = halo
        outside = edge[...]
        above = jnp.where(core == 0, outside, inside)
        below = jnp.where(core == 0, inside, outside)
        high, low = split_terms(jnp.concatenate([above, below], axis=0))
        x_high[rows : rows + 16, lanes] = high
        x_low[rows : rows + 16, lanes] = low
    segs = total // SEG
    chunk = 8
    height = rows + 16
    taps = [space[j : j + 1, :] for j in range(STAPS)]
    t_all = jnp.concatenate([t_high[...], t_high[...], t_low[...]], axis=0)

    def body(step, carry):
        seg0 = step * chunk
        spans = [pl.ds(pl.multiple_of((seg0 + s) * SEG, SEG), 2 * SEG) for s in range(chunk)]
        high = jnp.concatenate([x_high[:, span] for span in spans], axis=0)
        low = jnp.concatenate([x_low[:, span] for span in spans], axis=0)
        y = mxu(jnp.concatenate([high, low, high], axis=1), t_all)
        for s in range(chunk):
            block = y[s * height : (s + 1) * height]
            ext = jnp.concatenate(
                [block[rows : rows + 8], block[0:rows], block[rows + 8 : rows + 16]], axis=0
            )
            filtered = taps[0] * ext[6 : 6 + rows]
            for j in range(1, STAPS):
                filtered = filtered + taps[j] * ext[6 + j : 6 + j + rows]
            power = jnp.mean(filtered * filtered, axis=1, keepdims=True)
            white[seg0 + s] = (filtered * (1.0 / jnp.sqrt(power + 1e-5))).astype(BF16)
        return carry

    lax.fori_loop(0, segs // chunk, body, 0, unroll=True)
    own_row = pl.multiple_of(member * QG, QG)
    part = segs // 2
    out_first[...] = white[pl.ds((1 - odd) * part, part), pl.ds(own_row, QG), :]
    out_second[...] = white[pl.ds(odd * part, part), pl.ds(own_row, QG), :]
    for rel, out in ((1, out_1), (2, out_2), (3, out_3)):
        row = pl.multiple_of((member ^ rel) * QG, QG)
        out[0:segs] = white[:, pl.ds(row, QG), :]
        out[segs] = pid[...]


def transform(block, table):
    value = mxu(block.reshape(block.shape[0] * QG, SEG), table[...])
    return value.astype(BF16).astype(F32).reshape(block.shape[0], QG, 2 * SEG)


def bin_parts():
    for q8 in range(QG // 8):
        for lanes in range(SEG // 128):
            rows = slice(q8 * 8, q8 * 8 + 8)
            re_lanes = slice(lanes * 128, lanes * 128 + 128)
            im_lanes = slice(SEG + lanes * 128, SEG + lanes * 128 + 128)
            yield q8 * 8, rows, re_lanes, im_lanes


def add_product(sums, index, left, right):
    re = sums[2 * index] + (left[0] * right[0] + left[1] * right[1])
    im = sums[2 * index + 1] + (left[1] * right[0] - left[0] * right[1])
    return [re, im]


def store_sums(cross, first_pair, row, re_lanes, im_lanes, sums):
    for index in range(len(sums) // 2):
        at = slice((first_pair + index) * QG + row, (first_pair + index) * QG + row + 8)
        cross[at, re_lanes] = sums[2 * index]
        cross[at, im_lanes] = sums[2 * index + 1]


def inner_kernel(first, second, b1, b2, b3, near_0, far_0, table, spec, spec_near, spec_far, inner):
    member, _, odd = my_place()
    segs = spec.shape[1]
    part = segs // 2
    spec[member, pl.ds((1 - odd) * part, part)] = transform(first[...], table)
    spec[member, pl.ds(odd * part, part)] = transform(second[...], table)
    for rel, ref in ((1, b1), (2, b2), (3, b3)):
        spec[member ^ rel] = transform(ref[0:segs], table)
    spec_near[...] = transform(near_0[...], table)
    spec_far[...] = transform(far_0[...], table)
    for row, rows, re_lanes, im_lanes in bin_parts():

        def body(seg, sums):
            mine = [(spec[w, seg, rows, re_lanes], spec[w, seg, rows, im_lanes]) for w in range(PLANE)]
            result = []
            for k, (i, j) in enumerate(INNER):
                result += add_product(sums, k, mine[i], mine[j])
            return tuple(result)

        zero = jnp.zeros((8, 128), F32)
        sums = lax.fori_loop(0, segs, body, (zero,) * (2 * N_IN), unroll=4)
        store_sums(inner, 0, row, re_lanes, im_lanes, sums)


def cross_kernel(spec, spec_near, spec_far, inner, near_12, far_12, table, cross, spec_z):
    member, _, odd = my_place()
    part = spec_near.shape[0]
    for side, done, pair in ((odd, spec_near, near_12), (1 - odd, spec_far, far_12)):
        spec_z[side, member] = done[...]
        spec_z[side, member ^ 1] = transform(pair[0], table)
        spec_z[side, member ^ 2] = transform(pair[1], table)
        spec_z[side, member ^ 3] = jnp.zeros(done.shape, F32)
    cross[N_CROSS * QG : (N_CROSS + N_IN) * QG, :] = inner[...]
    for row, rows, re_lanes, im_lanes in bin_parts():
        for side, first_pair in ((0, N_CROSS + N_IN), (1, 0)):

            def body(seg, sums):
                at = seg + side * part
                mine = [(spec[w, at, rows, re_lanes], spec[w, at, rows, im_lanes]) for w in range(PLANE)]
                theirs = [
                    (spec_z[side, w, seg, rows, re_lanes], spec_z[side, w, seg, rows, im_lanes])
                    for w in range(PLANE)
                ]
                low, high = (theirs, mine) if side else (mine, theirs)
                result = []
                for k, (i, j) in enumerate(CROSS):
                    result += add_product(sums, k, low[i], high[j])
                return tuple(result)

            zero = jnp.zeros((8, 128), F32)
            sums = lax.fori_loop(0, part, body, (zero,) * (2 * N_CROSS), unroll=4)
            store_sums(cross, first_pair, row, re_lanes, im_lanes, sums)


def lags_kernel(
    spec, cross_in, near_3, far_3, table, l_high, l_low, out, out_first, out_second, last, cross
):
    member, _, odd = my_place()
    part = near_3.shape[0]
    diagonal = member ^ 3
    last[odd] = transform(near_3[...], table)
    last[1 - odd] = transform(far_3[...], table)
    cross[...] = cross_in[...]
    for row, rows, re_lanes, im_lanes in bin_parts():
        for side in range(2):

            def body(seg, sums):
                at = seg + side * part
                theirs = (last[side, seg, rows, re_lanes], last[side, seg, rows, im_lanes])
                result = []
                for w in range(PLANE):
                    mine = (spec[w, at, rows, re_lanes], spec[w, at, rows, im_lanes])
                    low, high = (theirs, mine) if side else (mine, theirs)
                    result += add_product(sums, w, low, high)
                return tuple(result)

            zero = jnp.zeros((8, 128), F32)
            sums = lax.fori_loop(0, part, body, (zero,) * (2 * PLANE), unroll=4)
            for w in range(PLANE):
                if side:
                    valid, pair = w <= diagonal, diagonal * (diagonal + 1) // 2 + w
                else:
                    valid, pair = w >= diagonal, N_CROSS + N_IN + w * (w + 1) // 2 + diagonal
                at = pl.ds(pl.multiple_of(jnp.where(valid, pair, 0) * QG + row, 8), 8)
                cross[at, re_lanes] += jnp.where(valid, sums[2 * w], 0.0)
                cross[at, im_lanes] += jnp.where(valid, sums[2 * w + 1], 0.0)
    high, low = split_terms(cross[...])

    def turned(left, right):
        return lax.dot_general(left, right, (((1,), (1,)), ((), ())), preferred_element_type=F32)

    lagged = turned(l_high[...], high) + turned(l_high[...], low) + turned(l_low[...], high)
    out[...] = lagged.astype(BF16)
    to_above = lagged[:, N_CROSS * QG :]
    to_below = lagged[:, : N_SENT * QG]
    out_first[...] = jnp.where(odd == 1, to_below, to_above).astype(BF16)
    out_second[...] = jnp.where(odd == 1, to_above, to_below).astype(BF16)


def choose_kernel(*refs):
    pids, chosen = refs[:4], refs[4]
    _, core, _ = my_place()
    row_id = lax.broadcasted_iota(jnp.int32, (N_ALL * QG, 128), 0)
    col_id = lax.broadcasted_iota(jnp.int32, (N_ALL * QG, 128), 1)
    row_key = jnp.where((row_id & 15) == (col_id & 15), (row_id >> 4).astype(F32), -1.0)
    lane = pl.multiple_of(core * 128, 128)
    for rel, pid in enumerate(pids):
        ids = pid[0, :, pl.ds(lane, 128)].astype(F32)
        match = (row_key == ids[0:1, :]) | (row_key == ids[8:9, :])
        chosen[:, rel * 128 : (rel + 1) * 128] = jnp.where(match, 1.0, 0.0).astype(BF16)


def select_kernel(chosen, *refs):
    mine, swapped, outs, lags = refs[0:3], refs[3:6], refs[6:10], refs[10]
    _, _, odd = my_place()
    own, sent = N_OWN * QG, N_SENT * QG
    for side, (here, first, second) in enumerate((mine, swapped)):
        at = slice(side * LAG_ROWS, (side + 1) * LAG_ROWS)
        below = jnp.where(odd == 1, first[...].astype(F32), second[...].astype(F32)).astype(BF16)
        above = jnp.where(odd == 1, second[...].astype(F32), first[...].astype(F32)).astype(BF16)
        lags[at, 0:own] = here[...]
        lags[at, own : own + sent] = below
        lags[at, own + sent : own + 2 * sent] = above
    picked = mxu(lags[...], chosen[...]).astype(BF16)
    for rel in range(4):
        for side in range(2):
            outs[rel][side] = picked[side * LAG_ROWS : (side + 1) * LAG_ROWS, rel * 128 : (rel + 1) * 128]


def finish_kernel(count, flags, *refs):
    pieces, table, out, stage, flat, done, sems = refs[:4], *refs[4:10]
    member, core, _ = my_place()
    for rel in range(4):
        for side in range(2):
            stage[(core ^ side) * 4 + (member ^ rel)] = pieces[rel][side].astype(F32)
    step = 16
    group = lax.broadcasted_iota(jnp.int32, (step, 128), 1) >> 4
    for row in range(0, LAG_ROWS, step):
        tiles = [stage[m, row : row + step] for m in range(8)]
        for bit in (4, 2, 1):
            upper = (group & bit) > 0
            for m in range(8):
                if not m & bit:
                    low, high = tiles[m], tiles[m | bit]
                    tiles[m] = jnp.where(upper, pltpu.roll(high, bit * QG, 1), low)
                    tiles[m | bit] = jnp.where(upper, high, pltpu.roll(low, 128 - bit * QG, 1))
        for s in range(8):
            flat[row : row + step, s * 128 : (s + 1) * 128] = tiles[s]
    flat_low = flat[...].astype(BF16)
    copies = []
    for k, (start, stop) in enumerate(((0, 64), (64, 128), (128, LAGS))):
        end = min(start + 80, LAG_ROWS) if stop == LAGS else stop
        back = mxu(table[start:end, :], flat_low)
        for s in range(SLOTS // 2):
            lanes = slice(s * 128, (s + 1) * 128)
            turned, alive = flags[s : s + 1, :] > 0.0, core * (SLOTS // 2) + s < count[0]
            value = jnp.where(turned, back[:, lanes], flat[start:end, lanes])
            done[start:stop, s, :] = jnp.where(alive, value, 0.0)[0 : stop - start]
        copies.append(pltpu.make_async_copy(done.at[start:stop], out.at[start:stop], sems.at[k]))
        copies[-1].start()
    for copy in copies:
        copy.wait()


VM = pl.BlockSpec(memory_space=pltpu.VMEM)
SM = pl.BlockSpec(memory_space=pltpu.SMEM)
PARAMS = pltpu.CompilerParams(vmem_limit_bytes=VMEM_LIMIT)


def shape(dims, kind):
    return jax.ShapeDtypeStruct(dims, kind)


def local(traces, channel_ok, time_taps, space_taps, pair_blocks, pair_count):
    n_chan = lax.axis_size("chan")
    n_plane = n_chan // PLANE
    chan_width, half = traces.shape
    segs = 2 * half // SEG
    part = segs // 2
    core = lax.axis_index("tm")
    odd = (lax.axis_index("chan") // PLANE) % 2
    pairs = jnp.transpose(pair_blocks)

    def to_core(x):
        return lax.ppermute(x, "tm", [(0, 1), (1, 0)])

    def in_plane(x, rel):
        return lax.ppermute(x, "chan", [(c, c ^ rel) for c in range(n_chan)])

    def plane_swap(x, start):
        route = []
        for p in range(start, n_plane - 1, 2):
            for k in range(PLANE):
                low, high = p * PLANE + k, (p + 1) * PLANE + k
                route += [(low, high), (high, low)]
        return lax.ppermute(x, "chan", route)

    rows = chan_width // 2
    head, tail = traces[0:2], traces[chan_width - 2 :]
    give = jnp.where(core == 0, tail, head)
    mine = jnp.where(core == 0, head, tail)
    give, mine, time_taps, space_taps, channel_ok, pairs = lax.optimization_barrier(
        (give, mine, time_taps, space_taps, channel_ok, pairs)
    )
    got = to_core(give)
    alive = (jnp.where(core == 0, channel_ok[0:2], channel_ok[chan_width - 2 :]) > 0)[:, None]
    mine = jnp.where(alive, mine, 0.0)
    small = jnp.pad(time_taps[None, :], ((0, 7), (0, 128 - TAPS)))
    small = small + jnp.pad(space_taps[None, :], ((1, 6), (0, 128 - STAPS)))
    whole = jnp.pad(pairs, ((0, 6), (0, 128 - SLOTS)))
    whole = whole + jnp.pad(channel_ok[None, :], ((2, 5), (0, 128 - chan_width)))
    got, mine, small, whole = lax.optimization_barrier((got, mine, small, whole))
    route = []
    for c in range(n_chan - 1):
        route += [(2 * c + 1, 2 * c + 2), (2 * c + 2, 2 * c + 1)]
    edges = jnp.concatenate([mine, jnp.where(alive, got, 0.0)], axis=0)
    edges, late = lax.optimization_barrier((edges, traces))
    halos = lax.ppermute(edges, BOTH, route)
    other = to_core(late)
    table = shape((2 * SEG, SEG), BF16)
    split = shape((rows, half), BF16)
    t_high, t_low, pid, space, ok, flags, own_high, own_low, own_near = pl.pallas_call(
        prepare_kernel,
        out_shape=[
            table, table, shape((QG, SLOTS * QG), BF16), shape((8, SEG), F32), shape((chan_width, 128), F32),
            shape((8, 128), F32), split, split, shape((8, half), F32),
        ],
        in_specs=[SM, SM, VM, VM],
        out_specs=[VM] * 9,
        compiler_params=PARAMS,
        name="prepare",
    )(small, whole, whole, late)
    block = shape((segs + 1, QG, SEG), BF16)
    short = shape((part, QG, SEG), BF16)
    first, second, *sent = pl.pallas_call(
        filter_kernel,
        out_shape=[short] * 2 + [block] * 3,
        in_specs=[VM] * 10,
        out_specs=[VM] * 5,
        scratch_shapes=[
            pltpu.VMEM((rows + 16, 2 * half + SEG), BF16),
            pltpu.VMEM((rows + 16, 2 * half + SEG), BF16),
            pltpu.VMEM((8, half), F32),
            pltpu.VMEM((segs, rows, SEG), BF16),
        ],
        compiler_params=PARAMS,
        name="filter_whiten",
    )(own_near, own_high, own_low, other, halos, space, ok, t_high, t_low, pid)
    b1, b2 = in_plane(sent[0], 1), in_plane(sent[1], 2)
    far_0, near_0 = plane_swap(second, 1), plane_swap(first, 0)
    near_0, last = lax.optimization_barrier((near_0, sent[2]))
    b3 = in_plane(last, 3)
    b1, b2, near_0, far_0 = lax.optimization_barrier((b1, b2, near_0, far_0))
    def halves(x):
        near = lax.dynamic_slice_in_dim(x, (1 - odd) * part, part, axis=0)
        far = lax.dynamic_slice_in_dim(x, odd * part, part, axis=0)
        return near, far

    (near_1, far_1), (near_2, far_2) = halves(b1), halves(b2)
    far_12 = plane_swap(jnp.stack([far_1, far_2]), 1)
    near_12 = plane_swap(jnp.stack([near_1, near_2]), 0)
    near_3, far_3 = halves(b3)
    far_3, near_3 = plane_swap(far_3, 1), plane_swap(near_3, 0)
    scale = 1.0 / math.sqrt(segs * SEG)
    l_high, l_low = inverse_np(scale)
    sent_shape = shape((LAG_ROWS, N_SENT * QG), BF16)
    table = jnp.asarray(forward_np())
    short = shape((part, QG, 2 * SEG), F32)
    spec, spec_near, spec_far, inner = pl.pallas_call(
        inner_kernel,
        out_shape=[shape((PLANE, segs, QG, 2 * SEG), F32), short, short, shape((N_IN * QG, 2 * SEG), F32)],
        in_specs=[VM] * 8,
        out_specs=[VM] * 4,
        compiler_params=PARAMS,
        name="inner_pairs",
    )(first, second, b1, b2, b3, near_0, far_0, table)
    cross = pl.pallas_call(
        cross_kernel,
        out_shape=shape((N_OWN * QG, 2 * SEG), F32),
        in_specs=[VM] * 7,
        out_specs=VM,
        scratch_shapes=[pltpu.VMEM((2, PLANE, part, QG, 2 * SEG), F32)],
        compiler_params=PARAMS,
        name="cross_pairs",
    )(spec, spec_near, spec_far, inner, near_12, far_12, table)
    lags, lags_first, lags_second = pl.pallas_call(
        lags_kernel,
        out_shape=[shape((LAG_ROWS, N_OWN * QG), BF16), sent_shape, sent_shape],
        in_specs=[VM] * 7,
        out_specs=[VM] * 3,
        scratch_shapes=[
            pltpu.VMEM((2, part, QG, 2 * SEG), F32),
            pltpu.VMEM((N_OWN * QG, 2 * SEG), F32),
        ],
        compiler_params=PARAMS,
        name="pair_lags",
    )(spec, cross, near_3, far_3, table, jnp.asarray(l_high), jnp.asarray(l_low))
    from_first, from_second = plane_swap(lags_first, 0), plane_swap(lags_second, 1)
    known = [lags, from_first, from_second]
    pid_spec = pl.BlockSpec((1, QG, SEG), lambda step: (segs, 0, 0))
    own_spec = pl.BlockSpec((1, QG, SEG), lambda step: (0, 0, 0))
    slots_shape = shape((2, LAG_ROWS, 128), BF16)
    chosen = pl.pallas_call(
        choose_kernel,
        grid=(1,),
        out_shape=shape((N_ALL * QG, 512), BF16),
        in_specs=[own_spec] + [pid_spec] * 3,
        out_specs=VM,
        compiler_params=PARAMS,
        name="choose",
    )(pid[None], b1, b2, b3)
    picked = pl.pallas_call(
        select_kernel,
        out_shape=[slots_shape] * 4,
        in_specs=[VM] * 7,
        out_specs=[VM] * 4,
        scratch_shapes=[pltpu.VMEM((2 * LAG_ROWS, N_ALL * QG), BF16)],
        compiler_params=PARAMS,
        name="select_slots",
    )(chosen, *known, *[to_core(x) for x in known])
    pieces = [picked[0]] + [in_plane(x, rel + 1) for rel, x in enumerate(picked[1:])]
    out = pl.pallas_call(
        finish_kernel,
        out_shape=shape((LAGS, SLOTS // 2, chan_width), F32),
        in_specs=[SM] + [VM] * 6,
        out_specs=pl.BlockSpec(memory_space=pl.ANY),
        scratch_shapes=[
            pltpu.VMEM((8, LAG_ROWS, 128), F32),
            pltpu.VMEM((LAG_ROWS, SLOTS // 2 * 128), F32),
            pltpu.VMEM((LAGS, SLOTS // 2, 128), F32),
            pltpu.SemaphoreType.DMA((3,)),
        ],
        compiler_params=PARAMS,
        name="finish_slots",
    )(pair_count, flags, *pieces, jnp.asarray(reverse_np()))
    return jnp.transpose(out, (1, 0, 2))


def solution(mesh):
    return jax.shard_map(
        local,
        mesh=mesh,
        in_specs=(P("chan", "tm"), P("chan"), P(), P(), P("chan", None), P("chan")),
        out_specs=P(("chan", "tm"), None, None),
        check_vma=False,
    )
```

```python
import math

import jax
import jax.numpy as jnp
import ml_dtypes
import numpy as np
from jax import lax
from jax.experimental import pallas as pl
from jax.experimental.pallas import tpu as pltpu
from jax.sharding import PartitionSpec as P

SEG = 256
MAXLAG = 100
TAPS = 33
STAPS = 5
SLOTS = 16
NFFT = 510
LAGS = 201
LAG_ROWS = 208
PLANE = 4
QG = 16
BOTH = ("chan", "tm")
F32 = jnp.float32
BF16 = jnp.bfloat16
VMEM_LIMIT = 20 * 1024 * 1024
INNER = [(0, 1), (0, 2), (0, 3), (1, 2), (1, 3), (2, 3)]
CROSS = [(i, j) for i in range(PLANE) for j in range(i + 1)]
N_IN, N_CROSS = len(INNER), len(CROSS)
N_OWN = N_CROSS + N_IN + N_CROSS
N_SENT = N_IN + N_CROSS
N_ALL = N_OWN + 2 * N_SENT


def split_np(table):
    high = table.astype(np.float32).astype(ml_dtypes.bfloat16)
    low = (table - high.astype(np.float64)).astype(np.float32).astype(ml_dtypes.bfloat16)
    return high, low


def forward_np():
    sample = np.arange(SEG)[:, None]
    bins = np.arange(SEG)[None, :]
    angle = (sample * bins % NFFT) * (2.0 * math.pi / NFFT)
    table = np.concatenate([np.cos(angle), -np.sin(angle)], axis=1)
    return table.astype(np.float32).astype(ml_dtypes.bfloat16)


def inverse_np(scale):
    lag = np.arange(LAG_ROWS)[:, None] - MAXLAG
    bins = np.arange(SEG)[None, :]
    angle = (lag * bins % NFFT) * (2.0 * math.pi / NFFT)
    weight = np.where((bins == 0) | (bins == SEG - 1), 1.0, 2.0) / NFFT * scale
    table = np.concatenate([weight * np.cos(angle), -weight * np.sin(angle)], axis=1)
    table[LAGS:] = 0.0
    return split_np(table)


def reverse_np():
    rows = np.arange(LAG_ROWS)
    table = (rows[:, None] + rows[None, :] == LAGS - 1).astype(np.float32)
    return table.astype(ml_dtypes.bfloat16)


def split_terms(value):
    high = value.astype(BF16)
    low = (value - high.astype(F32)).astype(BF16)
    return high, low


def mxu(a, b):
    return jnp.dot(a, b, preferred_element_type=F32)


def my_place():
    chan = lax.axis_index("chan")
    return chan % PLANE, lax.axis_index("tm"), (chan // PLANE) % 2


def pair_ids(first, second, plane):
    low, high = jnp.minimum(first, second), jnp.maximum(first, second)
    low_plane, low_at = low // PLANE - plane, low % PLANE
    high_plane, high_at = high // PLANE - plane, high % PLANE
    inner = jnp.int32(0)
    for k, (i, j) in enumerate(INNER):
        inner = jnp.where((low_at == i) & (high_at == j), k, inner)
    cross = low_at * (low_at + 1) // 2 + high_at
    one = jnp.where(
        low_plane == 0,
        jnp.where(high_plane == 0, N_CROSS + inner, N_CROSS + N_IN + cross),
        jnp.where(
            low_plane > 0,
            N_OWN + N_SENT + N_CROSS + inner,
            jnp.where(high_plane == 0, cross, N_OWN + inner),
        ),
    )
    two = jnp.where(
        low_plane == high_plane,
        N_ALL,
        jnp.where(low_plane == 0, N_OWN + N_SENT + cross, N_OWN + N_IN + cross),
    )
    return one, two


def tile_rows(own, core):
    rows = own.shape[0] // 2
    first_row = pl.multiple_of(core * rows, rows)
    near_row = pl.multiple_of(rows - 8 + 8 * (1 - core), 8)
    return pl.ds(first_row, rows), pl.ds(near_row, 8)


def prepare_kernel(
    small, whole, whole_rows, traces, t_high, t_low, pid, space, ok, flags, own_high, own_low, own_near,
):
    _, core, _ = my_place()
    plane = lax.axis_index("chan") // PLANE
    main, near = tile_rows(traces, core)
    t_high[...] = jnp.zeros(t_high.shape, BF16)
    t_low[...] = jnp.zeros(t_low.shape, BF16)
    shift = SEG // 2 - (TAPS - 1) // 2
    height = 128 + TAPS - 1
    tap = lax.broadcasted_iota(jnp.int32, (height, 128), 0) - lax.broadcasted_iota(
        jnp.int32, (height, 128), 1
    )
    band = jnp.zeros((height, 128), F32)
    for j in range(TAPS):
        band = jnp.where(tap == j, small[0, j], band)
    high, low = split_terms(band)
    for lanes in range(SEG // 128):
        at = (slice(lanes * 128 + shift, lanes * 128 + shift + height), slice(lanes * 128, lanes * 128 + 128))
        t_high[at] = high
        t_low[at] = low
    row = lax.broadcasted_iota(jnp.int32, space.shape, 0)
    value = jnp.zeros(space.shape, F32)
    for j in range(STAPS):
        value = jnp.where(row == j, small[1, j], value)
    space[...] = value
    slot = lax.broadcasted_iota(jnp.int32, pid.shape, 1) >> 4
    upper = lax.broadcasted_iota(jnp.int32, pid.shape, 0) < 8
    ids = jnp.zeros(pid.shape, jnp.int32)
    for s in range(SLOTS):
        one, two = pair_ids(whole[0, s], whole[1, s], plane)
        ids = jnp.where(slot == s, jnp.where(upper, one, two), ids)
    pid[...] = ids.astype(F32).astype(BF16)
    row = lax.broadcasted_iota(jnp.int32, flags.shape, 0)
    value = jnp.zeros(flags.shape, F32)
    for s in range(SLOTS // 2):
        slot = core * (SLOTS // 2) + s
        value = jnp.where(row == s, (whole[0, slot] > whole[1, slot]).astype(F32), value)
    flags[...] = value
    width = ok.shape[0]
    diagonal = lax.broadcasted_iota(jnp.int32, (width, width), 0) == lax.broadcasted_iota(
        jnp.int32, (width, width), 1
    )
    spread = jnp.where(diagonal, whole_rows[2:3, :width].astype(F32), 0.0)
    ok[...] = jnp.broadcast_to(jnp.sum(spread, axis=1, keepdims=True), ok.shape)
    own_high[...], own_low[...] = split_terms(traces[main, :] * ok[main, 0:1])
    own_near[...] = traces[near, :] * ok[near, 0:1]


def filter_kernel(
    own_near, own_high, own_low, other, halos, space, ok, t_high, t_low, pid,
    out_first, out_second, out_1, out_2, out_3, x_high, x_low, edge, white,
):
    member, core, odd = my_place()
    rows, half = own_high.shape
    main, near = tile_rows(other, core)
    pad = SEG // 2
    total = 2 * half
    zeros = jnp.zeros((rows + 16, pad), BF16)
    for buf in (x_high, x_low):
        buf[:, 0:pad] = zeros
        buf[:, pad + total : 2 * pad + total] = zeros
    own_lanes = pl.ds(pl.multiple_of(pad + core * half, pad), half)
    other_lanes = pl.ds(pl.multiple_of(pad + (1 - core) * half, pad), half)
    x_high[0:rows, own_lanes] = own_high[...]
    x_low[0:rows, own_lanes] = own_low[...]
    x_high[0:rows, other_lanes], x_low[0:rows, other_lanes] = split_terms(other[main, :] * ok[main, 0:1])
    other_near = other[near, :] * ok[near, 0:1]
    for inside, halo, lanes in ((own_near[...], halos[2:4], own_lanes), (other_near, halos[0:2], other_lanes)):
        for k in range(4):
            edge[2 * k : 2 * k + 2, :] = halo
        outside = edge[...]
        above = jnp.where(core == 0, outside, inside)
        below = jnp.where(core == 0, inside, outside)
        high, low = split_terms(jnp.concatenate([above, below], axis=0))
        x_high[rows : rows + 16, lanes] = high
        x_low[rows : rows + 16, lanes] = low
    segs = total // SEG
    chunk = 4
    height = rows + 16
    taps = [space[j : j + 1, :] for j in range(STAPS)]
    t_all = jnp.concatenate([t_high[...], t_high[...], t_low[...]], axis=0)

    def body(step, carry):
        seg0 = step * chunk
        spans = [pl.ds(pl.multiple_of((seg0 + s) * SEG, SEG), 2 * SEG) for s in range(chunk)]
        high = jnp.concatenate([x_high[:, span] for span in spans], axis=0)
        low = jnp.concatenate([x_low[:, span] for span in spans], axis=0)
        y = mxu(jnp.concatenate([high, low, high], axis=1), t_all)
        for s in range(chunk):
            block = y[s * height : (s + 1) * height]
            ext = jnp.concatenate(
                [block[rows : rows + 8], block[0:rows], block[rows + 8 : rows + 16]], axis=0
            )
            filtered = taps[0] * ext[6 : 6 + rows]
            for j in range(1, STAPS):
                filtered = filtered + taps[j] * ext[6 + j : 6 + j + rows]
            power = jnp.mean(filtered * filtered, axis=1, keepdims=True)
            white[seg0 + s] = (filtered * (1.0 / jnp.sqrt(power + 1e-5))).astype(BF16)
        return carry

    lax.fori_loop(0, segs // chunk, body, 0, unroll=True)
    own_row = pl.multiple_of(member * QG, QG)
    part = segs // 2
    out_first[...] = white[pl.ds((1 - odd) * part, part), pl.ds(own_row, QG), :]
    out_second[...] = white[pl.ds(odd * part, part), pl.ds(own_row, QG), :]
    for rel, out in ((1, out_1), (2, out_2), (3, out_3)):
        row = pl.multiple_of((member ^ rel) * QG, QG)
        out[0:segs] = white[:, pl.ds(row, QG), :]
        out[segs] = pid[...]


def transform(block, table):
    value = mxu(block.reshape(block.shape[0] * QG, SEG), table[...])
    return value.astype(BF16).astype(F32).reshape(block.shape[0], QG, 2 * SEG)


def bin_parts():
    for q8 in range(QG // 8):
        for lanes in range(SEG // 128):
            rows = slice(q8 * 8, q8 * 8 + 8)
            re_lanes = slice(lanes * 128, lanes * 128 + 128)
            im_lanes = slice(SEG + lanes * 128, SEG + lanes * 128 + 128)
            yield q8 * 8, rows, re_lanes, im_lanes


def add_product(sums, index, left, right):
    re = sums[2 * index] + (left[0] * right[0] + left[1] * right[1])
    im = sums[2 * index + 1] + (left[1] * right[0] - left[0] * right[1])
    return [re, im]


def store_sums(cross, first_pair, row, re_lanes, im_lanes, sums):
    for index in range(len(sums) // 2):
        at = slice((first_pair + index) * QG + row, (first_pair + index) * QG + row + 8)
        cross[at, re_lanes] = sums[2 * index]
        cross[at, im_lanes] = sums[2 * index + 1]


def inner_kernel(first, second, b1, b2, b3, near_0, far_0, table, spec, spec_near, spec_far, inner):
    member, _, odd = my_place()
    segs = spec.shape[1]
    part = segs // 2
    spec[member, pl.ds((1 - odd) * part, part)] = transform(first[...], table)
    spec[member, pl.ds(odd * part, part)] = transform(second[...], table)
    for rel, ref in ((1, b1), (2, b2), (3, b3)):
        spec[member ^ rel] = transform(ref[0:segs], table)
    spec_near[...] = transform(near_0[...], table)
    spec_far[...] = transform(far_0[...], table)
    for row, rows, re_lanes, im_lanes in bin_parts():

        def body(seg, sums):
            mine = [(spec[w, seg, rows, re_lanes], spec[w, seg, rows, im_lanes]) for w in range(PLANE)]
            result = []
            for k, (i, j) in enumerate(INNER):
                result += add_product(sums, k, mine[i], mine[j])
            return tuple(result)

        zero = jnp.zeros((8, 128), F32)
        sums = lax.fori_loop(0, segs, body, (zero,) * (2 * N_IN), unroll=4)
        store_sums(inner, 0, row, re_lanes, im_lanes, sums)


def cross_kernel(spec, spec_near, spec_far, inner, near_12, far_12, table, cross, spec_z):
    member, _, odd = my_place()
    part = spec_near.shape[0]
    for side, done, pair in ((odd, spec_near, near_12), (1 - odd, spec_far, far_12)):
        spec_z[side, member] = done[...]
        spec_z[side, member ^ 1] = transform(pair[0], table)
        spec_z[side, member ^ 2] = transform(pair[1], table)
        spec_z[side, member ^ 3] = jnp.zeros(done.shape, F32)
    cross[N_CROSS * QG : (N_CROSS + N_IN) * QG, :] = inner[...]
    for row, rows, re_lanes, im_lanes in bin_parts():
        for side, first_pair in ((0, N_CROSS + N_IN), (1, 0)):

            def body(seg, sums):
                at = seg + side * part
                mine = [(spec[w, at, rows, re_lanes], spec[w, at, rows, im_lanes]) for w in range(PLANE)]
                theirs = [
                    (spec_z[side, w, seg, rows, re_lanes], spec_z[side, w, seg, rows, im_lanes])
                    for w in range(PLANE)
                ]
                low, high = (theirs, mine) if side else (mine, theirs)
                result = []
                for k, (i, j) in enumerate(CROSS):
                    result += add_product(sums, k, low[i], high[j])
                return tuple(result)

            zero = jnp.zeros((8, 128), F32)
            sums = lax.fori_loop(0, part, body, (zero,) * (2 * N_CROSS), unroll=4)
            store_sums(cross, first_pair, row, re_lanes, im_lanes, sums)


def lags_kernel(
    spec, cross_in, near_3, far_3, table, l_high, l_low, out, out_first, out_second, last, cross
):
    member, _, odd = my_place()
    part = near_3.shape[0]
    diagonal = member ^ 3
    last[odd] = transform(near_3[...], table)
    last[1 - odd] = transform(far_3[...], table)
    cross[...] = cross_in[...]
    for row, rows, re_lanes, im_lanes in bin_parts():
        for side in range(2):

            def body(seg, sums):
                at = seg + side * part
                theirs = (last[side, seg, rows, re_lanes], last[side, seg, rows, im_lanes])
                result = []
                for w in range(PLANE):
                    mine = (spec[w, at, rows, re_lanes], spec[w, at, rows, im_lanes])
                    low, high = (theirs, mine) if side else (mine, theirs)
                    result += add_product(sums, w, low, high)
                return tuple(result)

            zero = jnp.zeros((8, 128), F32)
            sums = lax.fori_loop(0, part, body, (zero,) * (2 * PLANE), unroll=4)
            for w in range(PLANE):
                if side:
                    valid, pair = w <= diagonal, diagonal * (diagonal + 1) // 2 + w
                else:
                    valid, pair = w >= diagonal, N_CROSS + N_IN + w * (w + 1) // 2 + diagonal
                at = pl.ds(pl.multiple_of(jnp.where(valid, pair, 0) * QG + row, 8), 8)
                cross[at, re_lanes] += jnp.where(valid, sums[2 * w], 0.0)
                cross[at, im_lanes] += jnp.where(valid, sums[2 * w + 1], 0.0)
    high, low = split_terms(cross[...])

    def turned(left, right):
        return lax.dot_general(left, right, (((1,), (1,)), ((), ())), preferred_element_type=F32)

    lagged = turned(l_high[...], high) + turned(l_high[...], low) + turned(l_low[...], high)
    out[...] = lagged.astype(BF16)
    to_above = lagged[:, N_CROSS * QG :]
    to_below = lagged[:, : N_SENT * QG]
    out_first[...] = jnp.where(odd == 1, to_below, to_above).astype(BF16)
    out_second[...] = jnp.where(odd == 1, to_above, to_below).astype(BF16)


def choose_kernel(*refs):
    pids, chosen = refs[:4], refs[4]
    _, core, _ = my_place()
    row_id = lax.broadcasted_iota(jnp.int32, (N_ALL * QG, 128), 0)
    col_id = lax.broadcasted_iota(jnp.int32, (N_ALL * QG, 128), 1)
    row_key = jnp.where((row_id & 15) == (col_id & 15), (row_id >> 4).astype(F32), -1.0)
    lane = pl.multiple_of(core * 128, 128)
    for rel, pid in enumerate(pids):
        ids = pid[0, :, pl.ds(lane, 128)].astype(F32)
        match = (row_key == ids[0:1, :]) | (row_key == ids[8:9, :])
        chosen[:, rel * 128 : (rel + 1) * 128] = jnp.where(match, 1.0, 0.0).astype(BF16)


def select_kernel(chosen, *refs):
    mine, swapped, outs, lags = refs[0:3], refs[3:6], refs[6:10], refs[10]
    _, _, odd = my_place()
    own, sent = N_OWN * QG, N_SENT * QG
    for side, (here, first, second) in enumerate((mine, swapped)):
        at = slice(side * LAG_ROWS, (side + 1) * LAG_ROWS)
        below = jnp.where(odd == 1, first[...].astype(F32), second[...].astype(F32)).astype(BF16)
        above = jnp.where(odd == 1, second[...].astype(F32), first[...].astype(F32)).astype(BF16)
        lags[at, 0:own] = here[...]
        lags[at, own : own + sent] = below
        lags[at, own + sent : own + 2 * sent] = above
    picked = mxu(lags[...], chosen[...]).astype(BF16)
    for rel in range(4):
        for side in range(2):
            outs[rel][side] = picked[side * LAG_ROWS : (side + 1) * LAG_ROWS, rel * 128 : (rel + 1) * 128]


def finish_kernel(count, flags, *refs):
    pieces, table, out, stage, flat, done, sems = refs[:4], *refs[4:10]
    member, core, _ = my_place()
    for rel in range(4):
        for side in range(2):
            stage[(core ^ side) * 4 + (member ^ rel)] = pieces[rel][side].astype(F32)
    step = 16
    group = lax.broadcasted_iota(jnp.int32, (step, 128), 1) >> 4
    for row in range(0, LAG_ROWS, step):
        tiles = [stage[m, row : row + step] for m in range(8)]
        for bit in (4, 2, 1):
            upper = (group & bit) > 0
            for m in range(8):
                if not m & bit:
                    low, high = tiles[m], tiles[m | bit]
                    tiles[m] = jnp.where(upper, pltpu.roll(high, bit * QG, 1), low)
                    tiles[m | bit] = jnp.where(upper, high, pltpu.roll(low, 128 - bit * QG, 1))
        for s in range(8):
            flat[row : row + step, s * 128 : (s + 1) * 128] = tiles[s]
    flat_low = flat[...].astype(BF16)
    copies = []
    for k, (start, stop) in enumerate(((0, 64), (64, 128), (128, LAGS))):
        end = min(start + 80, LAG_ROWS) if stop == LAGS else stop
        back = mxu(table[start:end, :], flat_low)
        for s in range(SLOTS // 2):
            lanes = slice(s * 128, (s + 1) * 128)
            turned, alive = flags[s : s + 1, :] > 0.0, core * (SLOTS // 2) + s < count[0]
            value = jnp.where(turned, back[:, lanes], flat[start:end, lanes])
            done[start:stop, s, :] = jnp.where(alive, value, 0.0)[0 : stop - start]
        copies.append(pltpu.make_async_copy(done.at[start:stop], out.at[start:stop], sems.at[k]))
        copies[-1].start()
    for copy in copies:
        copy.wait()


VM = pl.BlockSpec(memory_space=pltpu.VMEM)
SM = pl.BlockSpec(memory_space=pltpu.SMEM)
PARAMS = pltpu.CompilerParams(vmem_limit_bytes=VMEM_LIMIT)


def shape(dims, kind):
    return jax.ShapeDtypeStruct(dims, kind)


def local(traces, channel_ok, time_taps, space_taps, pair_blocks, pair_count):
    n_chan = lax.axis_size("chan")
    n_plane = n_chan // PLANE
    chan_width, half = traces.shape
    segs = 2 * half // SEG
    part = segs // 2
    core = lax.axis_index("tm")
    odd = (lax.axis_index("chan") // PLANE) % 2
    pairs = jnp.transpose(pair_blocks)

    def to_core(x):
        return lax.ppermute(x, "tm", [(0, 1), (1, 0)])

    def in_plane(x, rel):
        return lax.ppermute(x, "chan", [(c, c ^ rel) for c in range(n_chan)])

    def plane_swap(x, start):
        route = []
        for p in range(start, n_plane - 1, 2):
            for k in range(PLANE):
                low, high = p * PLANE + k, (p + 1) * PLANE + k
                route += [(low, high), (high, low)]
        return lax.ppermute(x, "chan", route)

    rows = chan_width // 2
    head, tail = traces[0:2], traces[chan_width - 2 :]
    give = jnp.where(core == 0, tail, head)
    mine = jnp.where(core == 0, head, tail)
    give, mine, time_taps, space_taps, channel_ok, pairs = lax.optimization_barrier(
        (give, mine, time_taps, space_taps, channel_ok, pairs)
    )
    got = to_core(give)
    alive = (jnp.where(core == 0, channel_ok[0:2], channel_ok[chan_width - 2 :]) > 0)[:, None]
    mine = jnp.where(alive, mine, 0.0)
    small = jnp.pad(time_taps[None, :], ((0, 7), (0, 128 - TAPS)))
    small = small + jnp.pad(space_taps[None, :], ((1, 6), (0, 128 - STAPS)))
    whole = jnp.pad(pairs, ((0, 6), (0, 128 - SLOTS)))
    whole = whole + jnp.pad(channel_ok[None, :], ((2, 5), (0, 128 - chan_width)))
    got, mine, small, whole = lax.optimization_barrier((got, mine, small, whole))
    route = []
    for c in range(n_chan - 1):
        route += [(2 * c + 1, 2 * c + 2), (2 * c + 2, 2 * c + 1)]
    edges = jnp.concatenate([mine, jnp.where(alive, got, 0.0)], axis=0)
    edges, late = lax.optimization_barrier((edges, traces))
    halos = lax.ppermute(edges, BOTH, route)
    other = to_core(late)
    table = shape((2 * SEG, SEG), BF16)
    split = shape((rows, half), BF16)
    t_high, t_low, pid, space, ok, flags, own_high, own_low, own_near = pl.pallas_call(
        prepare_kernel,
        out_shape=[
            table, table, shape((QG, SLOTS * QG), BF16), shape((8, SEG), F32), shape((chan_width, 128), F32),
            shape((8, 128), F32), split, split, shape((8, half), F32),
        ],
        in_specs=[SM, SM, VM, VM],
        out_specs=[VM] * 9,
        compiler_params=PARAMS,
        name="prepare",
    )(small, whole, whole, late)
    block = shape((segs + 1, QG, SEG), BF16)
    short = shape((part, QG, SEG), BF16)
    first, second, *sent = pl.pallas_call(
        filter_kernel,
        out_shape=[short] * 2 + [block] * 3,
        in_specs=[VM] * 10,
        out_specs=[VM] * 5,
        scratch_shapes=[
            pltpu.VMEM((rows + 16, 2 * half + SEG), BF16),
            pltpu.VMEM((rows + 16, 2 * half + SEG), BF16),
            pltpu.VMEM((8, half), F32),
            pltpu.VMEM((segs, rows, SEG), BF16),
        ],
        compiler_params=PARAMS,
        name="filter_whiten",
    )(own_near, own_high, own_low, other, halos, space, ok, t_high, t_low, pid)
    b1, b2 = in_plane(sent[0], 1), in_plane(sent[1], 2)
    far_0, near_0 = plane_swap(second, 1), plane_swap(first, 0)
    near_0, last = lax.optimization_barrier((near_0, sent[2]))
    b3 = in_plane(last, 3)
    b1, b2, near_0, far_0 = lax.optimization_barrier((b1, b2, near_0, far_0))
    def halves(x):
        near = lax.dynamic_slice_in_dim(x, (1 - odd) * part, part, axis=0)
        far = lax.dynamic_slice_in_dim(x, odd * part, part, axis=0)
        return near, far

    (near_1, far_1), (near_2, far_2) = halves(b1), halves(b2)
    far_12 = plane_swap(jnp.stack([far_1, far_2]), 1)
    near_12 = plane_swap(jnp.stack([near_1, near_2]), 0)
    near_3, far_3 = halves(b3)
    far_3, near_3 = plane_swap(far_3, 1), plane_swap(near_3, 0)
    scale = 1.0 / math.sqrt(segs * SEG)
    l_high, l_low = inverse_np(scale)
    sent_shape = shape((LAG_ROWS, N_SENT * QG), BF16)
    table = jnp.asarray(forward_np())
    short = shape((part, QG, 2 * SEG), F32)
    spec, spec_near, spec_far, inner = pl.pallas_call(
        inner_kernel,
        out_shape=[shape((PLANE, segs, QG, 2 * SEG), F32), short, short, shape((N_IN * QG, 2 * SEG), F32)],
        in_specs=[VM] * 8,
        out_specs=[VM] * 4,
        compiler_params=PARAMS,
        name="inner_pairs",
    )(first, second, b1, b2, b3, near_0, far_0, table)
    cross = pl.pallas_call(
        cross_kernel,
        out_shape=shape((N_OWN * QG, 2 * SEG), F32),
        in_specs=[VM] * 7,
        out_specs=VM,
        scratch_shapes=[pltpu.VMEM((2, PLANE, part, QG, 2 * SEG), F32)],
        compiler_params=PARAMS,
        name="cross_pairs",
    )(spec, spec_near, spec_far, inner, near_12, far_12, table)
    lags, lags_first, lags_second = pl.pallas_call(
        lags_kernel,
        out_shape=[shape((LAG_ROWS, N_OWN * QG), BF16), sent_shape, sent_shape],
        in_specs=[VM] * 7,
        out_specs=[VM] * 3,
        scratch_shapes=[
            pltpu.VMEM((2, part, QG, 2 * SEG), F32),
            pltpu.VMEM((N_OWN * QG, 2 * SEG), F32),
        ],
        compiler_params=PARAMS,
        name="pair_lags",
    )(spec, cross, near_3, far_3, table, jnp.asarray(l_high), jnp.asarray(l_low))
    from_first, from_second = plane_swap(lags_first, 0), plane_swap(lags_second, 1)
    known = [lags, from_first, from_second]
    pid_spec = pl.BlockSpec((1, QG, SEG), lambda step: (segs, 0, 0))
    own_spec = pl.BlockSpec((1, QG, SEG), lambda step: (0, 0, 0))
    slots_shape = shape((2, LAG_ROWS, 128), BF16)
    chosen = pl.pallas_call(
        choose_kernel,
        grid=(1,),
        out_shape=shape((N_ALL * QG, 512), BF16),
        in_specs=[own_spec] + [pid_spec] * 3,
        out_specs=VM,
        compiler_params=PARAMS,
        name="choose",
    )(pid[None], b1, b2, b3)
    picked = pl.pallas_call(
        select_kernel,
        out_shape=[slots_shape] * 4,
        in_specs=[VM] * 7,
        out_specs=[VM] * 4,
        scratch_shapes=[pltpu.VMEM((2 * LAG_ROWS, N_ALL * QG), BF16)],
        compiler_params=PARAMS,
        name="select_slots",
    )(chosen, *known, *[to_core(x) for x in known])
    pieces = [picked[0]] + [in_plane(x, rel + 1) for rel, x in enumerate(picked[1:])]
    out = pl.pallas_call(
        finish_kernel,
        out_shape=shape((LAGS, SLOTS // 2, chan_width), F32),
        in_specs=[SM] + [VM] * 6,
        out_specs=pl.BlockSpec(memory_space=pl.ANY),
        scratch_shapes=[
            pltpu.VMEM((8, LAG_ROWS, 128), F32),
            pltpu.VMEM((LAG_ROWS, SLOTS // 2 * 128), F32),
            pltpu.VMEM((LAGS, SLOTS // 2, 128), F32),
            pltpu.SemaphoreType.DMA((3,)),
        ],
        compiler_params=PARAMS,
        name="finish_slots",
    )(pair_count, flags, *pieces, jnp.asarray(reverse_np()))
    return jnp.transpose(out, (1, 0, 2))


def solution(mesh):
    return jax.shard_map(
        local,
        mesh=mesh,
        in_specs=(P("chan", "tm"), P("chan"), P(), P(), P("chan", None), P("chan")),
        out_specs=P(("chan", "tm"), None, None),
        check_vma=False,
    )
```
